128 devices in a mesh: dp: 32 (over y_hi, x, z), tensor: 4 (over y_lo, core).
Axes of the slice: x: 4, y: 4 (y_hi: 2, y_lo: 2; y = y_hi * 2 + y_lo), z: 4, core: 2. Of those that a mesh axis runs over, the one named last changes fastest.
Arguments:
- hidden_in: bfloat16 [16384, 2048], P('dp'), may hold values from -6 to 6
- cotangent: bfloat16 [16384, 2048], P('dp'), may hold values from -6 to 6
- seq_lengths: int32 [32], replicated, may hold values from 1 to 512, 10240 in all
- slot_order: int32 [32], P('dp'), may hold values from 0 to 31, each once
- attn_gain: bfloat16 [2048], replicated, may hold values from 0.5 to 1.5
- w_query: bfloat16 [2048, 2048], P(None, 'tensor'), may hold values from -0.25 to 0.25
- w_key: bfloat16 [2048, 256], P(None, 'tensor'), may hold values from -0.125 to 0.125
- w_value: bfloat16 [2048, 256], P(None, 'tensor'), may hold values from -0.125 to 0.125
- w_out: bfloat16 [2048, 2048], P('tensor'), may hold values from -0.5 to 0.5
- mlp_gain: bfloat16 [2048], replicated, may hold values from 0.5 to 1.5
- w_gate: bfloat16 [2048, 5632], P(None, 'tensor'), may hold values from -0.125 to 0.125
- w_up: bfloat16 [2048, 5632], P(None, 'tensor'), may hold values from -0.125 to 0.125
- w_down: bfloat16 [5632, 2048], P('tensor'), may hold values from -0.078125 to 0.078125
Outputs:
- output: bfloat16 [16384, 2048], P(('dp', 'tensor'))
- input_grad: float32 [16384, 2048], P(('dp', 'tensor'))
- attn_gain_grad: float32 [2048], replicated
- query_grad: float32 [2048, 2048], P('dp', 'tensor')
- key_grad: float32 [2048, 256], P('dp', 'tensor')
- value_grad: float32 [2048, 256], P('dp', 'tensor')
- out_grad: float32 [2048, 2048], P('tensor', 'dp')
- mlp_gain_grad: float32 [2048], replicated
- gate_grad: float32 [2048, 5632], P('dp', 'tensor')
- up_grad: float32 [2048, 5632], P('dp', 'tensor')
- down_grad: float32 [5632, 2048], P('tensor', 'dp')
The draws below stay inside these ranges and needn't reach their ends.
Inputs may be any that keep to these rules, and one draw needn't show every extreme that they name: seq_lengths[i] counts the real tokens of sequence i; they sum to 10240 and the largest is exactly 512. Slot s (rows s * 512 to (s + 1) * 512 - 1) holds sequence slot_order[s]; every sequence is held once.
All inputs are finite; a program needn't handle non-finite values.
Results may differ from the reference program's by a relative error of at most 0.014.
Values may be sent and summed in bfloat16 or wider, within the bound.
No kernel may reach another device: no remote copies, remote signals or barrier semaphores. Data moves between devices by JAX's collectives and lax.ppermute only.
A program may use at most 256 MiB of HBM per device.

```python
import math
import jax
import jax.numpy as jnp
import numpy as np
from jax import lax

D = 2048
HEADS = 32
KV_HEADS = 4
HDIM = 64
FF = 5632
TOK_DEV = 512
TOKENS = 16384
N_DP = 32
N_TENSOR = 4


def with_spikes(array, key, source, target, parts, factor):
    owner, partner = [(jnp.arange(array.shape[dim]) // (array.shape[dim] // parts)).reshape([-1 if axis == dim else 1 for axis in range(array.ndim)]) for dim in (source, target)]
    chosen = jax.random.permutation(key, parts)[partner]
    strong = (owner == chosen) | (owner == (partner + parts // 2) % parts)
    return jnp.where(strong, factor * array, array)


def block_levels(own_key, shape, cuts, low, high):
    level = 1.0
    for axis_at, shards_of in cuts:
        steps = jax.random.uniform(jax.random.fold_in(jax.random.fold_in(own_key, 6), axis_at), (shards_of,), jnp.float32, low / len(cuts), high / len(cuts))
        level = level * jnp.repeat(jnp.exp(steps), shape[axis_at] // shards_of).reshape((-1,) + (1,) * (len(shape) - 1 - axis_at))
    return level


def length_profile(count, total, most, skew):
    portions = [(1 << 20) // math.isqrt(grade ** skew) + 1 for grade in range(2, count + 1)]
    surplus, holding = total - most - (count - 1), [1] * (count - 1)
    while surplus > 0:
        movable = [i for i in range(count - 1) if holding[i] < most]
        whole, remaining = sum([portions[i] for i in movable]), surplus
        for i in movable:
            addition = min(most - holding[i], max(1, remaining * portions[i] // whole), surplus)
            holding[i] = holding[i] + addition
            surplus = surplus - addition
    return np.array([most] + holding)


def ragged_sizes(stream_key, count, total, bound, slope):
    if count == 2:
        one = jax.random.randint(stream_key, (), max(1, total - bound), min(bound, total - 1) + 1)
        return jnp.stack([one, total - one])
    sizes = jnp.asarray(length_profile(count, total, bound, slope), jnp.int32)
    pairs = (count - 1) // 2
    giver, taker = sizes[1:1 + 2 * pairs:2], sizes[2:2 + 2 * pairs:2]
    room = jnp.minimum(giver - 1, bound - taker)
    moved = jax.random.randint(jax.random.fold_in(stream_key, 1), (pairs,), 0, 1 << 20) % (room + 1)
    sizes = sizes.at[1:1 + 2 * pairs:2].set(giver - moved).at[2:2 + 2 * pairs:2].set(taker + moved)
    return sizes[jax.random.permutation(jax.random.fold_in(stream_key, 2), count)]


def centred(stream_key, extent, spread, most, cuts=(), kind=jnp.bfloat16):
    loudness = block_levels(stream_key, extent, cuts, -0.22, 0.18) if cuts else 1.0
    values = jax.random.normal(stream_key, extent, jnp.float32) * spread * loudness
    return jnp.minimum(jnp.maximum(values, -most), most).astype(kind)


def bell_draw_with(key, shape, scale, most, cuts, heavy, held_as=jnp.bfloat16):
    array = scale * jax.random.normal(key, shape, jnp.float32)
    if cuts:
        array = array * block_levels(key, shape, cuts, -0.22, 0.18)
    return jnp.clip(with_spikes(array, jax.random.fold_in(key, 3), *heavy), -most, most).astype(held_as)


def setup_inputs(seed: int = 0) -> dict:
    arg_keys = jax.random.split(jax.random.key(seed), 14)
    return {
        "hidden_in": bell_draw_with(arg_keys[0], (TOKENS, D), 1.0, 6.0, ((0, 32),), (0, 1, 32, 2.75)),
        "cotangent": bell_draw_with(arg_keys[1], (TOKENS, D), 1.0, 6.0, ((0, 32),), (0, 1, 32, 2.75)),
        "seq_lengths": ragged_sizes(arg_keys[2], N_DP, N_DP * TOK_DEV * 5 // 8, TOK_DEV, 1).astype(jnp.int32),
        "slot_order": jax.random.permutation(arg_keys[3], N_DP).astype(jnp.int32),
        "attn_gain": jnp.clip(1.0 + 0.1 * jax.random.normal(arg_keys[4], (D,), jnp.float32), 0.5, 1.5).astype(jnp.bfloat16),
        "w_query": centred(arg_keys[5], (D, HEADS * HDIM), (D // 4) ** -0.5, 0.25, ((1, 4),)),
        "w_key": centred(arg_keys[6], (D, KV_HEADS * HDIM), D ** -0.5, 0.125, ((1, 4),)),
        "w_value": centred(arg_keys[7], (D, KV_HEADS * HDIM), D ** -0.5, 0.125, ((1, 4),)),
        "w_out": centred(arg_keys[8], (HEADS * HDIM, D), (HEADS * HDIM // 16) ** -0.5, 0.5, ((0, 4),)),
        "mlp_gain": jnp.clip(1.0 + 0.1 * jax.random.normal(arg_keys[9], (D,), jnp.float32), 0.5, 1.5).astype(jnp.bfloat16),
        "w_gate": centred(arg_keys[10], (D, FF), D ** -0.5, 0.125, ((1, 4),)),
        "w_up": centred(arg_keys[11], (D, FF), D ** -0.5, 0.125, ((1, 4),)),
        "w_down": centred(arg_keys[12], (FF, D), FF ** -0.5, 0.078125, ((0, 4),)),
    }


EPS = 1e-05
HIGH = lax.Precision.HIGHEST

@jax.custom_vjp
def low(v):
    return lax.optimization_barrier(v.astype(jnp.bfloat16)).astype(jnp.float32)

@jax.custom_vjp
def low_back(v):
    return v

def low_keep(v):
    return (low(v), None)

def low_pass(kept, grad):
    return (grad,)

def back_keep(v):
    return (v, None)

def back_low(kept, grad):
    return (low(grad),)
low.defvjp(low_keep, low_pass)
low_back.defvjp(back_keep, back_low)

def rope_tables(row_count, head_width):
    half_width = head_width // 2
    position = jnp.arange(row_count, dtype=jnp.float32)[:, None]
    exponent = jnp.arange(half_width, dtype=jnp.float32) * (2.0 / head_width)
    angles = position / jnp.power(10000.0, exponent)[None, :]
    return (jnp.cos(angles)[:, None, :], jnp.sin(angles)[:, None, :])

def rotate(values, cosine_tab, sine_tab):
    half_width = values.shape[-1] // 2
    first_half = values[..., :half_width]
    second_half = values[..., half_width:]
    return jnp.concatenate([first_half * cosine_tab - second_half * sine_tab, second_half * cosine_tab + first_half * sine_tab], axis=-1)

def rms_normed(values):
    return values * lax.rsqrt(lax.optimization_barrier(jnp.mean(values * values, axis=-1, keepdims=True)) + EPS)

def attend(pieces):
    queries, key_heads, value_heads, length = pieces
    position = jnp.arange(TOK_DEV, dtype=jnp.int32)
    allowed = (position[None, :] <= position[:, None]) & (position[None, :] < length)
    pair_count = N_TENSOR // 2
    pair_keys = 2 * KV_HEADS // N_TENSOR
    per_key = HEADS // (2 * KV_HEADS)
    grouped = queries.reshape(TOK_DEV, pair_count, 2, pair_keys, per_key, HDIM).transpose(0, 1, 3, 2, 4, 5)
    grouped = grouped.reshape(TOK_DEV, KV_HEADS, HEADS // KV_HEADS, HDIM)
    raw_scores = low_back(jnp.einsum('sgqd,tgd->gqst', grouped, key_heads, precision=HIGH) * HDIM ** (-0.5))
    masked = jnp.where(allowed, raw_scores, -1e+30)
    row_max = lax.optimization_barrier(jnp.max(masked, axis=-1, keepdims=True))
    exp_scores = jnp.exp(masked - row_max)
    probs_low = low(exp_scores / lax.optimization_barrier(jnp.sum(exp_scores, axis=-1, keepdims=True)))
    mixed_heads = jnp.einsum('gqst,tgd->sgqd', probs_low, value_heads, precision=HIGH)
    mixed_heads = mixed_heads.reshape(TOK_DEV, pair_count, pair_keys, 2, per_key, HDIM).transpose(0, 1, 3, 2, 4, 5)
    return low(low_back(mixed_heads.reshape(TOK_DEV, HEADS * HDIM)))

def reference(hidden_in, cotangent, seq_lengths, slot_order, attn_gain, w_query, w_key, w_value, w_out, mlp_gain, w_gate, w_up, w_down):
    picker = jnp.arange(N_DP, dtype=jnp.int32)[None, :] == slot_order[:, None]
    slot_length = lax.optimization_barrier(jnp.sum(jnp.where(picker, seq_lengths[None, :], 0), axis=1)).astype(jnp.int32)
    position = jnp.arange(TOK_DEV, dtype=jnp.int32)
    live_rows = (position[None, :] < slot_length[:, None]).reshape(TOKENS, 1).astype(jnp.float32)
    cosine_tab, sine_tab = rope_tables(TOK_DEV, HDIM)

    def forward(inputs, gain_one, query_weight, key_weight, value_weight, out_weight, gain_two, gate_weight, up_weight, down_weight):
        attn_in = low(rms_normed(inputs) * gain_one)
        query_pre = low_back(jnp.dot(attn_in, query_weight, precision=HIGH))
        key_pre = low_back(jnp.dot(attn_in, key_weight, precision=HIGH))
        value_all = low(low_back(jnp.dot(attn_in, value_weight, precision=HIGH)))
        queries = low(rotate(query_pre.reshape(N_DP, TOK_DEV, HEADS, HDIM), cosine_tab, sine_tab))
        key_heads = low(rotate(key_pre.reshape(N_DP, TOK_DEV, KV_HEADS, HDIM), cosine_tab, sine_tab))
        value_all = value_all.reshape(N_DP, TOK_DEV, KV_HEADS, HDIM)
        attended = lax.map(jax.checkpoint(attend), (queries, key_heads, value_all, slot_length))
        attended = attended.reshape(TOKENS, HEADS * HDIM)
        middle = inputs + low_back(jnp.dot(attended, out_weight, precision=HIGH))
        mlp_in = low(rms_normed(middle) * gain_two)
        gate_val = low(low_back(jnp.dot(mlp_in, gate_weight, precision=HIGH)))
        up_val = low(low_back(jnp.dot(mlp_in, up_weight, precision=HIGH)))
        hidden = low(gate_val * jax.nn.sigmoid(gate_val) * up_val)
        return middle + low_back(jnp.dot(hidden, down_weight, precision=HIGH))
    floats = [hidden_in.astype(jnp.float32), attn_gain.astype(jnp.float32), w_query.astype(jnp.float32), w_key.astype(jnp.float32), w_value.astype(jnp.float32), w_out.astype(jnp.float32), mlp_gain.astype(jnp.float32), w_gate.astype(jnp.float32), w_up.astype(jnp.float32), w_down.astype(jnp.float32)]
    output, pullback = jax.vjp(forward, *floats)
    gradient = pullback(cotangent.astype(jnp.float32) * live_rows)
    return (output.astype(jnp.bfloat16), gradient[0], gradient[1], gradient[2], gradient[3], gradient[4], gradient[5], gradient[6], gradient[7], gradient[8], gradient[9])
```

```python
import functools

import jax
import jax.numpy as jnp
from jax import lax
from jax.experimental import pallas as pl
from jax.experimental.pallas import tpu as pltpu
from jax.sharding import PartitionSpec as P

HDIM = 64
EPS = 1e-05
LOW = jnp.bfloat16
FULL = jnp.float32


def ring_perm(ring, bits):
    step = bits * (4 if ring == "x" else 1)
    return [(i, i ^ step) for i in range(32)]


def over_ring(value, ring, bits):
    return lax.ppermute(value, "dp", ring_perm(ring, bits))


def over_yh(value):
    return lax.ppermute(value, "dp", [(i, i ^ 16) for i in range(32)])


def over_tensor(value, bits):
    return lax.ppermute(value, "tensor", [(i, i ^ bits) for i in range(4)])


def dot(a, b):
    return jnp.dot(a, b, preferred_element_type=FULL)


def dot_t(a, b):
    return lax.dot_general(a, b, (((1,), (1,)), ((), ())), preferred_element_type=FULL)


def rotate(values, cosine_tab, sine_tab, sign):
    half_width = values.shape[-1] // 2
    first_half = values[..., :half_width]
    second_half = values[..., half_width:]
    return jnp.concatenate(
        [
            first_half * cosine_tab - sign * second_half * sine_tab,
            second_half * cosine_tab + sign * first_half * sine_tab,
        ],
        axis=-1,
    )


def dot_rows(a, b):
    return lax.dot_general(a, b, (((0,), (0,)), ((), ())), preferred_element_type=FULL)


def wgrad_body(n_src, crossed, ring, order, where, *refs):
    sides, fans = refs[:n_src], refs[n_src : 2 * n_src]
    send_ref, keep_ref, total = refs[2 * n_src :]
    value = dot_rows(sides[0][...], fans[0][...])
    for side, fan in zip(sides[1:], fans[1:]):
        if crossed:
            value = value + dot_rows(side[:256], fan[256:]) + dot_rows(side[256:], fan[:256])
        else:
            value = value + dot_rows(side[...], fan[...])
    total[...] = value

    def piece(bits):
        start = pl.multiple_of(where[8 + bits], 64)
        return total[pl.ds(start, 64), :].astype(LOW)

    if ring == "z":
        send_ref[0:64] = piece(order[0])
        send_ref[64:128] = piece(order[1])
        keep_ref[0:64] = piece(order[2])
        keep_ref[64:128] = piece(order[3])
    else:
        step = pl.program_id(0)

        @pl.when(step < 2)
        def _():
            for bits in range(4):
                send_ref[64 * bits : 64 * bits + 64] = piece(bits)

        @pl.when(step >= 2)
        def _():
            for bits in range(4):
                keep_ref[64 * bits : 64 * bits + 64] = piece(bits)


def wgrad(place, half_at, sides, fans, ring, first, crossed=False):
    n_src = len(sides)
    width = fans[0].shape[1]
    x, z = place
    order = (first, 2, 0, 4 - first)
    if ring == "x":
        steps = [x ^ bits for bits in order]
    else:
        steps = [x ^ bits for bits in range(4)]
    whole = [half_at * 4 + step for step in steps]
    pieces = [(z ^ bits) * 64 for bits in range(4)]
    where = jnp.stack(steps + whole + pieces).astype(jnp.int32)
    tokens = sides[0].shape[0]

    def side_spec(side):
        shift = 4 if side.shape[1] == 2048 else 0
        return pl.BlockSpec((tokens, 256), lambda i, where: (0, where[shift + i]))

    in_specs = [side_spec(side) for side in sides]
    in_specs += [pl.BlockSpec((tokens, width), lambda i, where: (0, 0)) for _ in fans]
    if ring == "x":
        out_specs = [
            pl.BlockSpec((256, width), lambda i, where: (jnp.minimum(i, 1), 0)),
            pl.BlockSpec((256, width), lambda i, where: (jnp.maximum(i - 2, 0), 0)),
        ]
    else:
        out_specs = [pl.BlockSpec((128, width), lambda i, where: (i, 0))] * 2
    send, keep = pl.pallas_call(
        functools.partial(wgrad_body, n_src, crossed, ring, order),
        grid_spec=pltpu.PrefetchScalarGridSpec(
            num_scalar_prefetch=1,
            grid=(4,),
            in_specs=in_specs,
            out_specs=out_specs,
            scratch_shapes=[pltpu.VMEM((256, width), FULL)],
        ),
        out_shape=[jax.ShapeDtypeStruct((512, width), LOW)] * 2,
        compiler_params=pltpu.CompilerParams(
            vmem_limit_bytes=40 * 1024 * 1024, dimension_semantics=("arbitrary",)
        ),
        cost_estimate=pl.CostEstimate(
            flops=2 * n_src * tokens * 1024 * width,
            bytes_accessed=2 * n_src * tokens * (1024 + width) + 4 * 1024 * width,
            transcendentals=0,
        ),
    )(where, *sides, *fans)
    return send, keep


def scatter_ring(send, keep, ring, first):
    width = send.shape[1]
    shape = (4, 2, 64, width) if ring == "z" else (2, 4, 64, width)
    axis = 1 if ring == "z" else 0
    got = over_ring(send, ring, first).reshape(shape)
    keep = keep.reshape(shape)

    def part(which):
        mine = lax.index_in_dim(keep, which, axis, False).astype(FULL)
        return mine + lax.index_in_dim(got, which, axis, False).astype(FULL)

    got_next = over_ring(part(1).astype(LOW), ring, 4 - first)
    return part(0) + got_next.astype(FULL)


def scatter_blocks(value, ring, first):
    send = jnp.stack([value[first], value[2]]).astype(LOW)
    got = over_ring(send, ring, first).astype(FULL)
    got_next = over_ring((value[4 - first] + got[1]).astype(LOW), ring, 4 - first)
    return value[0] + got[0] + got_next.astype(FULL)


def scatter_yh(first_half, second_half, same):
    keep = jnp.where(same, first_half, second_half)
    send = jnp.where(same, second_half, first_half).astype(LOW)
    return keep + over_yh(send).astype(FULL)


def regroup(total, ring, at):
    parts = [total[0]]
    for bits in (1, 2, 3):
        parts.append(over_ring(total[bits].astype(LOW), ring, bits).astype(FULL))
    low_bit, high_bit = (at & 1) == 1, (at & 2) == 2
    a, b, c, d = parts
    a, b, c, d = (
        jnp.where(low_bit, b, a),
        jnp.where(low_bit, a, b),
        jnp.where(low_bit, d, c),
        jnp.where(low_bit, c, d),
    )
    a, b, c, d = (
        jnp.where(high_bit, c, a),
        jnp.where(high_bit, d, b),
        jnp.where(high_bit, a, c),
        jnp.where(high_bit, b, d),
    )
    return jnp.concatenate([a, b, c, d], axis=1)


def gather_side(value, core, ring):
    mine = lax.dynamic_slice_in_dim(value, core * 1024, 1024, 1)
    near = [over_ring(mine, ring, bits) for bits in (1, 3, 2)]
    far = [over_tensor(part, 1) for part in near]
    return near, far


def spread_columns(value, ring, at):
    width = value.shape[1] // 4
    out = [lax.dynamic_slice_in_dim(value, at * width, width, 1)]
    for bits in (1, 3, 2):
        part = lax.dynamic_slice_in_dim(value, (at ^ bits) * width, width, 1)
        out.append(over_ring(part, ring, bits))
    return out


def grouped_grad(place, core, yh, side, gathered, fan, ring):
    x, z = place
    at = x if ring == "x" else z
    other = "z" if ring == "x" else "x"
    near, far = gathered
    fans = spread_columns(fan, ring, at)
    halves = []
    for half, (sides, first) in enumerate([(near, 1), (far, 3)]):
        half_at = core ^ half
        send, keep = wgrad(place, half_at, [side] + sides, fans, other, first, half == 1)
        halves.append(scatter_ring(send, keep, other, first))
    total = scatter_yh(halves[0], halves[1], yh == core)
    return regroup(total, ring, at)


def plain_grad(place, core, yh, side, fan, ring):
    other = "z" if ring == "x" else "x"
    halves = []
    for half, first in enumerate([1, 3]):
        send, keep = wgrad(place, core ^ half, [side], [fan], ring, first)
        value = scatter_ring(send, keep, ring, first)
        halves.append(scatter_blocks(value, other, first))
    return scatter_yh(halves[0], halves[1], yh == core)


def scatter_rows(part):
    got = over_tensor(part(256, 512).astype(LOW), 1).astype(FULL)
    mine = part(0, 256)
    got_next = over_tensor((mine[128:] + got[128:]).astype(LOW), 2)
    return mine[:128] + got[:128] + got_next.astype(FULL)


def gather_rows(own):
    pair = jnp.concatenate([own, over_tensor(own, 2)], axis=0)
    return jnp.concatenate([pair, over_tensor(pair, 1)], axis=0)


def sum_everywhere(value):
    for ring in ("x", "z"):
        value = value + over_ring(value, ring, 1) + over_ring(value, ring, 2) + over_ring(value, ring, 3)
    value = value + over_yh(value)
    value = value + over_tensor(value, 2)
    return value + over_tensor(value, 1)


def per_device(
    hidden_in,
    cotangent,
    seq_lengths,
    slot_order,
    attn_gain,
    w_query,
    w_key,
    w_value,
    w_out,
    mlp_gain,
    w_gate,
    w_up,
    w_down,
):
    rows = hidden_in.shape[0]
    own_rows = rows // 4
    heads = w_query.shape[1] // HDIM
    group = heads // 2
    ff = w_gate.shape[1]
    scaling = HDIM ** (-0.5)
    dp_at = lax.axis_index("dp")
    yh, x, z = dp_at // 16, (dp_at // 4) % 4, dp_at % 4
    place = (x, z)
    tensor_at = lax.axis_index("tensor")
    core = tensor_at % 2
    is_even = core == 0
    blocks = [tensor_at ^ bits for bits in (0, 2, 1, 3)]

    def reorder(value):
        return jnp.concatenate(
            [lax.dynamic_slice_in_dim(value, at * own_rows, own_rows, 0) for at in blocks], axis=0
        )

    sequence = slot_order[0]
    length = jnp.sum(
        jnp.where(jnp.arange(seq_lengths.shape[0], dtype=jnp.int32) == sequence, seq_lengths, 0)
    )
    position = jnp.concatenate(
        [at * own_rows + jnp.arange(own_rows, dtype=jnp.int32) for at in blocks]
    )
    live_rows = position < length
    live = live_rows[:, None].astype(FULL)
    allowed = (position[None, :] <= position[:, None]) & live_rows[None, :]
    half_width = HDIM // 2
    exponent = jnp.arange(half_width, dtype=FULL) * (2.0 / HDIM)
    angles = position.astype(FULL)[:, None] / jnp.power(10000.0, exponent)[None, :]
    cosine_tab, sine_tab = jnp.cos(angles)[:, None, :], jnp.sin(angles)[:, None, :]
    gain_one = attn_gain.astype(FULL)
    gain_two = mlp_gain.astype(FULL)

    dy_low = reorder(cotangent)
    dy_gathered = gather_side(dy_low, core, "z")

    hidden_rows = reorder(hidden_in)
    inputs = hidden_rows.astype(FULL)
    inv_one = lax.rsqrt(jnp.mean(inputs * inputs, axis=-1, keepdims=True) + EPS)
    attn_in = (inputs * inv_one * gain_one).astype(LOW)

    query_rot = rotate(
        dot(attn_in, w_query).reshape(rows, heads, HDIM), cosine_tab, sine_tab, 1.0
    )
    queries = query_rot.astype(LOW).reshape(rows, 2, group, HDIM)
    key_value = dot(attn_in, jnp.concatenate([w_key, w_value], axis=1))
    key_mine = rotate(key_value[:, None, :HDIM], cosine_tab, sine_tab, 1.0)[:, 0].astype(LOW)
    value_mine = key_value[:, HDIM:].astype(LOW)
    packed = jnp.concatenate([key_mine, value_mine], axis=1)
    partner = over_tensor(packed, 1)
    partner = jnp.concatenate([partner[2 * own_rows :], partner[: 2 * own_rows]], axis=0)
    first = jnp.where(is_even, packed, partner)
    second = jnp.where(is_even, partner, packed)
    both = jnp.stack([first, second], axis=1)
    key_heads, value_heads = both[..., :HDIM], both[..., HDIM:]

    def masked_scores():
        raw_scores = (
            jnp.einsum("sgqd,tgd->gqst", queries, key_heads, preferred_element_type=FULL)
            * scaling
        )
        return jnp.where(allowed, raw_scores, -1e30)

    masked = masked_scores()
    row_max = jnp.max(masked, axis=-1, keepdims=True)
    exp_scores = jnp.exp(masked - row_max)
    row_total = jnp.sum(exp_scores, axis=-1, keepdims=True)
    lse_kept = row_max + jnp.log(row_total)
    probs_low = (exp_scores / row_total).astype(LOW)
    attended = jnp.einsum("gqst,tgd->sgqd", probs_low, value_heads, preferred_element_type=FULL)
    attended = attended.reshape(rows, heads * HDIM).astype(LOW)

    attn_sum = scatter_rows(lambda a, b: dot(attended[a:b], w_out))
    middle = inputs[:own_rows] + attn_sum
    inv_two = lax.rsqrt(jnp.mean(middle * middle, axis=-1, keepdims=True) + EPS)
    normed_two = middle * inv_two
    mlp_in = gather_rows((normed_two * gain_two).astype(LOW))
    mlp_gathered = gather_side(mlp_in, core, "x")

    gate_val = dot(mlp_in, w_gate).astype(LOW).astype(FULL)
    up_val = dot(mlp_in, w_up).astype(LOW).astype(FULL)
    sigmoid_gate = jax.nn.sigmoid(gate_val)
    activated = gate_val * sigmoid_gate
    hidden = (activated * up_val).astype(LOW)
    hidden_live = jnp.where(live_rows[:, None], hidden, jnp.zeros_like(hidden))
    grad_hidden = dot_t(dy_low, w_down) * live
    grad_gate = (
        grad_hidden * up_val * sigmoid_gate * (1.0 + gate_val * (1.0 - sigmoid_gate))
    ).astype(LOW)
    grad_up = (grad_hidden * activated).astype(LOW)

    down_pad = jnp.pad(hidden_live, ((0, 0), (0, 1536 - ff)))
    down_rows = grouped_grad(place, core, yh, dy_low, dy_gathered, down_pad, "z")

    mlp_back = scatter_rows(
        lambda a, b: dot_t(grad_gate[a:b], w_gate) + dot_t(grad_up[a:b], w_up)
    )
    gate_up = jnp.concatenate(
        [grad_gate, grad_up, jnp.zeros((rows, 3072 - 2 * ff), LOW)], axis=1
    )
    gate_up_rows = grouped_grad(place, core, yh, mlp_in, mlp_gathered, gate_up, "x")

    mlp_out = scatter_rows(lambda a, b: dot(hidden[a:b], w_down))
    output_rows = (middle + mlp_out).astype(LOW)

    scaled_two = mlp_back * gain_two
    dmid = dy_low[:own_rows].astype(FULL) * live[:own_rows] + inv_two * (
        scaled_two - normed_two * jnp.mean(scaled_two * normed_two, axis=-1, keepdims=True)
    )
    gain_two_part = jnp.sum(mlp_back * normed_two, axis=0)
    dmid_low = gather_rows(dmid.astype(LOW))

    out_rows = plain_grad(place, core, yh, dmid_low, attended, "z")

    grad_attended = dot_t(dmid_low, w_out).astype(LOW).reshape(rows, 2, group, HDIM)
    probs_again = jnp.where(allowed, jnp.exp(masked_scores() - lse_kept), 0.0)
    probs_again_low = probs_again.astype(LOW)
    grad_probs = jnp.einsum(
        "sgqd,tgd->gqst", grad_attended, value_heads, preferred_element_type=FULL
    )
    grad_values = jnp.einsum(
        "gqst,sgqd->tgd", probs_again_low, grad_attended, preferred_element_type=FULL
    )
    row_delta = jnp.sum(grad_probs * probs_again, axis=-1, keepdims=True)
    grad_scores = (probs_again * (grad_probs - row_delta)).astype(LOW)
    grad_queries = (
        jnp.einsum("gqst,tgd->sgqd", grad_scores, key_heads, preferred_element_type=FULL)
        * scaling
    )
    grad_keys = (
        jnp.einsum("gqst,sgqd->tgd", grad_scores, queries, preferred_element_type=FULL) * scaling
    )
    grad_both = jnp.concatenate([grad_keys, grad_values], axis=2)
    kept = jnp.where(is_even, grad_both[:, 0], grad_both[:, 1])
    sent = jnp.where(is_even, grad_both[:, 1], grad_both[:, 0])
    incoming = over_tensor(sent, 1)
    key_value_total = kept + jnp.concatenate(
        [incoming[2 * own_rows :], incoming[: 2 * own_rows]], axis=0
    )
    query_low = rotate(
        grad_queries.reshape(rows, heads, HDIM), cosine_tab, sine_tab, -1.0
    ).astype(LOW)
    query_low = query_low.reshape(rows, heads * HDIM)
    key_low = rotate(key_value_total[:, None, :HDIM], cosine_tab, sine_tab, -1.0)[:, 0].astype(LOW)
    key_value_low = jnp.concatenate([key_low, key_value_total[:, HDIM:].astype(LOW)], axis=1)
    qkv_low = jnp.concatenate([query_low, key_value_low], axis=1)

    front = plain_grad(place, core, yh, attn_in, qkv_low[:, :384], "z")
    back = plain_grad(place, core, yh, attn_in, qkv_low[:, 384:], "x")
    qkv_rows = jnp.concatenate([front, back], axis=1)

    w_key_value = jnp.concatenate([w_key, w_value], axis=1)
    attn_back = scatter_rows(
        lambda a, b: dot_t(query_low[a:b], w_query) + dot_t(key_value_low[a:b], w_key_value)
    )
    normed_one = inputs[:own_rows] * inv_one[:own_rows]
    scaled_one = attn_back * gain_one
    input_grad = dmid + inv_one[:own_rows] * (
        scaled_one - normed_one * jnp.mean(scaled_one * normed_one, axis=-1, keepdims=True)
    )
    gain_one_part = jnp.sum(attn_back * normed_one, axis=0)
    gains = sum_everywhere(jnp.stack([gain_one_part, gain_two_part]))
    q_cols = heads * HDIM
    return (
        output_rows,
        input_grad,
        gains[0],
        qkv_rows[:, :q_cols],
        qkv_rows[:, q_cols : q_cols + HDIM],
        qkv_rows[:, q_cols + HDIM :],
        out_rows.T,
        gains[1],
        gate_up_rows[:, :ff],
        gate_up_rows[:, ff : 2 * ff],
        down_rows[:, :ff].T,
    )


def solution(mesh):
    return jax.shard_map(
        per_device,
        mesh=mesh,
        in_specs=(
            P("dp", None),
            P("dp", None),
            P(),
            P("dp"),
            P(),
            P(None, "tensor"),
            P(None, "tensor"),
            P(None, "tensor"),
            P("tensor", None),
            P(),
            P(None, "tensor"),
            P(None, "tensor"),
            P("tensor", None),
        ),
        out_specs=(
            P(("dp", "tensor"), None),
            P(("dp", "tensor"), None),
            P(),
            P("dp", "tensor"),
            P("dp", "tensor"),
            P("dp", "tensor"),
            P("tensor", "dp"),
            P(),
            P("dp", "tensor"),
            P("dp", "tensor"),
            P("tensor", "dp"),
        ),
        check_vma=False,
    )
```

```python
import functools

import jax
import jax.numpy as jnp
from jax import lax
from jax.experimental import pallas as pl
from jax.experimental.pallas import tpu as pltpu
from jax.sharding import PartitionSpec as P

HDIM = 64
EPS = 1e-05
LOW = jnp.bfloat16
FULL = jnp.float32


def ring_perm(ring, bits):
    step = bits * (4 if ring == "x" else 1)
    return [(i, i ^ step) for i in range(32)]


class Links:
    def __init__(self):
        self.last = {}

    def send(self, value, ring, bits):
        names = [(ring, name) for name in ((1, 3) if bits == 2 else (bits,))]
        before = [self.last[name] for name in names if name in self.last]
        if before:
            value = tie(value, *before)
        out = over_ring(value, ring, bits)
        for name in names:
            self.last[name] = out
        return out


def over_ring(value, ring, bits):
    return lax.ppermute(value, "dp", ring_perm(ring, bits))


def over_yh(value):
    return lax.ppermute(value, "dp", [(i, i ^ 16) for i in range(32)])


def over_tensor(value, bits):
    return lax.ppermute(value, "tensor", [(i, i ^ bits) for i in range(4)])


def dot(a, b):
    return jnp.dot(a, b, preferred_element_type=FULL)


def dot_t(a, b):
    return lax.dot_general(a, b, (((1,), (1,)), ((), ())), preferred_element_type=FULL)


def rotate(values, cosine_tab, sine_tab, sign):
    half_width = values.shape[-1] // 2
    first_half = values[..., :half_width]
    second_half = values[..., half_width:]
    return jnp.concatenate(
        [
            first_half * cosine_tab - sign * second_half * sine_tab,
            second_half * cosine_tab + sign * first_half * sine_tab,
        ],
        axis=-1,
    )


def dot_rows(a, b):
    return lax.dot_general(a, b, (((0,), (0,)), ((), ())), preferred_element_type=FULL)


def wgrad_body(ring, orders, where, side, fan, *refs):
    step = pl.program_id(0)
    value = dot_rows(side[...], fan[...])
    if ring == "z":
        total = refs[4]
        total[...] = value

    for half in range(2):
        send_ref, keep_ref = refs[2 * half : 2 * half + 2]
        at = step - 4 * half
        if ring == "z":
            def piece(bits):
                start = pl.multiple_of(where[8 + bits], 64)
                return total[pl.ds(start, 64), :].astype(LOW)

            @pl.when((at >= 0) & (at < 4))
            def _():
                order = orders[half]
                send_ref[0:64] = piece(order[0])
                send_ref[64:128] = piece(order[1])
                keep_ref[0:64] = piece(order[2])
                keep_ref[64:128] = piece(order[3])
        else:

            @pl.when((at >= 0) & (at < 2))
            def _():
                send_ref[...] = value.astype(LOW)

            @pl.when((at >= 2) & (at < 4))
            def _():
                keep_ref[...] = value.astype(LOW)


def wgrad(place, core, side, fan, ring):
    tokens, width = fan.shape
    x, z = place
    orders = [(first, 2, 0, 4 - first) for first in (1, 3)]
    blocks = []
    for half in range(2):
        steps = orders[half] if ring == "x" else range(4)
        blocks += [(core ^ half) * 4 + (x ^ bits) for bits in steps]
    where = jnp.stack(blocks + [(z ^ bits) * 64 for bits in range(4)]).astype(jnp.int32)
    rows = 256 if ring == "x" else 128

    def place_of(low, high):
        return pl.BlockSpec((rows, width), lambda i, where: (jnp.clip(i - low, 0, high), 0))

    if ring == "x":
        out_specs = [place_of(low, 1) for low in (0, 2, 4, 6)]
    else:
        out_specs = [place_of(low, 3) for low in (0, 0, 4, 4)]
    return pl.pallas_call(
        functools.partial(wgrad_body, ring, orders),
        grid_spec=pltpu.PrefetchScalarGridSpec(
            num_scalar_prefetch=1,
            grid=(8,),
            in_specs=[
                pl.BlockSpec((tokens, 256), lambda i, where: (0, where[i])),
                pl.BlockSpec((tokens, width), lambda i, where: (0, 0)),
            ],
            out_specs=out_specs,
            scratch_shapes=[pltpu.VMEM((256, width), FULL)] if ring == "z" else [],
        ),
        out_shape=[jax.ShapeDtypeStruct((512, width), LOW)] * 4,
        compiler_params=pltpu.CompilerParams(
            vmem_limit_bytes=40 * 1024 * 1024, dimension_semantics=("arbitrary",)
        ),
        cost_estimate=pl.CostEstimate(
            flops=2 * tokens * 2048 * width,
            bytes_accessed=2 * tokens * (2048 + width) + 4 * 2048 * width,
            transcendentals=0,
        ),
    )(where, side, fan)


def wgrad_whole_body(count, *refs):
    sides, fans, out = refs[:count], refs[count : 2 * count], refs[2 * count]
    width = fans[0].shape[1]
    for at, (side, fan) in enumerate(zip(sides, fans)):
        value = dot_rows(side[...], fan[...]).astype(LOW)
        out[0, :, 0, :, at * width : (at + 1) * width] = value.reshape(4, 64, width)


def wgrad_whole(sides, fans):
    tokens, width = fans[0].shape
    count = len(fans)
    out = pl.pallas_call(
        functools.partial(wgrad_whole_body, count),
        grid=(8,),
        in_specs=[pl.BlockSpec((tokens, 256), lambda i: (0, i))] * count
        + [pl.BlockSpec((tokens, width), lambda i: (0, 0))] * count,
        out_specs=pl.BlockSpec(
            (1, 4, 1, 64, count * width), lambda i: (i % 4, 0, i // 4, 0, 0)
        ),
        out_shape=jax.ShapeDtypeStruct((4, 4, 2, 64, count * width), LOW),
        compiler_params=pltpu.CompilerParams(
            vmem_limit_bytes=40 * 1024 * 1024, dimension_semantics=("arbitrary",)
        ),
        cost_estimate=pl.CostEstimate(
            flops=2 * count * tokens * 2048 * width,
            bytes_accessed=2 * count * (tokens * (2048 + width) + 2048 * width),
            transcendentals=0,
        ),
    )(*sides, *fans)
    return out.reshape(2048, count * width)


def scatter_planes(value):
    groups = [[16 * yh + i for i in range(16)] for yh in range(2)]
    return lax.psum_scatter(
        value, "dp", scatter_dimension=0, axis_index_groups=groups, tiled=True
    )


def tie(value, *others):
    return lax.optimization_barrier((value, *others))[0]


class Grad:
    def __init__(self, links, place, core, side, fan, ring):
        self.links, self.ring = links, ring
        send0, keep0, send1, keep1 = wgrad(place, core, side, fan, ring)
        self.shape = (4, 2, 64, fan.shape[1]) if ring == "z" else (2, 4, 64, fan.shape[1])
        self.sent = [send0, send1]
        self.keep = [keep0.reshape(self.shape), keep1.reshape(self.shape)]

    def part(self, value, which):
        axis = 1 if self.ring == "z" else 0
        return lax.index_in_dim(value, which, axis, False).astype(FULL)

    def first(self):
        got = [self.links.send(self.sent[half], self.ring, (1, 3)[half]) for half in range(2)]
        self.got = [item.reshape(self.shape) for item in got]

    def second(self):
        self.sent = [
            (self.part(self.keep[half], 1) + self.part(self.got[half], 1)).astype(LOW)
            for half in range(2)
        ]
        self.got_next = [
            self.links.send(self.sent[half], self.ring, (3, 1)[half]) for half in range(2)
        ]

    def halves(self):
        halves = []
        for half in range(2):
            got_next = self.got_next[half]
            got = tie(self.got[half], got_next)
            halves.append(
                self.part(self.keep[half], 0) + self.part(got, 0) + got_next.astype(FULL)
            )
        return halves


def finish_together(links, grads, same):
    parts = [grad.halves() for grad in grads]
    values = [jnp.concatenate([part[half] for part in parts], axis=2) for half in range(2)]
    got, totals = [], []
    for half, first in enumerate((1, 3)):
        send = jnp.stack([values[half][first], values[half][2]]).astype(LOW)
        got.append(links.send(send, "x", first))
    got_next = []
    for half, first in enumerate((1, 3)):
        send = (values[half][4 - first] + got[half][1].astype(FULL)).astype(LOW)
        got_next.append(links.send(send, "x", 4 - first))
    for half in range(2):
        totals.append(
            values[half][0] + got[half][0].astype(FULL) + got_next[half].astype(FULL)
        )
    send = jnp.where(same, totals[1], totals[0]).astype(LOW)
    total = jnp.where(same, totals[0], totals[1]) + over_yh(send).astype(FULL)
    out, at = [], 0
    for part in parts:
        width = part[0].shape[2]
        out.append(total[:, at : at + width])
        at += width
    return out


def sent(*tasks):
    return [item for task in tasks for item in task.sent]


def sum_everywhere(value):
    for ring in ("x", "z"):
        value = value + over_ring(value, ring, 1) + over_ring(value, ring, 2) + over_ring(value, ring, 3)
    value = value + over_yh(value)
    value = value + over_tensor(value, 2)
    return value + over_tensor(value, 1)


def per_device(
    hidden_in,
    cotangent,
    seq_lengths,
    slot_order,
    attn_gain,
    w_query,
    w_key,
    w_value,
    w_out,
    mlp_gain,
    w_gate,
    w_up,
    w_down,
):
    rows = hidden_in.shape[0]
    own_rows = rows // 4
    heads = w_query.shape[1] // HDIM
    group = heads // 2
    ff = w_gate.shape[1]
    scaling = HDIM ** (-0.5)
    dp_at = lax.axis_index("dp")
    yh, x, z = dp_at // 16, (dp_at // 4) % 4, dp_at % 4
    place = (x, z)
    tensor_at = lax.axis_index("tensor")
    core = tensor_at % 2
    is_even = core == 0
    blocks = [tensor_at ^ bits for bits in (0, 2, 1, 3)]

    def reorder(value):
        return jnp.concatenate(
            [lax.dynamic_slice_in_dim(value, at * own_rows, own_rows, 0) for at in blocks], axis=0
        )

    sequence = slot_order[0]
    length = jnp.sum(
        jnp.where(jnp.arange(seq_lengths.shape[0], dtype=jnp.int32) == sequence, seq_lengths, 0)
    )
    position = jnp.concatenate(
        [at * own_rows + jnp.arange(own_rows, dtype=jnp.int32) for at in blocks]
    )
    live_rows = position < length
    live = live_rows[:, None].astype(FULL)
    allowed = (position[None, :] <= position[:, None]) & live_rows[None, :]
    half_width = HDIM // 2
    exponent = jnp.arange(half_width, dtype=FULL) * (2.0 / HDIM)
    angles = position.astype(FULL)[:, None] / jnp.power(10000.0, exponent)[None, :]
    cosine_tab, sine_tab = jnp.cos(angles)[:, None, :], jnp.sin(angles)[:, None, :]
    gain_one = attn_gain.astype(FULL)
    gain_two = mlp_gain.astype(FULL)

    links = Links()
    dy_low = reorder(cotangent)

    hidden_rows = reorder(hidden_in)
    inputs = hidden_rows.astype(FULL)
    inv_one = lax.rsqrt(jnp.mean(inputs * inputs, axis=-1, keepdims=True) + EPS)
    attn_in = (inputs * inv_one * gain_one).astype(LOW)

    key_value = dot(attn_in, jnp.concatenate([w_key, w_value], axis=1))
    key_mine = rotate(key_value[:, None, :HDIM], cosine_tab, sine_tab, 1.0)[:, 0].astype(LOW)
    value_mine = key_value[:, HDIM:].astype(LOW)
    packed = jnp.concatenate([key_mine, value_mine], axis=1)
    partner = over_tensor(packed, 1)
    query_rot = rotate(
        dot(tie(attn_in, packed), w_query).reshape(rows, heads, HDIM), cosine_tab, sine_tab, 1.0
    )
    queries = query_rot.astype(LOW).reshape(rows, 2, group, HDIM)
    partner = tie(partner, queries)
    partner = jnp.concatenate([partner[2 * own_rows :], partner[: 2 * own_rows]], axis=0)
    first = jnp.where(is_even, packed, partner)
    second = jnp.where(is_even, partner, packed)
    both = jnp.stack([first, second], axis=1)
    key_heads, value_heads = both[..., :HDIM], both[..., HDIM:]

    def masked_scores():
        raw_scores = (
            jnp.einsum("sgqd,tgd->gqst", queries, key_heads, preferred_element_type=FULL)
            * scaling
        )
        return jnp.where(allowed, raw_scores, -1e30)

    masked = masked_scores()
    row_max = jnp.max(masked, axis=-1, keepdims=True)
    exp_scores = jnp.exp(masked - row_max)
    row_total = jnp.sum(exp_scores, axis=-1, keepdims=True)
    lse_kept = row_max + jnp.log(row_total)
    probs_low = (exp_scores / row_total).astype(LOW)
    attended = jnp.einsum("gqst,tgd->sgqd", probs_low, value_heads, preferred_element_type=FULL)
    attended = attended.reshape(rows, heads * HDIM).astype(LOW)

    half = 2 * own_rows

    got = over_tensor(dot(attended[half:], w_out).astype(LOW), 1).astype(FULL)
    mine = dot(attended[:half], w_out)
    send = (mine[own_rows:] + got[own_rows:]).astype(LOW)
    got_next = over_tensor(send, 2)
    middle = inputs[:own_rows] + mine[:own_rows] + got[:own_rows] + got_next.astype(FULL)
    inv_two = lax.rsqrt(jnp.mean(middle * middle, axis=-1, keepdims=True) + EPS)
    normed_two = middle * inv_two
    own = (normed_two * gain_two).astype(LOW)

    got = over_tensor(own, 2)
    got_own = over_tensor(own, 1)
    grad_hidden = dot_t(tie(dy_low, own), w_down)
    got = tie(got, grad_hidden)
    mlp_in = jnp.concatenate([own, got, got_own, over_tensor(got, 1)], axis=0)

    gate_val = dot(mlp_in, w_gate).astype(LOW).astype(FULL)
    up_val = dot(mlp_in, w_up).astype(LOW).astype(FULL)
    sigmoid_gate = jax.nn.sigmoid(gate_val)
    activated = gate_val * sigmoid_gate
    hidden = (activated * up_val).astype(LOW)
    hidden_live = jnp.where(live_rows[:, None], hidden, jnp.zeros_like(hidden))
    grad_hidden = grad_hidden * live
    grad_gate = (
        grad_hidden * up_val * sigmoid_gate * (1.0 + gate_val * (1.0 - sigmoid_gate))
    ).astype(LOW)
    grad_up = (grad_hidden * activated).astype(LOW)

    def mlp_part(a, b):
        return dot_t(grad_gate[a:b], w_gate) + dot_t(grad_up[a:b], w_up)

    def grad_of(side, fan, ring):
        return Grad(links, place, core, side, fan, ring)

    same = yh == core
    mlp_grads = wgrad_whole([dy_low, mlp_in, mlp_in], [hidden_live, grad_gate, grad_up])
    mlp_sum = scatter_planes(mlp_grads)
    grad_gate = tie(grad_gate, mlp_grads)
    part_low = mlp_part(half, rows).astype(LOW)
    got = over_tensor(part_low, 1)
    mine = mlp_part(0, half)
    got = tie(got, mine).astype(FULL)
    send = (mine[own_rows:] + got[own_rows:]).astype(LOW)
    got_next = over_tensor(send, 2)
    mlp_back = mine[:own_rows] + got[:own_rows] + got_next.astype(FULL)

    scaled_two = mlp_back * gain_two
    dmid = dy_low[:own_rows].astype(FULL) * live[:own_rows] + inv_two * (
        scaled_two - normed_two * jnp.mean(scaled_two * normed_two, axis=-1, keepdims=True)
    )
    gain_two_part = jnp.sum(mlp_back * normed_two, axis=0)
    own = dmid.astype(LOW)
    got = over_tensor(own, 2)
    pair = jnp.concatenate([own, got], axis=0)
    got_last = over_tensor(pair, 1)
    dmid_low = jnp.concatenate([pair, got_last], axis=0)

    grad_attended = dot_t(dmid_low, w_out).astype(LOW).reshape(rows, 2, group, HDIM)
    probs_again = jnp.where(allowed, jnp.exp(masked_scores() - lse_kept), 0.0)
    probs_again_low = probs_again.astype(LOW)
    grad_probs = jnp.einsum(
        "sgqd,tgd->gqst", grad_attended, value_heads, preferred_element_type=FULL
    )
    grad_values = jnp.einsum(
        "gqst,sgqd->tgd", probs_again_low, grad_attended, preferred_element_type=FULL
    )
    row_delta = jnp.sum(grad_probs * probs_again, axis=-1, keepdims=True)
    grad_scores = (probs_again * (grad_probs - row_delta)).astype(LOW)
    grad_queries = (
        jnp.einsum("gqst,tgd->sgqd", grad_scores, key_heads, preferred_element_type=FULL)
        * scaling
    )
    grad_keys = (
        jnp.einsum("gqst,sgqd->tgd", grad_scores, queries, preferred_element_type=FULL) * scaling
    )
    grad_both = jnp.concatenate([grad_keys, grad_values], axis=2)
    kept = jnp.where(is_even, grad_both[:, 0], grad_both[:, 1])
    outgoing = jnp.where(is_even, grad_both[:, 1], grad_both[:, 0])
    incoming = over_tensor(outgoing, 1)
    out = grad_of(tie(dmid_low, outgoing), attended, "z")
    out.first()
    incoming = tie(incoming, *out.sent)
    key_value_total = kept + jnp.concatenate([incoming[half:], incoming[:half]], axis=0)
    query_low = rotate(
        grad_queries.reshape(rows, heads, HDIM), cosine_tab, sine_tab, -1.0
    ).astype(LOW)
    query_low = query_low.reshape(rows, heads * HDIM)
    key_low = rotate(key_value_total[:, None, :HDIM], cosine_tab, sine_tab, -1.0)[:, 0].astype(LOW)
    key_value_low = jnp.concatenate([key_low, key_value_total[:, HDIM:].astype(LOW)], axis=1)
    qkv_low = jnp.concatenate([query_low, key_value_low], axis=1)
    w_key_value = jnp.concatenate([w_key, w_value], axis=1)

    def attn_part(a, b):
        return dot_t(query_low[a:b], w_query) + dot_t(key_value_low[a:b], w_key_value)

    part_low = attn_part(half, rows).astype(LOW)
    got = over_tensor(part_low, 1).astype(FULL)
    mine = attn_part(0, half)
    send = (mine[own_rows:] + got[own_rows:]).astype(LOW)
    got_next = over_tensor(send, 2)
    qkv = grad_of(attn_in, tie(qkv_low, send), "z")
    qkv.first()
    got_next = tie(got_next, *qkv.sent)
    mlp_send = dot(tie(hidden, *qkv.sent)[half:], w_down).astype(LOW)
    mlp_got = over_tensor(mlp_send, 1)
    mlp_mine = dot(tie(hidden, mlp_send)[:half], w_down)
    out.second()
    got_next = tie(got_next, mlp_mine, *out.sent)
    attn_back = mine[:own_rows] + got[:own_rows] + got_next.astype(FULL)

    mlp_send = (mlp_mine[own_rows:] + mlp_got[own_rows:].astype(FULL)).astype(LOW)
    output_rows = middle + mlp_mine[:own_rows] + mlp_got[:own_rows].astype(FULL)
    output_rows = (output_rows + over_tensor(mlp_send, 2).astype(FULL)).astype(LOW)

    qkv.second()
    attn_back = tie(attn_back, *qkv.sent)
    out_rows, qkv_rows = finish_together(links, [out, qkv], same)
    mlp_send = lax.dynamic_slice_in_dim(mlp_sum, (1 - yh) * 64, 64, 0)
    mlp_rows = lax.dynamic_slice_in_dim(mlp_sum, yh * 64, 64, 0).astype(FULL)
    mlp_rows = mlp_rows + over_yh(mlp_send).astype(FULL)

    normed_one = inputs[:own_rows] * inv_one[:own_rows]
    scaled_one = attn_back * gain_one
    input_grad = dmid + inv_one[:own_rows] * (
        scaled_one - normed_one * jnp.mean(scaled_one * normed_one, axis=-1, keepdims=True)
    )
    gain_one_part = jnp.sum(attn_back * normed_one, axis=0)
    gains = sum_everywhere(jnp.stack([gain_one_part, gain_two_part]))
    q_cols = heads * HDIM
    return (
        output_rows,
        input_grad,
        gains[0],
        qkv_rows[:, :q_cols],
        qkv_rows[:, q_cols : q_cols + HDIM],
        qkv_rows[:, q_cols + HDIM :],
        out_rows.T,
        gains[1],
        mlp_rows[:, ff : 2 * ff],
        mlp_rows[:, 2 * ff :],
        mlp_rows[:, :ff].T,
    )


def solution(mesh):
    return jax.shard_map(
        per_device,
        mesh=mesh,
        in_specs=(
            P("dp", None),
            P("dp", None),
            P(),
            P("dp"),
            P(),
            P(None, "tensor"),
            P(None, "tensor"),
            P(None, "tensor"),
            P("tensor", None),
            P(),
            P(None, "tensor"),
            P(None, "tensor"),
            P("tensor", None),
        ),
        out_specs=(
            P(("dp", "tensor"), None),
            P(("dp", "tensor"), None),
            P(),
            P("dp", "tensor"),
            P("dp", "tensor"),
            P("dp", "tensor"),
            P("tensor", "dp"),
            P(),
            P("dp", "tensor"),
            P("dp", "tensor"),
            P("tensor", "dp"),
        ),
        check_vma=False,
    )
```

```python
import functools

import jax
import jax.numpy as jnp
import numpy as np
from jax import lax
from jax.experimental import pallas as pl
from jax.experimental.pallas import tpu as pltpu
from jax.sharding import PartitionSpec as P

HDIM = 64
EPS = 1e-05
LOW = jnp.bfloat16
FULL = jnp.float32


def ring_perm(ring, bits):
    step = bits * (4 if ring == "x" else 1)
    return [(i, i ^ step) for i in range(32)]


class Links:
    def __init__(self):
        self.last = {}

    def send(self, value, ring, bits):
        names = [(ring, name) for name in ((1, 3) if bits == 2 else (bits,))]
        before = [self.last[name] for name in names if name in self.last]
        if before:
            value = tie(value, *before)
        out = over_ring(value, ring, bits)
        for name in names:
            self.last[name] = out
        return out


def over_ring(value, ring, bits):
    return lax.ppermute(value, "dp", ring_perm(ring, bits))


def over_yh(value):
    return lax.ppermute(value, "dp", [(i, i ^ 16) for i in range(32)])


def over_tensor(value, bits):
    return lax.ppermute(value, "tensor", [(i, i ^ bits) for i in range(4)])


def dot(a, b):
    return jnp.dot(a, b, preferred_element_type=FULL)


def dot_t(a, b):
    return lax.dot_general(a, b, (((1,), (1,)), ((), ())), preferred_element_type=FULL)


def dot_rows(a, b):
    return lax.dot_general(a, b, (((0,), (0,)), ((), ())), preferred_element_type=FULL)


def rope_tables(rows):
    position = np.arange(rows, dtype=np.float32)[:, None]
    exponent = np.arange(HDIM // 2, dtype=np.float32) * np.float32(2.0 / HDIM)
    angles = position / np.power(np.float32(10000.0), exponent)[None, :]
    angles = angles.astype(np.float32).astype(np.float64)
    cosine, sine = np.cos(angles).astype(np.float32), np.sin(angles).astype(np.float32)
    return (
        np.concatenate([cosine] * 4, axis=1),
        np.concatenate([-sine, sine, -sine, sine], axis=1),
    )


def turned(value, cosine, sine):
    width = value.shape[1]
    lane = lax.broadcasted_iota(jnp.int32, value.shape, 1) % HDIM
    swapped = jnp.where(
        lane < HDIM // 2,
        pltpu.roll(value, width - HDIM // 2, 1),
        pltpu.roll(value, HDIM // 2, 1),
    )
    count = width // 128
    if count > 1:
        cosine = jnp.concatenate([cosine] * count, axis=1)
        sine = jnp.concatenate([sine] * count, axis=1)
    return value * cosine + swapped * sine


def project_body(where, rows, gain, w_query, w_key, w_value, cosine, sine, *refs):
    normed_out, query_out, pair_out, cosine_out, sine_out, w_pair = refs
    cosine_out[...] = cosine[...]
    sine_out[...] = sine[...]

    @pl.when(pl.program_id(0) == 0)
    def _():
        w_pair[...] = jnp.concatenate([w_key[...], w_value[...]], axis=0)

    value = rows[...].astype(FULL)
    inv = lax.rsqrt(jnp.mean(value * value, axis=-1, keepdims=True) + EPS)
    normed = (value * inv * gain[...].astype(FULL)).astype(LOW)
    normed_out[...] = normed
    query_out[...] = turned(dot(normed, w_query[...]), cosine[...], sine[...]).astype(LOW)
    pair = dot_t(normed, w_pair[...])
    lane = lax.broadcasted_iota(jnp.int32, pair.shape, 1)
    pair_out[...] = jnp.where(lane < HDIM, turned(pair, cosine[...], sine[...]), pair).astype(LOW)


def project(blocks, hidden_in, gain, w_query, w_key, w_value):
    rows, model = hidden_in.shape
    step = rows // 4
    cosine, sine = rope_tables(rows)

    def chosen(width):
        return pl.BlockSpec((step, width), lambda i, where: (where[i], 0))

    def whole(value):
        return pl.BlockSpec(value.shape, lambda i, where: (0, 0))

    def placed(width):
        return pl.BlockSpec((step, width), lambda i, where: (i, 0))

    heads = w_query.shape[1]
    return pl.pallas_call(
        project_body,
        grid_spec=pltpu.PrefetchScalarGridSpec(
            num_scalar_prefetch=1,
            grid=(4,),
            in_specs=[
                chosen(model),
                whole(gain),
                whole(w_query),
                whole(w_key),
                whole(w_value),
                chosen(128),
                chosen(128),
            ],
            out_specs=[placed(model), placed(heads)] + [placed(2 * HDIM)] * 3,
            scratch_shapes=[pltpu.VMEM((2 * HDIM, model), LOW)],
        ),
        out_shape=[
            jax.ShapeDtypeStruct((rows, model), LOW),
            jax.ShapeDtypeStruct((rows, heads), LOW),
            jax.ShapeDtypeStruct((rows, 2 * HDIM), LOW),
            jax.ShapeDtypeStruct((rows, 2 * HDIM), FULL),
            jax.ShapeDtypeStruct((rows, 2 * HDIM), FULL),
        ],
        compiler_params=pltpu.CompilerParams(
            vmem_limit_bytes=60 * 1024 * 1024, dimension_semantics=("arbitrary",)
        ),
        cost_estimate=pl.CostEstimate(
            flops=2 * rows * model * (heads + 2 * HDIM),
            bytes_accessed=2 * (2 * rows * model + model * (heads + 4 * HDIM) + rows * 640),
            transcendentals=rows,
        ),
    )(
        jnp.stack(blocks).astype(jnp.int32),
        hidden_in,
        gain,
        w_query,
        w_key,
        w_value,
        jnp.asarray(cosine),
        jnp.asarray(sine),
    )


def swap_halves(value):
    half = value.shape[0] // 2
    return jnp.concatenate([value[half:], value[:half]], axis=0)


def heads_of(where, mine, partner, step):
    use_mine = (step // 2 == 0) == (where[4] == 1)
    return jnp.where(use_mine, mine[...].astype(FULL), swap_halves(partner[...]).astype(FULL))


def allowed_pairs(where, rows):
    step = rows // 4

    def positions(shape, axis):
        index = lax.broadcasted_iota(jnp.int32, shape, axis)
        base = where[3] - 3
        for block in (2, 1, 0):
            base = jnp.where(index < (block + 1) * step, where[block] - block, base)
        return index + base * step

    keys, queries = positions((rows, 1), 0), positions((1, rows), 1)
    return (keys <= queries) & (keys < where[5])


def placed_heads(head):
    low = lax.broadcasted_iota(jnp.int32, head.shape, 1) < HDIM
    return (
        jnp.where(low, head, 0.0).astype(LOW),
        jnp.where(low, 0.0, pltpu.roll(head, HDIM, 1)).astype(LOW),
    )


def attend_body(where, query, mine, partner, out, lse_out):
    both = heads_of(where, mine, partner, pl.program_id(0))
    allowed = allowed_pairs(where, both.shape[0])
    value_t = both.T[HDIM:].astype(LOW)
    mixed = []
    for index, key in enumerate(placed_heads(both)):
        scores = dot_t(key, query[...]) * HDIM ** (-0.5)
        scores = jnp.where(allowed, scores, -1e30)
        top = jnp.max(scores, axis=0, keepdims=True)
        weights = jnp.exp(scores - top)
        total = jnp.sum(weights, axis=0, keepdims=True)
        lse_out[0, index : index + 1, :] = top + jnp.log(total)
        mixed.append(dot(value_t, (weights / total).astype(LOW)))
    out[...] = jnp.concatenate(mixed, axis=0).T.astype(LOW)


def attend_specs(rows, lanes):
    pair = pl.BlockSpec((rows, lanes), lambda i, where: (0, i))
    whole = pl.BlockSpec((rows, lanes), lambda i, where: (0, 0))
    lse = pl.BlockSpec((1, 2, rows), lambda i, where: (i, 0, 0))
    return pair, whole, lse


def attend(where, query, mine, partner):
    rows, lanes = mine.shape
    steps = query.shape[1] // lanes
    pair, whole, lse = attend_specs(rows, lanes)
    return pl.pallas_call(
        attend_body,
        grid_spec=pltpu.PrefetchScalarGridSpec(
            num_scalar_prefetch=1,
            grid=(steps,),
            in_specs=[pair, whole, whole],
            out_specs=[pair, lse],
        ),
        out_shape=[
            jax.ShapeDtypeStruct(query.shape, LOW),
            jax.ShapeDtypeStruct((steps, 2, rows), FULL),
        ],
        compiler_params=pltpu.CompilerParams(
            vmem_limit_bytes=24 * 1024 * 1024, dimension_semantics=("arbitrary",)
        ),
        cost_estimate=pl.CostEstimate(
            flops=4 * rows * rows * query.shape[1],
            bytes_accessed=8 * rows * query.shape[1],
            transcendentals=2 * steps * rows * rows,
        ),
    )(where, query, mine, partner)


def attend_back_body(where, query, mine, partner, grad, lse, cosine, sine, dquery, dboth, acc):
    step = pl.program_id(0)
    both = heads_of(where, mine, partner, step)
    allowed = allowed_pairs(where, both.shape[0])
    low = lax.broadcasted_iota(jnp.int32, both.shape, 1) < HDIM
    key_t = both.T[:HDIM].astype(LOW)
    keys = placed_heads(both)
    values = placed_heads(pltpu.roll(both, HDIM, 1))
    dkeys, dvalues, mixed = [], [], []
    for index in range(2):
        scores = dot_t(keys[index], query[...]) * HDIM ** (-0.5)
        probs = jnp.where(allowed, jnp.exp(scores - lse[0, index : index + 1, :]), 0.0)
        dprobs = dot_t(values[index], grad[...])
        delta = jnp.sum(dprobs * probs, axis=0, keepdims=True)
        dscores = (probs * (dprobs - delta)).astype(LOW)
        dvalues.append(dot(probs.astype(LOW), grad[...]))
        dkeys.append(dot(dscores, query[...]))
        mixed.append(dot(key_t, dscores))
    turn_back = jnp.concatenate(mixed, axis=0).T * HDIM ** (-0.5)
    dquery[...] = turned(turn_back, cosine[...], -sine[...]).astype(LOW)
    dkey = jnp.where(low, dkeys[0], dkeys[1]) * HDIM ** (-0.5)
    dvalue = jnp.where(low, dvalues[0], dvalues[1])

    @pl.when(step % 2 == 0)
    def _():
        acc[0], acc[1] = dkey, dvalue

    @pl.when(step % 2 == 1)
    def _():
        key_sum, value_sum = acc[0] + dkey, acc[1] + dvalue
        dboth[0] = jnp.where(
            low,
            key_sum + pltpu.roll(key_sum, HDIM, 1),
            value_sum + pltpu.roll(value_sum, HDIM, 1),
        )


def attend_back(where, query, mine, partner, grad, lse, cosine, sine):
    rows, lanes = mine.shape
    steps = query.shape[1] // lanes
    pair, whole, lse_spec = attend_specs(rows, lanes)
    slot = pl.BlockSpec((1, rows, lanes), lambda i, where: ((i // 2) ^ (1 - where[4]), 0, 0))
    return pl.pallas_call(
        attend_back_body,
        grid_spec=pltpu.PrefetchScalarGridSpec(
            num_scalar_prefetch=1,
            grid=(steps,),
            in_specs=[pair, whole, whole, pair, lse_spec, whole, whole],
            out_specs=[pair, slot],
            scratch_shapes=[pltpu.VMEM((2, rows, lanes), FULL)],
        ),
        out_shape=[
            jax.ShapeDtypeStruct(query.shape, LOW),
            jax.ShapeDtypeStruct((2, rows, lanes), FULL),
        ],
        compiler_params=pltpu.CompilerParams(
            vmem_limit_bytes=24 * 1024 * 1024, dimension_semantics=("arbitrary",)
        ),
        cost_estimate=pl.CostEstimate(
            flops=10 * rows * rows * query.shape[1],
            bytes_accessed=8 * rows * query.shape[1],
            transcendentals=2 * steps * rows * rows,
        ),
    )(where, query, mine, partner, grad, lse, cosine, sine)


def join_back_body(dboth, incoming, cosine, sine, out):
    total = dboth[0] + swap_halves(incoming[...])
    low = lax.broadcasted_iota(jnp.int32, total.shape, 1) < HDIM
    out[...] = jnp.where(low, turned(total, cosine[...], -sine[...]), total).astype(LOW)


def join_back(dboth, incoming, cosine, sine):
    return pl.pallas_call(
        join_back_body,
        out_shape=jax.ShapeDtypeStruct(incoming.shape, LOW),
        compiler_params=pltpu.CompilerParams(vmem_limit_bytes=24 * 1024 * 1024),
    )(dboth, incoming, cosine, sine)


def feed_body(*refs):
    pieces, (w_gate, w_up, dhidden) = refs[:4], refs[4:7]
    rows_out, hidden_out, dgate_out, dup_out = refs[7:]
    step = pieces[0].shape[0]

    @pl.when(pl.program_id(0) == 0)
    def _():
        for index, piece in enumerate(pieces):
            rows_out[index * step : (index + 1) * step] = piece[...]

    gate = dot(rows_out[...], w_gate[...]).astype(LOW).astype(FULL)
    up = dot(rows_out[...], w_up[...]).astype(LOW).astype(FULL)
    sigmoid = jax.nn.sigmoid(gate)
    activated = gate * sigmoid
    hidden_out[...] = (activated * up).astype(LOW)
    back = dhidden[...]
    dgate_out[...] = (back * up * sigmoid * (1.0 + gate * (1.0 - sigmoid))).astype(LOW)
    dup_out[...] = (back * activated).astype(LOW)


def feed(pieces, w_gate, w_up, dhidden):
    rows, width = dhidden.shape
    model = w_gate.shape[0]
    across = pl.BlockSpec((rows, 256), lambda i: (0, i))
    weight = pl.BlockSpec((model, 256), lambda i: (0, i))
    piece = pl.BlockSpec(pieces[0].shape, lambda i: (0, 0))
    return pl.pallas_call(
        feed_body,
        grid=(pl.cdiv(width, 256),),
        in_specs=[piece] * 4 + [weight, weight, across],
        out_specs=[pl.BlockSpec((rows, model), lambda i: (0, 0))] + [across] * 3,
        out_shape=[jax.ShapeDtypeStruct((rows, model), LOW)]
        + [jax.ShapeDtypeStruct((rows, width), LOW)] * 3,
        compiler_params=pltpu.CompilerParams(
            vmem_limit_bytes=60 * 1024 * 1024, dimension_semantics=("arbitrary",)
        ),
        cost_estimate=pl.CostEstimate(
            flops=4 * rows * model * width,
            bytes_accessed=4 * model * width + 10 * rows * width + 4 * rows * model,
            transcendentals=rows * width,
        ),
    )(*pieces, w_gate, w_up, dhidden)


def feed_back_body(dgate, dup, w_gate, w_up, mine, other):
    value = dot_t(dgate[...], w_gate[...]) + dot_t(dup[...], w_up[...])
    half = value.shape[0] // 2
    mine[...] = value[:half]
    other[...] = value[half:].astype(LOW)


def feed_back(dgate, dup, w_gate, w_up):
    rows, width = dgate.shape
    model = w_gate.shape[0]
    whole = pl.BlockSpec((rows, width), lambda i: (0, 0))
    weight = pl.BlockSpec((256, width), lambda i: (i, 0))
    across = pl.BlockSpec((rows // 2, 256), lambda i: (0, i))
    return pl.pallas_call(
        feed_back_body,
        grid=(model // 256,),
        in_specs=[whole, whole, weight, weight],
        out_specs=[across, across],
        out_shape=[
            jax.ShapeDtypeStruct((rows // 2, model), FULL),
            jax.ShapeDtypeStruct((rows // 2, model), LOW),
        ],
        compiler_params=pltpu.CompilerParams(
            vmem_limit_bytes=60 * 1024 * 1024, dimension_semantics=("arbitrary",)
        ),
        cost_estimate=pl.CostEstimate(
            flops=4 * rows * model * width,
            bytes_accessed=4 * model * width + 4 * rows * width + 3 * rows * model,
            transcendentals=0,
        ),
    )(dgate, dup, w_gate, w_up)


def wgrad_body(ring, orders, where, side, fan, *refs):
    step = pl.program_id(0)
    value = dot_rows(side[...], fan[...])
    if ring == "z":
        total = refs[4]
        total[...] = value

    for half in range(2):
        send_ref, keep_ref = refs[2 * half : 2 * half + 2]
        at = step - 4 * half
        if ring == "z":
            def piece(bits):
                start = pl.multiple_of(where[8 + bits], 64)
                return total[pl.ds(start, 64), :].astype(LOW)

            @pl.when((at >= 0) & (at < 4))
            def _():
                order = orders[half]
                send_ref[0:64] = piece(order[0])
                send_ref[64:128] = piece(order[1])
                keep_ref[0:64] = piece(order[2])
                keep_ref[64:128] = piece(order[3])
        else:

            @pl.when((at >= 0) & (at < 2))
            def _():
                send_ref[...] = value.astype(LOW)

            @pl.when((at >= 2) & (at < 4))
            def _():
                keep_ref[...] = value.astype(LOW)


def wgrad(place, core, side, fan, ring):
    tokens, width = fan.shape
    x, z = place
    orders = [(first, 2, 0, 4 - first) for first in (1, 3)]
    blocks = []
    for half in range(2):
        steps = orders[half] if ring == "x" else range(4)
        blocks += [(core ^ half) * 4 + (x ^ bits) for bits in steps]
    where = jnp.stack(blocks + [(z ^ bits) * 64 for bits in range(4)]).astype(jnp.int32)
    rows = 256 if ring == "x" else 128

    def place_of(low, high):
        return pl.BlockSpec((rows, width), lambda i, where: (jnp.clip(i - low, 0, high), 0))

    if ring == "x":
        out_specs = [place_of(low, 1) for low in (0, 2, 4, 6)]
    else:
        out_specs = [place_of(low, 3) for low in (0, 0, 4, 4)]
    return pl.pallas_call(
        functools.partial(wgrad_body, ring, orders),
        grid_spec=pltpu.PrefetchScalarGridSpec(
            num_scalar_prefetch=1,
            grid=(8,),
            in_specs=[
                pl.BlockSpec((tokens, 256), lambda i, where: (0, where[i])),
                pl.BlockSpec((tokens, width), lambda i, where: (0, 0)),
            ],
            out_specs=out_specs,
            scratch_shapes=[pltpu.VMEM((256, width), FULL)] if ring == "z" else [],
        ),
        out_shape=[jax.ShapeDtypeStruct((512, width), LOW)] * 4,
        compiler_params=pltpu.CompilerParams(
            vmem_limit_bytes=24 * 1024 * 1024, dimension_semantics=("arbitrary",)
        ),
        cost_estimate=pl.CostEstimate(
            flops=2 * tokens * 2048 * width,
            bytes_accessed=2 * tokens * (2048 + width) + 4 * 2048 * width,
            transcendentals=0,
        ),
    )(where, side, fan)


def wgrad_whole_body(count, *refs):
    sides, fans, out = refs[:count], refs[count : 2 * count], refs[2 * count]
    width = fans[0].shape[1]
    for at, (side, fan) in enumerate(zip(sides, fans)):
        value = dot_rows(side[...], fan[...]).astype(LOW)
        out[0, :, 0, :, at * width : (at + 1) * width] = value.reshape(4, 64, width)


def wgrad_whole(sides, fans):
    tokens, width = fans[0].shape
    count = len(fans)
    out = pl.pallas_call(
        functools.partial(wgrad_whole_body, count),
        grid=(8,),
        in_specs=[pl.BlockSpec((tokens, 256), lambda i: (0, i))] * count
        + [pl.BlockSpec((tokens, width), lambda i: (0, 0))] * count,
        out_specs=pl.BlockSpec(
            (1, 4, 1, 64, count * width), lambda i: (i % 4, 0, i // 4, 0, 0)
        ),
        out_shape=jax.ShapeDtypeStruct((4, 4, 2, 64, count * width), LOW),
        compiler_params=pltpu.CompilerParams(
            vmem_limit_bytes=60 * 1024 * 1024, dimension_semantics=("arbitrary",)
        ),
        cost_estimate=pl.CostEstimate(
            flops=2 * count * tokens * 2048 * width,
            bytes_accessed=2 * count * (tokens * (2048 + width) + 2048 * width),
            transcendentals=0,
        ),
    )(*sides, *fans)
    return out.reshape(2048, count * width)


def scatter_planes(value):
    groups = [[16 * yh + i for i in range(16)] for yh in range(2)]
    return lax.psum_scatter(
        value, "dp", scatter_dimension=0, axis_index_groups=groups, tiled=True
    )


def tie(value, *others):
    return lax.optimization_barrier((value, *others))[0]


class Grad:
    def __init__(self, links, place, core, side, fan, ring):
        self.links, self.ring = links, ring
        send0, keep0, send1, keep1 = wgrad(place, core, side, fan, ring)
        self.shape = (4, 2, 64, fan.shape[1]) if ring == "z" else (2, 4, 64, fan.shape[1])
        self.sent = [send0, send1]
        self.keep = [keep0.reshape(self.shape), keep1.reshape(self.shape)]

    def part(self, value, which):
        axis = 1 if self.ring == "z" else 0
        return lax.index_in_dim(value, which, axis, False).astype(FULL)

    def first(self):
        got = [self.links.send(self.sent[half], self.ring, (1, 3)[half]) for half in range(2)]
        self.got = [item.reshape(self.shape) for item in got]

    def second(self):
        self.sent = [
            (self.part(self.keep[half], 1) + self.part(self.got[half], 1)).astype(LOW)
            for half in range(2)
        ]
        self.got_next = [
            self.links.send(self.sent[half], self.ring, (3, 1)[half]) for half in range(2)
        ]

    def halves(self):
        halves = []
        for half in range(2):
            got_next = self.got_next[half]
            got = tie(self.got[half], got_next)
            halves.append(
                self.part(self.keep[half], 0) + self.part(got, 0) + got_next.astype(FULL)
            )
        return halves


class End:
    def __init__(self, links, grad, at):
        ring = "z" if grad.ring == "x" else "x"
        values = jnp.stack(grad.halves(), axis=1)

        def block(bits):
            index = at ^ bits if ring == "z" else bits
            return lax.dynamic_index_in_dim(values, index, 0, False)

        self.keep = block(0)
        self.sent = [block(bits).astype(LOW) for bits in (1, 3, 2)]
        self.got = [over_ring(item, ring, bits) for item, bits in zip(self.sent, (1, 3, 2))]

    def totals(self):
        return self.keep + sum(item.astype(FULL) for item in self.got)


def finish_together(ends, same):
    parts = [end.totals() for end in ends]
    values = jnp.concatenate(parts, axis=2)
    send = jnp.where(same, values[1], values[0]).astype(LOW)
    total = jnp.where(same, values[0], values[1]) + over_yh(send).astype(FULL)
    out, at = [], 0
    for part in parts:
        width = part.shape[2]
        out.append(total[:, at : at + width])
        at += width
    return out


def sent(*tasks):
    return [item for task in tasks for item in task.sent]


def per_device(
    hidden_in,
    cotangent,
    seq_lengths,
    slot_order,
    attn_gain,
    w_query,
    w_key,
    w_value,
    w_out,
    mlp_gain,
    w_gate,
    w_up,
    w_down,
):
    rows = hidden_in.shape[0]
    own_rows = rows // 4
    heads = w_query.shape[1] // HDIM
    ff = w_gate.shape[1]
    dp_at = lax.axis_index("dp")
    yh, x, z = dp_at // 16, (dp_at // 4) % 4, dp_at % 4
    place = (x, z)
    tensor_at = lax.axis_index("tensor")
    core = tensor_at % 2
    blocks = [tensor_at ^ bits for bits in (0, 2, 1, 3)]

    def reorder(value):
        return jnp.concatenate(
            [lax.dynamic_slice_in_dim(value, at * own_rows, own_rows, 0) for at in blocks], axis=0
        )

    sequence = slot_order[0]
    length = jnp.sum(
        jnp.where(jnp.arange(seq_lengths.shape[0], dtype=jnp.int32) == sequence, seq_lengths, 0)
    )
    position = jnp.concatenate(
        [at * own_rows + jnp.arange(own_rows, dtype=jnp.int32) for at in blocks]
    )
    live_rows = position < length
    gain_one = attn_gain.astype(FULL)
    gain_two = mlp_gain.astype(FULL)

    links = Links()
    dy_low = jnp.where(live_rows[:, None], reorder(cotangent), jnp.zeros((), LOW))

    attn_in, queries, packed, cosine, sine = project(
        blocks, hidden_in, attn_gain[None, :], w_query, w_key.T, w_value.T
    )
    partner = over_tensor(packed, 1)
    where = jnp.stack(blocks + [1 - core, length]).astype(jnp.int32)
    attended, lse = attend(where, queries, packed, partner)

    half = 2 * own_rows

    got = over_tensor(dot(attended[half:], w_out).astype(LOW), 1)
    mine = dot(attended[:half], w_out)
    send = (mine[own_rows:] + got[own_rows:].astype(FULL)).astype(LOW)
    got_next = over_tensor(send, 2)
    inputs = lax.dynamic_slice_in_dim(hidden_in, tensor_at * own_rows, own_rows, 0).astype(FULL)
    got = tie(got, got_next)
    middle = inputs + mine[:own_rows] + got[:own_rows].astype(FULL) + got_next.astype(FULL)
    inv_two = lax.rsqrt(jnp.mean(middle * middle, axis=-1, keepdims=True) + EPS)
    normed_two = middle * inv_two
    own = (normed_two * gain_two).astype(LOW)

    got = over_tensor(own, 2)
    got_own = over_tensor(own, 1)
    grad_hidden = dot_t(tie(dy_low, own), w_down)
    got = tie(got, grad_hidden)
    mlp_in, hidden, grad_gate, grad_up = feed(
        [own, got, got_own, over_tensor(got, 1)], w_gate, w_up, grad_hidden
    )

    def grad_of(side, fan, ring):
        return Grad(links, place, core, side, fan, ring)

    same = yh == core
    mlp_grads = wgrad_whole([dy_low, mlp_in, mlp_in], [hidden, grad_gate, grad_up])
    mlp_sum = scatter_planes(mlp_grads)
    grad_gate = tie(grad_gate, mlp_grads)
    mine, other = feed_back(grad_gate, grad_up, w_gate, w_up)
    got = over_tensor(other, 1)
    send = (mine[own_rows:] + got[own_rows:].astype(FULL)).astype(LOW)
    got_next = over_tensor(send, 2)
    mlp_send = dot(tie(hidden, send)[half:], w_down).astype(LOW)
    mlp_got = over_tensor(mlp_send, 1)
    mlp_mine = dot(tie(hidden, mlp_send)[:half], w_down)
    got_next = tie(got_next, mlp_mine)
    got = tie(got, got_next)
    mlp_back = mine[:own_rows] + got[:own_rows].astype(FULL) + got_next.astype(FULL)

    scaled_two = mlp_back * gain_two
    dmid = dy_low[:own_rows].astype(FULL) + inv_two * (
        scaled_two - normed_two * jnp.mean(scaled_two * normed_two, axis=-1, keepdims=True)
    )
    gain_two_part = jnp.sum(mlp_back * normed_two, axis=0)
    own = dmid.astype(LOW)
    got = over_tensor(own, 2)
    mlp_got = tie(mlp_got, own)
    mlp_send = (mlp_mine[own_rows:] + mlp_got[own_rows:].astype(FULL)).astype(LOW)
    output_rows = middle + mlp_mine[:own_rows] + mlp_got[:own_rows].astype(FULL)
    got = tie(got, mlp_send, output_rows)
    mlp_got = over_tensor(tie(mlp_send, got), 2)
    pair = jnp.concatenate([own, got], axis=0)
    got_last = over_tensor(pair, 1)
    dmid_low = jnp.concatenate([pair, got_last], axis=0)

    grad_attended = dot_t(dmid_low, w_out).astype(LOW)
    query_low, dboth = attend_back(
        where, queries, packed, partner, grad_attended, lse, cosine, sine
    )
    incoming = over_tensor(dboth[1], 1)
    incoming = tie(incoming, mlp_got)
    key_value_low = join_back(dboth, incoming, cosine, sine)
    qkv_low = jnp.concatenate([query_low, key_value_low], axis=1)
    w_key_value = jnp.concatenate([w_key, w_value], axis=1)

    def attn_part(a, b):
        return dot_t(query_low[a:b], w_query) + dot_t(key_value_low[a:b], w_key_value)

    part_low = attn_part(half, rows).astype(LOW)
    got = over_tensor(part_low, 1)
    mine = attn_part(0, half)
    send = (mine[own_rows:] + got[own_rows:].astype(FULL)).astype(LOW)
    got_next = over_tensor(send, 2)
    qkv = grad_of(attn_in, tie(qkv_low, send), "z")
    qkv.first()
    out = grad_of(tie(dmid_low, *qkv.sent), attended, "x")
    out.first()
    got_next = tie(got_next, *out.sent)
    got = tie(got, got_next)
    attn_back = mine[:own_rows] + got[:own_rows].astype(FULL) + got_next.astype(FULL)

    output_rows = (output_rows + mlp_got.astype(FULL)).astype(LOW)

    inv_one = lax.rsqrt(jnp.mean(inputs * inputs, axis=-1, keepdims=True) + EPS)
    normed_one = inputs * inv_one
    scaled_one = attn_back * gain_one
    input_grad = dmid + inv_one * (
        scaled_one - normed_one * jnp.mean(scaled_one * normed_one, axis=-1, keepdims=True)
    )
    gain_one_part = jnp.sum(attn_back * normed_one, axis=0)
    mlp_keep = lax.dynamic_slice_in_dim(mlp_sum, yh * 64, 64, 0).astype(FULL)
    mlp_send = lax.dynamic_slice_in_dim(mlp_sum, (1 - yh) * 64, 64, 0)
    gains = jnp.stack([gain_one_part, gain_two_part])
    for bits in (1, 3):
        gains = gains + over_ring(gains, "x", bits)
    for bits in (1, 3):
        gains = gains + over_ring(gains, "z", bits)
    out.second()
    qkv.second()
    gains = tie(gains, *sent(out, qkv), mlp_send)
    mlp_rows_got = over_yh(mlp_send)
    gains = gains + over_yh(gains)
    gains = gains + over_tensor(gains, 2)
    gains = gains + over_tensor(gains, 1)
    qkv.got_next[0] = tie(qkv.got_next[0], mlp_rows_got)
    ends = [End(links, out, z), End(links, qkv, x)]
    out_rows, qkv_rows = finish_together(ends, same)
    mlp_rows = mlp_keep + mlp_rows_got.astype(FULL)
    q_cols = heads * HDIM
    return (
        output_rows,
        input_grad,
        gains[0],
        qkv_rows[:, :q_cols],
        qkv_rows[:, q_cols : q_cols + HDIM],
        qkv_rows[:, q_cols + HDIM :],
        out_rows.T,
        gains[1],
        mlp_rows[:, ff : 2 * ff],
        mlp_rows[:, 2 * ff :],
        mlp_rows[:, :ff].T,
    )


def solution(mesh):
    return jax.shard_map(
        per_device,
        mesh=mesh,
        in_specs=(
            P("dp", None),
            P("dp", None),
            P(),
            P("dp"),
            P(),
            P(None, "tensor"),
            P(None, "tensor"),
            P(None, "tensor"),
            P("tensor", None),
            P(),
            P(None, "tensor"),
            P(None, "tensor"),
            P("tensor", None),
        ),
        out_specs=(
            P(("dp", "tensor"), None),
            P(("dp", "tensor"), None),
            P(),
            P("dp", "tensor"),
            P("dp", "tensor"),
            P("dp", "tensor"),
            P("tensor", "dp"),
            P(),
            P("dp", "tensor"),
            P("dp", "tensor"),
            P("tensor", "dp"),
        ),
        check_vma=False,
    )
```

```python
import functools

import jax
import jax.numpy as jnp
import numpy as np
from jax import lax
from jax.experimental import pallas as pl
from jax.experimental.pallas import tpu as pltpu
from jax.sharding import PartitionSpec as P

HDIM = 64
EPS = 1e-05
LOW = jnp.bfloat16
FULL = jnp.float32


def ring_perm(ring, bits):
    step = bits * (4 if ring == "x" else 1)
    return [(i, i ^ step) for i in range(32)]


class Links:
    def __init__(self):
        self.last = {}

    def send(self, value, ring, bits):
        names = [(ring, name) for name in ((1, 3) if bits == 2 else (bits,))]
        before = [self.last[name] for name in names if name in self.last]
        if before:
            value = tie(value, *before)
        out = over_ring(value, ring, bits)
        for name in names:
            self.last[name] = out
        return out


def over_ring(value, ring, bits):
    return lax.ppermute(value, "dp", ring_perm(ring, bits))


def over_yh(value):
    return lax.ppermute(value, "dp", [(i, i ^ 16) for i in range(32)])


def over_tensor(value, bits):
    return lax.ppermute(value, "tensor", [(i, i ^ bits) for i in range(4)])


def dot(a, b):
    return jnp.dot(a, b, preferred_element_type=FULL)


def dot_t(a, b):
    return lax.dot_general(a, b, (((1,), (1,)), ((), ())), preferred_element_type=FULL)


def dot_rows(a, b):
    return lax.dot_general(a, b, (((0,), (0,)), ((), ())), preferred_element_type=FULL)


def rope_tables(rows):
    position = np.arange(rows, dtype=np.float32)[:, None]
    exponent = np.arange(HDIM // 2, dtype=np.float32) * np.float32(2.0 / HDIM)
    angles = position / np.power(np.float32(10000.0), exponent)[None, :]
    angles = angles.astype(np.float32).astype(np.float64)
    cosine, sine = np.cos(angles).astype(np.float32), np.sin(angles).astype(np.float32)
    return (
        np.concatenate([cosine] * 4, axis=1),
        np.concatenate([-sine, sine, -sine, sine], axis=1),
    )


def turned(value, cosine, sine):
    width = value.shape[1]
    lane = lax.broadcasted_iota(jnp.int32, value.shape, 1) % HDIM
    swapped = jnp.where(
        lane < HDIM // 2,
        pltpu.roll(value, width - HDIM // 2, 1),
        pltpu.roll(value, HDIM // 2, 1),
    )
    count = width // 128
    if count > 1:
        cosine = jnp.concatenate([cosine] * count, axis=1)
        sine = jnp.concatenate([sine] * count, axis=1)
    return value * cosine + swapped * sine


def project_body(where, rows, gain, w_query, w_key, w_value, cosine, sine, *refs):
    normed_out, query_out, pair_out, cosine_out, sine_out, w_pair = refs
    cosine_out[...] = cosine[...]
    sine_out[...] = sine[...]

    @pl.when(pl.program_id(0) == 0)
    def _():
        w_pair[...] = jnp.concatenate([w_key[...], w_value[...]], axis=0)

    value = rows[...].astype(FULL)
    inv = lax.rsqrt(jnp.mean(value * value, axis=-1, keepdims=True) + EPS)
    normed = (value * inv * gain[...].astype(FULL)).astype(LOW)
    normed_out[...] = normed
    query_out[...] = turned(dot(normed, w_query[...]), cosine[...], sine[...]).astype(LOW)
    pair = dot_t(normed, w_pair[...])
    lane = lax.broadcasted_iota(jnp.int32, pair.shape, 1)
    pair_out[...] = jnp.where(lane < HDIM, turned(pair, cosine[...], sine[...]), pair).astype(LOW)


def project(blocks, hidden_in, gain, w_query, w_key, w_value):
    rows, model = hidden_in.shape
    step = rows // 4
    cosine, sine = rope_tables(rows)

    def chosen(width):
        return pl.BlockSpec((step, width), lambda i, where: (where[i], 0))

    def whole(value):
        return pl.BlockSpec(value.shape, lambda i, where: (0, 0))

    def placed(width):
        return pl.BlockSpec((step, width), lambda i, where: (i, 0))

    heads = w_query.shape[1]
    return pl.pallas_call(
        project_body,
        grid_spec=pltpu.PrefetchScalarGridSpec(
            num_scalar_prefetch=1,
            grid=(4,),
            in_specs=[
                chosen(model),
                whole(gain),
                whole(w_query),
                whole(w_key),
                whole(w_value),
                chosen(128),
                chosen(128),
            ],
            out_specs=[placed(model), placed(heads)] + [placed(2 * HDIM)] * 3,
            scratch_shapes=[pltpu.VMEM((2 * HDIM, model), LOW)],
        ),
        out_shape=[
            jax.ShapeDtypeStruct((rows, model), LOW),
            jax.ShapeDtypeStruct((rows, heads), LOW),
            jax.ShapeDtypeStruct((rows, 2 * HDIM), LOW),
            jax.ShapeDtypeStruct((rows, 2 * HDIM), FULL),
            jax.ShapeDtypeStruct((rows, 2 * HDIM), FULL),
        ],
        compiler_params=pltpu.CompilerParams(
            vmem_limit_bytes=60 * 1024 * 1024, dimension_semantics=("arbitrary",)
        ),
        cost_estimate=pl.CostEstimate(
            flops=2 * rows * model * (heads + 2 * HDIM),
            bytes_accessed=2 * (2 * rows * model + model * (heads + 4 * HDIM) + rows * 640),
            transcendentals=rows,
        ),
    )(
        jnp.stack(blocks).astype(jnp.int32),
        hidden_in,
        gain,
        w_query,
        w_key,
        w_value,
        jnp.asarray(cosine),
        jnp.asarray(sine),
    )


def swap_halves(value):
    half = value.shape[0] // 2
    return jnp.concatenate([value[half:], value[:half]], axis=0)


def heads_of(where, mine, partner, step):
    use_mine = (step // 2 == 0) == (where[4] == 1)
    return jnp.where(use_mine, mine[...].astype(FULL), swap_halves(partner[...]).astype(FULL))


def allowed_pairs(where, rows):
    step = rows // 4

    def positions(shape, axis):
        index = lax.broadcasted_iota(jnp.int32, shape, axis)
        base = where[3] - 3
        for block in (2, 1, 0):
            base = jnp.where(index < (block + 1) * step, where[block] - block, base)
        return index + base * step

    keys, queries = positions((rows, 1), 0), positions((1, rows), 1)
    return (keys <= queries) & (keys < where[5])


def placed_heads(head):
    low = lax.broadcasted_iota(jnp.int32, head.shape, 1) < HDIM
    return (
        jnp.where(low, head, 0.0).astype(LOW),
        jnp.where(low, 0.0, pltpu.roll(head, HDIM, 1)).astype(LOW),
    )


def attend_body(where, query, mine, partner, out, lse_out):
    both = heads_of(where, mine, partner, pl.program_id(0))
    allowed = allowed_pairs(where, both.shape[0])
    value_t = both.T[HDIM:].astype(LOW)
    mixed = []
    for index, key in enumerate(placed_heads(both)):
        scores = dot_t(key, query[...]) * HDIM ** (-0.5)
        scores = jnp.where(allowed, scores, -1e30)
        top = jnp.max(scores, axis=0, keepdims=True)
        weights = jnp.exp(scores - top)
        total = jnp.sum(weights, axis=0, keepdims=True)
        lse_out[0, index : index + 1, :] = top + jnp.log(total)
        mixed.append(dot(value_t, (weights / total).astype(LOW)))
    out[...] = jnp.concatenate(mixed, axis=0).T.astype(LOW)


def attend_specs(rows, lanes):
    pair = pl.BlockSpec((rows, lanes), lambda i, where: (0, i))
    whole = pl.BlockSpec((rows, lanes), lambda i, where: (0, 0))
    lse = pl.BlockSpec((1, 2, rows), lambda i, where: (i, 0, 0))
    return pair, whole, lse


def attend(where, query, mine, partner):
    rows, lanes = mine.shape
    steps = query.shape[1] // lanes
    pair, whole, lse = attend_specs(rows, lanes)
    return pl.pallas_call(
        attend_body,
        grid_spec=pltpu.PrefetchScalarGridSpec(
            num_scalar_prefetch=1,
            grid=(steps,),
            in_specs=[pair, whole, whole],
            out_specs=[pair, lse],
        ),
        out_shape=[
            jax.ShapeDtypeStruct(query.shape, LOW),
            jax.ShapeDtypeStruct((steps, 2, rows), FULL),
        ],
        compiler_params=pltpu.CompilerParams(
            vmem_limit_bytes=24 * 1024 * 1024, dimension_semantics=("arbitrary",)
        ),
        cost_estimate=pl.CostEstimate(
            flops=4 * rows * rows * query.shape[1],
            bytes_accessed=8 * rows * query.shape[1],
            transcendentals=2 * steps * rows * rows,
        ),
    )(where, query, mine, partner)


def attend_back_body(where, query, mine, partner, grad, lse, cosine, sine, dquery, dboth, acc):
    step = pl.program_id(0)
    both = heads_of(where, mine, partner, step)
    allowed = allowed_pairs(where, both.shape[0])
    low = lax.broadcasted_iota(jnp.int32, both.shape, 1) < HDIM
    key_t = both.T[:HDIM].astype(LOW)
    keys = placed_heads(both)
    values = placed_heads(pltpu.roll(both, HDIM, 1))
    dkeys, dvalues, mixed = [], [], []
    for index in range(2):
        scores = dot_t(keys[index], query[...]) * HDIM ** (-0.5)
        probs = jnp.where(allowed, jnp.exp(scores - lse[0, index : index + 1, :]), 0.0)
        dprobs = dot_t(values[index], grad[...])
        delta = jnp.sum(dprobs * probs, axis=0, keepdims=True)
        dscores = (probs * (dprobs - delta)).astype(LOW)
        dvalues.append(dot(probs.astype(LOW), grad[...]))
        dkeys.append(dot(dscores, query[...]))
        mixed.append(dot(key_t, dscores))
    turn_back = jnp.concatenate(mixed, axis=0).T * HDIM ** (-0.5)
    dquery[...] = turned(turn_back, cosine[...], -sine[...]).astype(LOW)
    dkey = jnp.where(low, dkeys[0], dkeys[1]) * HDIM ** (-0.5)
    dvalue = jnp.where(low, dvalues[0], dvalues[1])

    @pl.when(step % 2 == 0)
    def _():
        acc[0], acc[1] = dkey, dvalue

    @pl.when(step % 2 == 1)
    def _():
        key_sum, value_sum = acc[0] + dkey, acc[1] + dvalue
        dboth[0] = jnp.where(
            low,
            key_sum + pltpu.roll(key_sum, HDIM, 1),
            value_sum + pltpu.roll(value_sum, HDIM, 1),
        )


def attend_back(where, query, mine, partner, grad, lse, cosine, sine):
    rows, lanes = mine.shape
    steps = query.shape[1] // lanes
    pair, whole, lse_spec = attend_specs(rows, lanes)
    slot = pl.BlockSpec((1, rows, lanes), lambda i, where: ((i // 2) ^ (1 - where[4]), 0, 0))
    return pl.pallas_call(
        attend_back_body,
        grid_spec=pltpu.PrefetchScalarGridSpec(
            num_scalar_prefetch=1,
            grid=(steps,),
            in_specs=[pair, whole, whole, pair, lse_spec, whole, whole],
            out_specs=[pair, slot],
            scratch_shapes=[pltpu.VMEM((2, rows, lanes), FULL)],
        ),
        out_shape=[
            jax.ShapeDtypeStruct(query.shape, LOW),
            jax.ShapeDtypeStruct((2, rows, lanes), FULL),
        ],
        compiler_params=pltpu.CompilerParams(
            vmem_limit_bytes=24 * 1024 * 1024, dimension_semantics=("arbitrary",)
        ),
        cost_estimate=pl.CostEstimate(
            flops=10 * rows * rows * query.shape[1],
            bytes_accessed=8 * rows * query.shape[1],
            transcendentals=2 * steps * rows * rows,
        ),
    )(where, query, mine, partner, grad, lse, cosine, sine)


def join_back_body(dboth, incoming, cosine, sine, out):
    total = dboth[0] + swap_halves(incoming[...])
    low = lax.broadcasted_iota(jnp.int32, total.shape, 1) < HDIM
    out[...] = jnp.where(low, turned(total, cosine[...], -sine[...]), total).astype(LOW)


def join_back(dboth, incoming, cosine, sine):
    return pl.pallas_call(
        join_back_body,
        out_shape=jax.ShapeDtypeStruct(incoming.shape, LOW),
        compiler_params=pltpu.CompilerParams(vmem_limit_bytes=24 * 1024 * 1024),
    )(dboth, incoming, cosine, sine)


def put_turned(value, out):
    for block in range(0, 32, 2):
        pair = value[:, block * 64 : block * 64 + 128].T
        for which in range(2):
            at = ((block + which) % 16 * 2 + block // 16) * 64
            out[at : at + 64] = pair[which * 64 : which * 64 + 64]


def prepare_body(where, cotangent, out, out_t):
    value = cotangent[...]
    step = value.shape[0]
    row = lax.broadcasted_iota(jnp.int32, (step, 1), 0) + where[pl.program_id(0)] * step
    value = jnp.where(row < where[5], value, jnp.zeros_like(value))
    out[...] = value
    put_turned(value, out_t)


def prepare(where, cotangent):
    rows, model = cotangent.shape
    step = rows // 4
    return pl.pallas_call(
        prepare_body,
        grid_spec=pltpu.PrefetchScalarGridSpec(
            num_scalar_prefetch=1,
            grid=(4,),
            in_specs=[pl.BlockSpec((step, model), lambda i, where: (where[i], 0))],
            out_specs=[
                pl.BlockSpec((step, model), lambda i, where: (i, 0)),
                pl.BlockSpec((model, step), lambda i, where: (0, i)),
            ],
        ),
        out_shape=[
            jax.ShapeDtypeStruct((rows, model), LOW),
            jax.ShapeDtypeStruct((model, rows), LOW),
        ],
        compiler_params=pltpu.CompilerParams(
            vmem_limit_bytes=24 * 1024 * 1024, dimension_semantics=("arbitrary",)
        ),
        cost_estimate=pl.CostEstimate(
            flops=rows * model, bytes_accessed=6 * rows * model, transcendentals=0
        ),
    )(where, cotangent)


def feed_body(*refs):
    pieces, (w_gate, w_up, dhidden, dy_t) = refs[:4], refs[4:8]
    hidden_out, dgate_out, dup_out, grads, rows, rows_t = refs[8:]
    height = pieces[0].shape[0]
    step, last = pl.program_id(0), pl.num_programs(0) - 1

    @pl.when(step == 0)
    def _():
        for index, piece in enumerate(pieces):
            rows[index * height : (index + 1) * height] = piece[...]
        put_turned(rows[...], rows_t)

    gate = dot(rows[...], w_gate[...]).astype(LOW).astype(FULL)
    up = dot(rows[...], w_up[...]).astype(LOW).astype(FULL)
    sigmoid = jax.nn.sigmoid(gate)
    activated = gate * sigmoid
    hidden = (activated * up).astype(LOW)
    back = dhidden[...]
    dgate = (back * up * sigmoid * (1.0 + gate * (1.0 - sigmoid))).astype(LOW)
    dup = (back * activated).astype(LOW)
    hidden_out[...], dgate_out[...], dup_out[...] = hidden, dgate, dup
    found = [
        dot(dy_t[...], hidden).astype(LOW),
        dot(rows_t[...], dgate).astype(LOW),
        dot(rows_t[...], dup).astype(LOW),
    ]
    rest = grads.shape[1] // 6

    @pl.when(step < last)
    def _():
        for at, value in enumerate(found):
            grads[:, at * 256 : (at + 1) * 256] = value

    @pl.when(step == last)
    def _():
        for at, value in enumerate(found):
            grads[:, at * rest : (at + 1) * rest] = value[:, :rest]


def feed(pieces, w_gate, w_up, dhidden, dy_t):
    rows, width = dhidden.shape
    model = w_gate.shape[0]
    across = pl.BlockSpec((rows, 256), lambda i: (0, i))
    weight = pl.BlockSpec((model, 256), lambda i: (0, i))
    whole = lambda value: pl.BlockSpec(value.shape, lambda i: (0, 0))
    return pl.pallas_call(
        feed_body,
        grid=(pl.cdiv(width, 256),),
        in_specs=[whole(piece) for piece in pieces] + [weight, weight, across, whole(dy_t)],
        out_specs=[across] * 3 + [pl.BlockSpec((model, 768), lambda i: (0, i))],
        out_shape=[jax.ShapeDtypeStruct((rows, width), LOW)] * 3
        + [jax.ShapeDtypeStruct((model, 3 * width), LOW)],
        scratch_shapes=[pltpu.VMEM((rows, model), LOW), pltpu.VMEM((model, rows), LOW)],
        compiler_params=pltpu.CompilerParams(
            vmem_limit_bytes=60 * 1024 * 1024, dimension_semantics=("arbitrary",)
        ),
        cost_estimate=pl.CostEstimate(
            flops=10 * rows * model * width,
            bytes_accessed=10 * model * width + 10 * rows * width + 4 * rows * model,
            transcendentals=rows * width,
        ),
    )(*pieces, w_gate, w_up, dhidden, dy_t)


def split_turns(value):
    width = value.shape[1] // 3
    turns, rest = width // 256, width % 256
    out = []
    for at in range(3):
        parts = [value[:, i * 768 + at * 256 : i * 768 + at * 256 + 256] for i in range(turns)]
        start = turns * 768 + at * rest
        out.append(jnp.concatenate(parts + [value[:, start : start + rest]], axis=1))
    return out


def feed_back_body(dgate, dup, w_gate, w_up, mine, other):
    value = dot_t(dgate[...], w_gate[...]) + dot_t(dup[...], w_up[...])
    half = value.shape[0] // 2
    mine[...] = value[:half]
    other[...] = value[half:].astype(LOW)


def feed_back(dgate, dup, w_gate, w_up):
    rows, width = dgate.shape
    model = w_gate.shape[0]
    whole = pl.BlockSpec((rows, width), lambda i: (0, 0))
    weight = pl.BlockSpec((256, width), lambda i: (i, 0))
    across = pl.BlockSpec((rows // 2, 256), lambda i: (0, i))
    return pl.pallas_call(
        feed_back_body,
        grid=(model // 256,),
        in_specs=[whole, whole, weight, weight],
        out_specs=[across, across],
        out_shape=[
            jax.ShapeDtypeStruct((rows // 2, model), FULL),
            jax.ShapeDtypeStruct((rows // 2, model), LOW),
        ],
        compiler_params=pltpu.CompilerParams(
            vmem_limit_bytes=60 * 1024 * 1024, dimension_semantics=("arbitrary",)
        ),
        cost_estimate=pl.CostEstimate(
            flops=4 * rows * model * width,
            bytes_accessed=4 * model * width + 4 * rows * width + 3 * rows * model,
            transcendentals=0,
        ),
    )(dgate, dup, w_gate, w_up)


def input_back_body(dquery, dpair, w_query, w_key, w_value, rows, mine, other, gain, w_pair):
    w_pair[:HDIM] = w_key[...]
    w_pair[HDIM:] = w_value[...]
    value = dot_t(dquery[...], w_query[...]) + dot(dpair[...], w_pair[...])
    half = value.shape[0] // 2
    mine[...] = value[:half]
    other[...] = value[half:].astype(LOW)
    gain[...] = jnp.sum(value * rows[...].astype(FULL), axis=0, keepdims=True)


def input_back(dquery, dpair, w_query, w_key, w_value, normed):
    rows, model = normed.shape
    whole = lambda value: pl.BlockSpec(value.shape, lambda i: (0, 0))
    across = lambda height: pl.BlockSpec((height, 256), lambda i: (0, i))
    return pl.pallas_call(
        input_back_body,
        grid=(model // 256,),
        in_specs=[
            whole(dquery),
            whole(dpair),
            pl.BlockSpec((256, w_query.shape[1]), lambda i: (i, 0)),
            across(HDIM),
            across(HDIM),
            across(rows),
        ],
        out_specs=[across(rows // 2), across(rows // 2), across(1)],
        out_shape=[
            jax.ShapeDtypeStruct((rows // 2, model), FULL),
            jax.ShapeDtypeStruct((rows // 2, model), LOW),
            jax.ShapeDtypeStruct((1, model), FULL),
        ],
        scratch_shapes=[pltpu.VMEM((2 * HDIM, 256), LOW)],
        compiler_params=pltpu.CompilerParams(
            vmem_limit_bytes=60 * 1024 * 1024, dimension_semantics=("arbitrary",)
        ),
        cost_estimate=pl.CostEstimate(
            flops=2 * rows * model * 640,
            bytes_accessed=model * 1280 + 5 * rows * model,
            transcendentals=0,
        ),
    )(dquery, dpair, w_query, w_key, w_value, normed)


def wgrad_body(ring, orders, where, side, fan, *refs):
    step = pl.program_id(0)
    value = dot_rows(side[...], fan[...])
    if ring == "z":
        total = refs[4]
        total[...] = value

    for half in range(2):
        send_ref, keep_ref = refs[2 * half : 2 * half + 2]
        at = step - 4 * half
        if ring == "z":
            def piece(bits):
                start = pl.multiple_of(where[8 + bits], 64)
                return total[pl.ds(start, 64), :].astype(LOW)

            @pl.when((at >= 0) & (at < 4))
            def _():
                order = orders[half]
                send_ref[0:64] = piece(order[0])
                send_ref[64:128] = piece(order[1])
                keep_ref[0:64] = piece(order[2])
                keep_ref[64:128] = piece(order[3])
        else:

            @pl.when((at >= 0) & (at < 2))
            def _():
                send_ref[...] = value.astype(LOW)

            @pl.when((at >= 2) & (at < 4))
            def _():
                keep_ref[...] = value.astype(LOW)


def wgrad(place, core, side, fan, ring):
    tokens, width = fan.shape
    x, z = place
    orders = [(first, 2, 0, 4 - first) for first in (1, 3)]
    blocks = []
    for half in range(2):
        steps = orders[half] if ring == "x" else range(4)
        blocks += [(core ^ half) * 4 + (x ^ bits) for bits in steps]
    where = jnp.stack(blocks + [(z ^ bits) * 64 for bits in range(4)]).astype(jnp.int32)
    rows = 256 if ring == "x" else 128

    def place_of(low, high):
        return pl.BlockSpec((rows, width), lambda i, where: (jnp.clip(i - low, 0, high), 0))

    if ring == "x":
        out_specs = [place_of(low, 1) for low in (0, 2, 4, 6)]
    else:
        out_specs = [place_of(low, 3) for low in (0, 0, 4, 4)]
    return pl.pallas_call(
        functools.partial(wgrad_body, ring, orders),
        grid_spec=pltpu.PrefetchScalarGridSpec(
            num_scalar_prefetch=1,
            grid=(8,),
            in_specs=[
                pl.BlockSpec((tokens, 256), lambda i, where: (0, where[i])),
                pl.BlockSpec((tokens, width), lambda i, where: (0, 0)),
            ],
            out_specs=out_specs,
            scratch_shapes=[pltpu.VMEM((256, width), FULL)] if ring == "z" else [],
        ),
        out_shape=[jax.ShapeDtypeStruct((512, width), LOW)] * 4,
        compiler_params=pltpu.CompilerParams(
            vmem_limit_bytes=24 * 1024 * 1024, dimension_semantics=("arbitrary",)
        ),
        cost_estimate=pl.CostEstimate(
            flops=2 * tokens * 2048 * width,
            bytes_accessed=2 * tokens * (2048 + width) + 4 * 2048 * width,
            transcendentals=0,
        ),
    )(where, side, fan)


def scatter_planes(value):
    groups = [[16 * yh + i for i in range(16)] for yh in range(2)]
    return lax.psum_scatter(
        value, "dp", scatter_dimension=0, axis_index_groups=groups, tiled=True
    )


def tie(value, *others):
    return lax.optimization_barrier((value, *others))[0]


class Grad:
    def __init__(self, links, place, core, side, fan, ring):
        self.links, self.ring = links, ring
        send0, keep0, send1, keep1 = wgrad(place, core, side, fan, ring)
        self.shape = (4, 2, 64, fan.shape[1]) if ring == "z" else (2, 4, 64, fan.shape[1])
        self.sent = [send0, send1]
        self.keep = [keep0.reshape(self.shape), keep1.reshape(self.shape)]

    def part(self, value, which):
        axis = 1 if self.ring == "z" else 0
        return lax.index_in_dim(value, which, axis, False).astype(FULL)

    def first(self):
        got = [self.links.send(self.sent[half], self.ring, (1, 3)[half]) for half in range(2)]
        self.got = [item.reshape(self.shape) for item in got]

    def second(self):
        self.sent = [
            (self.part(self.keep[half], 1) + self.part(self.got[half], 1)).astype(LOW)
            for half in range(2)
        ]
        self.got_next = [
            self.links.send(self.sent[half], self.ring, (3, 1)[half]) for half in range(2)
        ]

    def halves(self):
        halves = []
        for half in range(2):
            got_next = self.got_next[half]
            got = tie(self.got[half], got_next)
            halves.append(
                self.part(self.keep[half], 0) + self.part(got, 0) + got_next.astype(FULL)
            )
        return halves


class End:
    def __init__(self, links, grad, at):
        ring = "z" if grad.ring == "x" else "x"
        values = jnp.stack(grad.halves(), axis=1)

        def block(bits):
            index = at ^ bits if ring == "z" else bits
            return lax.dynamic_index_in_dim(values, index, 0, False)

        self.keep = block(0)
        self.sent = [block(bits).astype(LOW) for bits in (1, 3, 2)]
        before = [links.last[ring, 1], links.last[ring, 3]]
        self.got = [
            over_ring(tie(item, *before), ring, bits)
            for item, bits in zip(self.sent, (1, 3, 2))
        ]

    def totals(self):
        return self.keep + sum(item.astype(FULL) for item in self.got)


def finish_together(ends, same):
    parts = [end.totals() for end in ends]
    values = jnp.concatenate(parts, axis=2)
    send = jnp.where(same, values[1], values[0]).astype(LOW)
    total = jnp.where(same, values[0], values[1]) + over_yh(send).astype(FULL)
    out, at = [], 0
    for part in parts:
        width = part.shape[2]
        out.append(total[:, at : at + width])
        at += width
    return out


def sent(*tasks):
    return [item for task in tasks for item in task.sent]


def sum_ring(value, ring):
    return value + over_ring(value, ring, 1) + over_ring(value, ring, 3) + over_ring(value, ring, 2)


def per_device(
    hidden_in,
    cotangent,
    seq_lengths,
    slot_order,
    attn_gain,
    w_query,
    w_key,
    w_value,
    w_out,
    mlp_gain,
    w_gate,
    w_up,
    w_down,
):
    rows = hidden_in.shape[0]
    own_rows = rows // 4
    heads = w_query.shape[1] // HDIM
    ff = w_gate.shape[1]
    dp_at = lax.axis_index("dp")
    yh, x, z = dp_at // 16, (dp_at // 4) % 4, dp_at % 4
    place = (x, z)
    tensor_at = lax.axis_index("tensor")
    core = tensor_at % 2
    blocks = [tensor_at ^ bits for bits in (0, 2, 1, 3)]

    sequence = slot_order[0]
    length = jnp.sum(
        jnp.where(jnp.arange(seq_lengths.shape[0], dtype=jnp.int32) == sequence, seq_lengths, 0)
    )
    gain_one = attn_gain.astype(FULL)
    gain_two = mlp_gain.astype(FULL)

    links = Links()
    links = Links()
    attn_in, queries, packed, cosine, sine = project(
        blocks, hidden_in, attn_gain[None, :], w_query, w_key.T, w_value.T
    )
    partner = over_tensor(packed, 1)
    where = jnp.stack(blocks + [1 - core, length]).astype(jnp.int32)
    attended, lse = attend(where, queries, packed, partner)
    dy_low, dy_t = prepare(where, cotangent)

    half = 2 * own_rows

    got = over_tensor(dot(attended[half:], w_out).astype(LOW), 1)
    mine = dot(attended[:half], w_out)
    send = (mine[own_rows:] + got[own_rows:].astype(FULL)).astype(LOW)
    got_next = tie(over_tensor(send, 2), dy_low, dy_t)
    inputs = lax.dynamic_slice_in_dim(hidden_in, tensor_at * own_rows, own_rows, 0).astype(FULL)
    got = tie(got, got_next)
    middle = inputs + mine[:own_rows] + got[:own_rows].astype(FULL) + got_next.astype(FULL)
    inv_two = lax.rsqrt(jnp.mean(middle * middle, axis=-1, keepdims=True) + EPS)
    normed_two = middle * inv_two
    own = (normed_two * gain_two).astype(LOW)

    got = over_tensor(own, 2)
    got_own = over_tensor(own, 1)
    grad_hidden = dot_t(tie(dy_low, own), w_down)
    got = tie(got, grad_hidden)
    hidden, grad_gate, grad_up, mlp_grads = feed(
        [own, got, got_own, over_tensor(got, 1)], w_gate, w_up, grad_hidden, dy_t
    )

    def grad_of(side, fan, ring):
        return Grad(links, place, core, side, fan, ring)

    same = yh == core
    mlp_sum = scatter_planes(mlp_grads)
    mine, other = feed_back(grad_gate, grad_up, w_gate, w_up)
    got = over_tensor(other, 1)
    send = (mine[own_rows:] + got[own_rows:].astype(FULL)).astype(LOW)
    got_next = over_tensor(send, 2)
    mlp_send = dot(tie(hidden, send)[half:], w_down).astype(LOW)
    mlp_got = over_tensor(mlp_send, 1)
    mlp_mine = dot(tie(hidden, mlp_send)[:half], w_down)
    got_next = tie(got_next, mlp_mine)
    got = tie(got, got_next)
    mlp_back = mine[:own_rows] + got[:own_rows].astype(FULL) + got_next.astype(FULL)

    scaled_two = mlp_back * gain_two
    dmid = dy_low[:own_rows].astype(FULL) + inv_two * (
        scaled_two - normed_two * jnp.mean(scaled_two * normed_two, axis=-1, keepdims=True)
    )
    gain_two_part = jnp.sum(mlp_back * normed_two, axis=0)
    own = dmid.astype(LOW)
    got = over_tensor(own, 2)
    mlp_got = tie(mlp_got, own)
    mlp_send = (mlp_mine[own_rows:] + mlp_got[own_rows:].astype(FULL)).astype(LOW)
    output_rows = middle + mlp_mine[:own_rows] + mlp_got[:own_rows].astype(FULL)
    got = tie(got, mlp_send, output_rows)
    mlp_got = over_tensor(tie(mlp_send, got), 2)
    pair = jnp.concatenate([own, got], axis=0)
    got_last = over_tensor(pair, 1)
    dmid_low = jnp.concatenate([pair, got_last], axis=0)

    grad_attended = dot_t(dmid_low, w_out).astype(LOW)
    query_low, dboth = attend_back(
        where, queries, packed, partner, grad_attended, lse, cosine, sine
    )
    incoming = over_tensor(dboth[1], 1)
    incoming = tie(incoming, mlp_got)
    key_value_low = join_back(dboth, incoming, cosine, sine)
    qkv_low = jnp.concatenate([query_low, key_value_low], axis=1)
    mine, other, gain_one_sum = input_back(
        query_low, key_value_low, w_query, w_key.T, w_value.T, attn_in
    )
    gains = jnp.stack([gain_one_sum[0] / gain_one, gain_two_part])
    got = over_tensor(other, 1)
    send = (mine[own_rows:] + got[own_rows:].astype(FULL)).astype(LOW)
    got_next = over_tensor(send, 2)
    for ring in ("x", "z"):
        gains = sum_ring(tie(gains, send), ring)
    qkv = grad_of(attn_in, tie(qkv_low, gains), "z")
    out = grad_of(tie(dmid_low, *qkv.sent), attended, "x")
    qkv.first()
    out.first()
    got = tie(got, got_next)
    attn_back = mine[:own_rows] + got[:own_rows].astype(FULL) + got_next.astype(FULL)

    output_rows = (output_rows + mlp_got.astype(FULL)).astype(LOW)

    inv_one = lax.rsqrt(jnp.mean(inputs * inputs, axis=-1, keepdims=True) + EPS)
    normed_one = inputs * inv_one
    scaled_one = attn_back * gain_one
    input_grad = dmid + inv_one * (
        scaled_one - normed_one * jnp.mean(scaled_one * normed_one, axis=-1, keepdims=True)
    )
    mlp_keep = lax.dynamic_slice_in_dim(mlp_sum, yh * 64, 64, 0).astype(FULL)
    mlp_send = lax.dynamic_slice_in_dim(mlp_sum, (1 - yh) * 64, 64, 0)
    gains = tie(gains, input_grad, *out.sent)
    gains = gains + over_yh(gains)
    gains = gains + over_tensor(gains, 2)
    gains = gains + over_tensor(gains, 1)
    out.second()
    qkv.second()
    mlp_rows_got = over_yh(mlp_send)
    qkv.got_next[0] = tie(qkv.got_next[0], mlp_rows_got)
    ends = [End(links, out, z), End(links, qkv, x)]
    out_rows, qkv_rows = finish_together(ends, same)
    down_rows, gate_rows, up_rows = split_turns(mlp_keep + mlp_rows_got.astype(FULL))
    q_cols = heads * HDIM
    return (
        output_rows,
        input_grad,
        gains[0],
        qkv_rows[:, :q_cols],
        qkv_rows[:, q_cols : q_cols + HDIM],
        qkv_rows[:, q_cols + HDIM :],
        out_rows.T,
        gains[1],
        gate_rows,
        up_rows,
        down_rows.T,
    )


def solution(mesh):
    return jax.shard_map(
        per_device,
        mesh=mesh,
        in_specs=(
            P("dp", None),
            P("dp", None),
            P(),
            P("dp"),
            P(),
            P(None, "tensor"),
            P(None, "tensor"),
            P(None, "tensor"),
            P("tensor", None),
            P(),
            P(None, "tensor"),
            P(None, "tensor"),
            P("tensor", None),
        ),
        out_specs=(
            P(("dp", "tensor"), None),
            P(("dp", "tensor"), None),
            P(),
            P("dp", "tensor"),
            P("dp", "tensor"),
            P("dp", "tensor"),
            P("tensor", "dp"),
            P(),
            P("dp", "tensor"),
            P("dp", "tensor"),
            P("tensor", "dp"),
        ),
        check_vma=False,
    )
```

```python
import functools

import jax
import jax.numpy as jnp
import numpy as np
from jax import lax
from jax.experimental import pallas as pl
from jax.experimental.pallas import tpu as pltpu
from jax.sharding import PartitionSpec as P

HDIM = 64
EPS = 1e-05
LOW = jnp.bfloat16
FULL = jnp.float32


def ring_perm(ring, bits):
    step = bits * (4 if ring == "x" else 1)
    return [(i, i ^ step) for i in range(32)]


class Links:
    def __init__(self):
        self.last = {}

    def send(self, value, ring, bits):
        names = [(ring, name) for name in ((1, 3) if bits == 2 else (bits,))]
        before = [self.last[name] for name in names if name in self.last]
        if before:
            value = tie(value, *before)
        out = over_ring(value, ring, bits)
        for name in names:
            self.last[name] = out
        return out


def over_ring(value, ring, bits):
    return lax.ppermute(value, "dp", ring_perm(ring, bits))


def over_yh(value):
    return lax.ppermute(value, "dp", [(i, i ^ 16) for i in range(32)])


def over_tensor(value, bits):
    return lax.ppermute(value, "tensor", [(i, i ^ bits) for i in range(4)])


def dot(a, b):
    return jnp.dot(a, b, preferred_element_type=FULL)


def dot_t(a, b):
    return lax.dot_general(a, b, (((1,), (1,)), ((), ())), preferred_element_type=FULL)


def dot_rows(a, b):
    return lax.dot_general(a, b, (((0,), (0,)), ((), ())), preferred_element_type=FULL)


def rope_tables(rows):
    position = np.arange(rows, dtype=np.float32)[:, None]
    exponent = np.arange(HDIM // 2, dtype=np.float32) * np.float32(2.0 / HDIM)
    angles = position / np.power(np.float32(10000.0), exponent)[None, :]
    angles = angles.astype(np.float32).astype(np.float64)
    cosine, sine = np.cos(angles).astype(np.float32), np.sin(angles).astype(np.float32)
    return (
        np.concatenate([cosine] * 4, axis=1),
        np.concatenate([-sine, sine, -sine, sine], axis=1),
    )


def turned(value, cosine, sine):
    width = value.shape[1]
    lane = lax.broadcasted_iota(jnp.int32, value.shape, 1) % HDIM
    swapped = jnp.where(
        lane < HDIM // 2,
        pltpu.roll(value, width - HDIM // 2, 1),
        pltpu.roll(value, HDIM // 2, 1),
    )
    count = width // 128
    if count > 1:
        cosine = jnp.concatenate([cosine] * count, axis=1)
        sine = jnp.concatenate([sine] * count, axis=1)
    return value * cosine + swapped * sine


def project_body(where, *refs):
    rows, cosine, sine, (gain, w_query, w_key, w_value) = refs[:2], refs[2:4], refs[4:6], refs[6:10]
    normed_out, query_out, pair_out, cosine_out, sine_out, w_pair = refs[10:]
    rows, cosine, sine = [
        jnp.concatenate([pair[0][...], pair[1][...]], axis=0) for pair in (rows, cosine, sine)
    ]
    cosine_out[...] = cosine
    sine_out[...] = sine

    @pl.when(pl.program_id(0) == 0)
    def _():
        w_pair[...] = jnp.concatenate([w_key[...], w_value[...]], axis=0)

    value = rows.astype(FULL)
    inv = lax.rsqrt(jnp.mean(value * value, axis=-1, keepdims=True) + EPS)
    normed = (value * inv * gain[...].astype(FULL)).astype(LOW)
    normed_out[...] = normed
    query_out[...] = turned(dot(normed, w_query[...]), cosine, sine).astype(LOW)
    pair = dot_t(normed, w_pair[...])
    lane = lax.broadcasted_iota(jnp.int32, pair.shape, 1)
    pair_out[...] = jnp.where(lane < HDIM, turned(pair, cosine, sine), pair).astype(LOW)


def project(blocks, hidden_in, gain, w_query, w_key, w_value):
    rows, model = hidden_in.shape
    step = rows // 4
    cosine, sine = rope_tables(rows)

    def chosen(width):
        return [
            pl.BlockSpec((step, width), lambda i, where, at=at: (where[2 * i + at], 0))
            for at in range(2)
        ]

    def whole(value):
        return pl.BlockSpec(value.shape, lambda i, where: (0, 0))

    def placed(width):
        return pl.BlockSpec((2 * step, width), lambda i, where: (i, 0))

    heads = w_query.shape[1]
    return pl.pallas_call(
        project_body,
        grid_spec=pltpu.PrefetchScalarGridSpec(
            num_scalar_prefetch=1,
            grid=(2,),
            in_specs=chosen(model)
            + chosen(128)
            + chosen(128)
            + [whole(gain), whole(w_query), whole(w_key), whole(w_value)],
            out_specs=[placed(model), placed(heads)] + [placed(2 * HDIM)] * 3,
            scratch_shapes=[pltpu.VMEM((2 * HDIM, model), LOW)],
        ),
        out_shape=[
            jax.ShapeDtypeStruct((rows, model), LOW),
            jax.ShapeDtypeStruct((rows, heads), LOW),
            jax.ShapeDtypeStruct((rows, 2 * HDIM), LOW),
            jax.ShapeDtypeStruct((rows, 2 * HDIM), FULL),
            jax.ShapeDtypeStruct((rows, 2 * HDIM), FULL),
        ],
        compiler_params=pltpu.CompilerParams(
            vmem_limit_bytes=60 * 1024 * 1024, dimension_semantics=("arbitrary",)
        ),
        cost_estimate=pl.CostEstimate(
            flops=2 * rows * model * (heads + 2 * HDIM),
            bytes_accessed=2 * (2 * rows * model + model * (heads + 4 * HDIM) + rows * 640),
            transcendentals=rows,
        ),
    )(
        jnp.stack(blocks).astype(jnp.int32),
        *[hidden_in] * 2,
        *[jnp.asarray(cosine)] * 2,
        *[jnp.asarray(sine)] * 2,
        gain,
        w_query,
        w_key,
        w_value,
    )


def swap_halves(value):
    half = value.shape[0] // 2
    return jnp.concatenate([value[half:], value[:half]], axis=0)


def heads_of(where, mine, partner, step):
    use_mine = (step // 2 == 0) == (where[4] == 1)
    return jnp.where(use_mine, mine[...].astype(FULL), swap_halves(partner[...]).astype(FULL))


def allowed_pairs(where, rows):
    step = rows // 4

    def positions(shape, axis):
        index = lax.broadcasted_iota(jnp.int32, shape, axis)
        base = where[3] - 3
        for block in (2, 1, 0):
            base = jnp.where(index < (block + 1) * step, where[block] - block, base)
        return index + base * step

    keys, queries = positions((rows, 1), 0), positions((1, rows), 1)
    return (keys <= queries) & (keys < where[5])


def placed_heads(head):
    low = lax.broadcasted_iota(jnp.int32, head.shape, 1) < HDIM
    return (
        jnp.where(low, head, 0.0).astype(LOW),
        jnp.where(low, 0.0, pltpu.roll(head, HDIM, 1)).astype(LOW),
    )


def attend_body(where, query, mine, partner, out, lse_out):
    both = heads_of(where, mine, partner, pl.program_id(0))
    allowed = allowed_pairs(where, both.shape[0])
    value_t = both.T[HDIM:].astype(LOW)
    mixed = []
    for index, key in enumerate(placed_heads(both)):
        scores = dot_t(key, query[...]) * HDIM ** (-0.5)
        scores = jnp.where(allowed, scores, -1e30)
        top = jnp.max(scores, axis=0, keepdims=True)
        weights = jnp.exp(scores - top)
        total = jnp.sum(weights, axis=0, keepdims=True)
        lse_out[0, index : index + 1, :] = top + jnp.log(total)
        mixed.append(dot(value_t, (weights / total).astype(LOW)))
    out[...] = jnp.concatenate(mixed, axis=0).T.astype(LOW)


def attend_specs(rows, lanes):
    pair = pl.BlockSpec((rows, lanes), lambda i, where: (0, i))
    whole = pl.BlockSpec((rows, lanes), lambda i, where: (0, 0))
    lse = pl.BlockSpec((1, 2, rows), lambda i, where: (i, 0, 0))
    return pair, whole, lse


def attend(where, query, mine, partner):
    rows, lanes = mine.shape
    steps = query.shape[1] // lanes
    pair, whole, lse = attend_specs(rows, lanes)
    return pl.pallas_call(
        attend_body,
        grid_spec=pltpu.PrefetchScalarGridSpec(
            num_scalar_prefetch=1,
            grid=(steps,),
            in_specs=[pair, whole, whole],
            out_specs=[pair, lse],
        ),
        out_shape=[
            jax.ShapeDtypeStruct(query.shape, LOW),
            jax.ShapeDtypeStruct((steps, 2, rows), FULL),
        ],
        compiler_params=pltpu.CompilerParams(
            vmem_limit_bytes=24 * 1024 * 1024, dimension_semantics=("arbitrary",)
        ),
        cost_estimate=pl.CostEstimate(
            flops=4 * rows * rows * query.shape[1],
            bytes_accessed=8 * rows * query.shape[1],
            transcendentals=2 * steps * rows * rows,
        ),
    )(where, query, mine, partner)


def attend_back_body(where, query, mine, partner, grad, lse, cosine, sine, dquery, dboth, acc):
    step = pl.program_id(0)
    both = heads_of(where, mine, partner, step)
    allowed = allowed_pairs(where, both.shape[0])
    low = lax.broadcasted_iota(jnp.int32, both.shape, 1) < HDIM
    key_t = both.T[:HDIM].astype(LOW)
    keys = placed_heads(both)
    values = placed_heads(pltpu.roll(both, HDIM, 1))
    dkeys, dvalues, mixed = [], [], []
    for index in range(2):
        scores = dot_t(keys[index], query[...]) * HDIM ** (-0.5)
        probs = jnp.where(allowed, jnp.exp(scores - lse[0, index : index + 1, :]), 0.0)
        dprobs = dot_t(values[index], grad[...])
        delta = jnp.sum(dprobs * probs, axis=0, keepdims=True)
        dscores = (probs * (dprobs - delta)).astype(LOW)
        dvalues.append(dot(probs.astype(LOW), grad[...]))
        dkeys.append(dot(dscores, query[...]))
        mixed.append(dot(key_t, dscores))
    turn_back = jnp.concatenate(mixed, axis=0).T * HDIM ** (-0.5)
    dquery[...] = turned(turn_back, cosine[...], -sine[...]).astype(LOW)
    dkey = jnp.where(low, dkeys[0], dkeys[1]) * HDIM ** (-0.5)
    dvalue = jnp.where(low, dvalues[0], dvalues[1])

    @pl.when(step % 2 == 0)
    def _():
        acc[0], acc[1] = dkey, dvalue

    @pl.when(step % 2 == 1)
    def _():
        key_sum, value_sum = acc[0] + dkey, acc[1] + dvalue
        dboth[0] = jnp.where(
            low,
            key_sum + pltpu.roll(key_sum, HDIM, 1),
            value_sum + pltpu.roll(value_sum, HDIM, 1),
        )


def attend_back(where, query, mine, partner, grad, lse, cosine, sine):
    rows, lanes = mine.shape
    steps = query.shape[1] // lanes
    pair, whole, lse_spec = attend_specs(rows, lanes)
    slot = pl.BlockSpec((1, rows, lanes), lambda i, where: ((i // 2) ^ (1 - where[4]), 0, 0))
    return pl.pallas_call(
        attend_back_body,
        grid_spec=pltpu.PrefetchScalarGridSpec(
            num_scalar_prefetch=1,
            grid=(steps,),
            in_specs=[pair, whole, whole, pair, lse_spec, whole, whole],
            out_specs=[pair, slot],
            scratch_shapes=[pltpu.VMEM((2, rows, lanes), FULL)],
        ),
        out_shape=[
            jax.ShapeDtypeStruct(query.shape, LOW),
            jax.ShapeDtypeStruct((2, rows, lanes), FULL),
        ],
        compiler_params=pltpu.CompilerParams(
            vmem_limit_bytes=24 * 1024 * 1024, dimension_semantics=("arbitrary",)
        ),
        cost_estimate=pl.CostEstimate(
            flops=10 * rows * rows * query.shape[1],
            bytes_accessed=8 * rows * query.shape[1],
            transcendentals=2 * steps * rows * rows,
        ),
    )(where, query, mine, partner, grad, lse, cosine, sine)


def join_back_body(dboth, incoming, cosine, sine, out):
    total = dboth[0] + swap_halves(incoming[...])
    low = lax.broadcasted_iota(jnp.int32, total.shape, 1) < HDIM
    out[...] = jnp.where(low, turned(total, cosine[...], -sine[...]), total).astype(LOW)


def join_back(dboth, incoming, cosine, sine):
    return pl.pallas_call(
        join_back_body,
        out_shape=jax.ShapeDtypeStruct(incoming.shape, LOW),
        compiler_params=pltpu.CompilerParams(vmem_limit_bytes=24 * 1024 * 1024),
    )(dboth, incoming, cosine, sine)


def put_turned(value, out):
    for block in range(0, 32, 2):
        pair = value[:, block * 64 : block * 64 + 128].T
        for which in range(2):
            at = ((block + which) % 16 * 2 + block // 16) * 64
            out[at : at + 64] = pair[which * 64 : which * 64 + 64]


def prepare_body(where, cotangent, out, out_t):
    value = cotangent[...]
    step = value.shape[0]
    row = lax.broadcasted_iota(jnp.int32, (step, 1), 0) + where[pl.program_id(0)] * step
    value = jnp.where(row < where[5], value, jnp.zeros_like(value))
    out[...] = value
    put_turned(value, out_t)


def prepare(where, cotangent):
    rows, model = cotangent.shape
    step = rows // 4
    return pl.pallas_call(
        prepare_body,
        grid_spec=pltpu.PrefetchScalarGridSpec(
            num_scalar_prefetch=1,
            grid=(4,),
            in_specs=[pl.BlockSpec((step, model), lambda i, where: (where[i], 0))],
            out_specs=[
                pl.BlockSpec((step, model), lambda i, where: (i, 0)),
                pl.BlockSpec((model, step), lambda i, where: (0, i)),
            ],
        ),
        out_shape=[
            jax.ShapeDtypeStruct((rows, model), LOW),
            jax.ShapeDtypeStruct((model, rows), LOW),
        ],
        compiler_params=pltpu.CompilerParams(
            vmem_limit_bytes=24 * 1024 * 1024, dimension_semantics=("arbitrary",)
        ),
        cost_estimate=pl.CostEstimate(
            flops=rows * model, bytes_accessed=6 * rows * model, transcendentals=0
        ),
    )(where, cotangent)


def gated(gate, up, back):
    gate, up = gate.astype(LOW).astype(FULL), up.astype(LOW).astype(FULL)
    sigmoid = jax.nn.sigmoid(gate)
    activated = gate * sigmoid
    dgate = back * up * sigmoid * (1.0 + gate * (1.0 - sigmoid))
    return (activated * up).astype(LOW), dgate.astype(LOW), (back * activated).astype(LOW)


def feed_body(*refs):
    pieces, near, (w_gate, w_up, dhidden, dy_t) = refs[:4], refs[4:7], refs[7:11]
    outs, (grads, far, rows_t) = refs[11:14], refs[14:]
    height = pieces[0].shape[0]
    step, last = pl.program_id(0), pl.num_programs(0) - 1

    @pl.when(step == 0)
    def _():
        far[:height] = pieces[1][...]
        far[height:] = pieces[3][...]
        put_turned(jnp.concatenate([piece[...] for piece in pieces], axis=0), rows_t)

    rest = grads.shape[1] // 6

    def columns(width):
        at = slice(0, width)

        products = [dot(far[...], weight[:, at]) for weight in (w_gate, w_up)]
        back = jnp.concatenate(
            [dhidden[height : 2 * height, at], dhidden[3 * height :, at]], axis=0
        )
        fans = []
        for close, other, out in zip(near, gated(*products, back), outs):
            close = close[:, at]
            parts = [close[:height], other[:height], close[height:], other[height:]]
            fans.append(jnp.concatenate(parts, axis=0))
            out[:, at] = fans[-1]
        for index, (side, fan) in enumerate(zip((dy_t, rows_t, rows_t), fans)):
            grads[:, index * width : (index + 1) * width] = dot(side[...], fan).astype(LOW)

    pl.when(step < last)(lambda: columns(256))
    pl.when(step == last)(lambda: columns(rest))


def feed(pieces, near, w_gate, w_up, dhidden, dy_t):
    rows, width = dhidden.shape
    model = w_gate.shape[0]
    across = pl.BlockSpec((rows, 256), lambda i: (0, i))
    weight = pl.BlockSpec((model, 256), lambda i: (0, i))
    whole = lambda value: pl.BlockSpec(value.shape, lambda i: (0, 0))
    return pl.pallas_call(
        feed_body,
        grid=(pl.cdiv(width, 256),),
        in_specs=[whole(piece) for piece in pieces]
        + [pl.BlockSpec((rows // 2, 256), lambda i: (0, i))] * 3
        + [weight, weight, across, whole(dy_t)],
        out_specs=[across] * 3 + [pl.BlockSpec((model, 768), lambda i: (0, i))],
        out_shape=[jax.ShapeDtypeStruct((rows, width), LOW)] * 3
        + [jax.ShapeDtypeStruct((model, 3 * width), LOW)],
        scratch_shapes=[pltpu.VMEM((rows // 2, model), LOW), pltpu.VMEM((model, rows), LOW)],
        compiler_params=pltpu.CompilerParams(
            vmem_limit_bytes=48 * 1024 * 1024, dimension_semantics=("arbitrary",)
        ),
        cost_estimate=pl.CostEstimate(
            flops=10 * rows * model * width,
            bytes_accessed=10 * model * width + 10 * rows * width + 4 * rows * model,
            transcendentals=rows * width,
        ),
    )(*pieces, *near, w_gate, w_up, dhidden, dy_t)


def split_turns(value):
    width = value.shape[1] // 3
    turns, rest = width // 256, width % 256
    out = []
    for at in range(3):
        parts = [value[:, i * 768 + at * 256 : i * 768 + at * 256 + 256] for i in range(turns)]
        start = turns * 768 + at * rest
        out.append(jnp.concatenate(parts + [value[:, start : start + rest]], axis=1))
    return out


def feed_back_body(dgate, dup, w_gate, w_up, mine, other):
    value = dot_t(dgate[...], w_gate[...]) + dot_t(dup[...], w_up[...])
    half = value.shape[0] // 2
    mine[...] = value[:half]
    other[...] = value[half:].astype(LOW)


def feed_back(dgate, dup, w_gate, w_up):
    rows, width = dgate.shape
    model = w_gate.shape[0]
    whole = pl.BlockSpec((rows, width), lambda i: (0, 0))
    weight = pl.BlockSpec((256, width), lambda i: (i, 0))
    across = pl.BlockSpec((rows // 2, 256), lambda i: (0, i))
    return pl.pallas_call(
        feed_back_body,
        grid=(model // 256,),
        in_specs=[whole, whole, weight, weight],
        out_specs=[across, across],
        out_shape=[
            jax.ShapeDtypeStruct((rows // 2, model), FULL),
            jax.ShapeDtypeStruct((rows // 2, model), LOW),
        ],
        compiler_params=pltpu.CompilerParams(
            vmem_limit_bytes=60 * 1024 * 1024, dimension_semantics=("arbitrary",)
        ),
        cost_estimate=pl.CostEstimate(
            flops=4 * rows * model * width,
            bytes_accessed=4 * model * width + 4 * rows * width + 3 * rows * model,
            transcendentals=0,
        ),
    )(dgate, dup, w_gate, w_up)


def input_back_body(dquery, dpair, w_query, w_key, w_value, rows, mine, other, gain, w_pair):
    w_pair[:HDIM] = w_key[...]
    w_pair[HDIM:] = w_value[...]
    value = dot_t(dquery[...], w_query[...]) + dot(dpair[...], w_pair[...])
    half = value.shape[0] // 2
    mine[...] = value[:half]
    other[...] = value[half:].astype(LOW)
    gain[...] = jnp.sum(value * rows[...].astype(FULL), axis=0, keepdims=True)


def input_back(dquery, dpair, w_query, w_key, w_value, normed):
    rows, model = normed.shape
    whole = lambda value: pl.BlockSpec(value.shape, lambda i: (0, 0))
    across = lambda height: pl.BlockSpec((height, 256), lambda i: (0, i))
    return pl.pallas_call(
        input_back_body,
        grid=(model // 256,),
        in_specs=[
            whole(dquery),
            whole(dpair),
            pl.BlockSpec((256, w_query.shape[1]), lambda i: (i, 0)),
            across(HDIM),
            across(HDIM),
            across(rows),
        ],
        out_specs=[across(rows // 2), across(rows // 2), across(1)],
        out_shape=[
            jax.ShapeDtypeStruct((rows // 2, model), FULL),
            jax.ShapeDtypeStruct((rows // 2, model), LOW),
            jax.ShapeDtypeStruct((1, model), FULL),
        ],
        scratch_shapes=[pltpu.VMEM((2 * HDIM, 256), LOW)],
        compiler_params=pltpu.CompilerParams(
            vmem_limit_bytes=60 * 1024 * 1024, dimension_semantics=("arbitrary",)
        ),
        cost_estimate=pl.CostEstimate(
            flops=2 * rows * model * 640,
            bytes_accessed=model * 1280 + 5 * rows * model,
            transcendentals=0,
        ),
    )(dquery, dpair, w_query, w_key, w_value, normed)


def wgrad_body(ring, orders, where, side, fan, *refs):
    step = pl.program_id(0)
    value = dot_rows(side[...], fan[...])
    if ring == "z":
        total = refs[4]
        total[...] = value

    for half in range(2):
        send_ref, keep_ref = refs[2 * half : 2 * half + 2]
        at = step - 4 * half
        if ring == "z":
            def piece(bits):
                start = pl.multiple_of(where[8 + bits], 64)
                return total[pl.ds(start, 64), :].astype(LOW)

            @pl.when((at >= 0) & (at < 4))
            def _():
                order = orders[half]
                send_ref[0:64] = piece(order[0])
                send_ref[64:128] = piece(order[1])
                keep_ref[0:64] = piece(order[2])
                keep_ref[64:128] = piece(order[3])
        else:

            @pl.when((at >= 0) & (at < 2))
            def _():
                send_ref[...] = value.astype(LOW)

            @pl.when((at >= 2) & (at < 4))
            def _():
                keep_ref[...] = value.astype(LOW)


def wgrad(place, core, side, fan, ring):
    tokens, width = fan.shape
    x, z = place
    orders = [(first, 2, 0, 4 - first) for first in (1, 3)]
    blocks = []
    for half in range(2):
        steps = orders[half] if ring == "x" else range(4)
        blocks += [(core ^ half) * 4 + (x ^ bits) for bits in steps]
    where = jnp.stack(blocks + [(z ^ bits) * 64 for bits in range(4)]).astype(jnp.int32)
    rows = 256 if ring == "x" else 128

    def place_of(low, high):
        return pl.BlockSpec((rows, width), lambda i, where: (jnp.clip(i - low, 0, high), 0))

    if ring == "x":
        out_specs = [place_of(low, 1) for low in (0, 2, 4, 6)]
    else:
        out_specs = [place_of(low, 3) for low in (0, 0, 4, 4)]
    return pl.pallas_call(
        functools.partial(wgrad_body, ring, orders),
        grid_spec=pltpu.PrefetchScalarGridSpec(
            num_scalar_prefetch=1,
            grid=(8,),
            in_specs=[
                pl.BlockSpec((tokens, 256), lambda i, where: (0, where[i])),
                pl.BlockSpec((tokens, width), lambda i, where: (0, 0)),
            ],
            out_specs=out_specs,
            scratch_shapes=[pltpu.VMEM((256, width), FULL)] if ring == "z" else [],
        ),
        out_shape=[jax.ShapeDtypeStruct((512, width), LOW)] * 4,
        compiler_params=pltpu.CompilerParams(
            vmem_limit_bytes=24 * 1024 * 1024, dimension_semantics=("arbitrary",)
        ),
        cost_estimate=pl.CostEstimate(
            flops=2 * tokens * 2048 * width,
            bytes_accessed=2 * tokens * (2048 + width) + 4 * 2048 * width,
            transcendentals=0,
        ),
    )(where, side, fan)


def scatter_planes(value):
    groups = [[16 * yh + i for i in range(16)] for yh in range(2)]
    return lax.psum_scatter(
        value, "dp", scatter_dimension=0, axis_index_groups=groups, tiled=True
    )


def tie(value, *others):
    return lax.optimization_barrier((value, *others))[0]


class Grad:
    def __init__(self, links, place, core, side, fan, ring):
        self.links, self.ring = links, ring
        send0, keep0, send1, keep1 = wgrad(place, core, side, fan, ring)
        self.shape = (4, 2, 64, fan.shape[1]) if ring == "z" else (2, 4, 64, fan.shape[1])
        self.sent = [send0, send1]
        self.keep = [keep0.reshape(self.shape), keep1.reshape(self.shape)]

    def part(self, value, which):
        axis = 1 if self.ring == "z" else 0
        return lax.index_in_dim(value, which, axis, False).astype(FULL)

    def first(self):
        got = [self.links.send(self.sent[half], self.ring, (1, 3)[half]) for half in range(2)]
        self.got = [item.reshape(self.shape) for item in got]

    def second(self):
        self.sent = [
            (self.part(self.keep[half], 1) + self.part(self.got[half], 1)).astype(LOW)
            for half in range(2)
        ]
        self.got_next = [
            self.links.send(self.sent[half], self.ring, (3, 1)[half]) for half in range(2)
        ]

    def halves(self):
        halves = []
        for half in range(2):
            got_next = self.got_next[half]
            got = tie(self.got[half], got_next)
            halves.append(
                self.part(self.keep[half], 0) + self.part(got, 0) + got_next.astype(FULL)
            )
        return halves


class End:
    def __init__(self, links, grad, at):
        ring = "z" if grad.ring == "x" else "x"
        values = jnp.stack(grad.halves(), axis=1)

        def block(bits):
            index = at ^ bits if ring == "z" else bits
            return lax.dynamic_index_in_dim(values, index, 0, False)

        self.keep = block(0)
        self.sent = [block(bits).astype(LOW) for bits in (1, 3, 2)]
        before = [links.last[ring, 1], links.last[ring, 3]]
        self.got = [
            over_ring(tie(item, *before), ring, bits)
            for item, bits in zip(self.sent, (1, 3, 2))
        ]

    def totals(self):
        return self.keep + sum(item.astype(FULL) for item in self.got)


def finish_together(ends, same):
    parts = [end.totals() for end in ends]
    values = jnp.concatenate(parts, axis=2)
    send = jnp.where(same, values[1], values[0]).astype(LOW)
    total = jnp.where(same, values[0], values[1]) + over_yh(send).astype(FULL)
    out, at = [], 0
    for part in parts:
        width = part.shape[2]
        out.append(total[:, at : at + width])
        at += width
    return out


def sent(*tasks):
    return [item for task in tasks for item in task.sent]


def sum_ring(value, ring):
    return value + over_ring(value, ring, 1) + over_ring(value, ring, 3) + over_ring(value, ring, 2)


def per_device(
    hidden_in,
    cotangent,
    seq_lengths,
    slot_order,
    attn_gain,
    w_query,
    w_key,
    w_value,
    w_out,
    mlp_gain,
    w_gate,
    w_up,
    w_down,
):
    rows = hidden_in.shape[0]
    own_rows = rows // 4
    heads = w_query.shape[1] // HDIM
    ff = w_gate.shape[1]
    dp_at = lax.axis_index("dp")
    yh, x, z = dp_at // 16, (dp_at // 4) % 4, dp_at % 4
    place = (x, z)
    tensor_at = lax.axis_index("tensor")
    core = tensor_at % 2
    blocks = [tensor_at ^ bits for bits in (0, 2, 1, 3)]

    sequence = slot_order[0]
    length = jnp.sum(
        jnp.where(jnp.arange(seq_lengths.shape[0], dtype=jnp.int32) == sequence, seq_lengths, 0)
    )
    gain_one = attn_gain.astype(FULL)
    gain_two = mlp_gain.astype(FULL)

    links = Links()
    links = Links()
    attn_in, queries, packed, cosine, sine = project(
        blocks, hidden_in, attn_gain[None, :], w_query, w_key.T, w_value.T
    )
    partner = over_tensor(packed, 1)
    where = jnp.stack(blocks + [1 - core, length]).astype(jnp.int32)
    attended, lse = attend(where, queries, packed, partner)

    half = 2 * own_rows

    got = over_tensor(dot(attended[half:], w_out).astype(LOW), 1)
    mine = dot(attended[:half], w_out)
    send = (mine[own_rows:] + got[own_rows:].astype(FULL)).astype(LOW)
    dy_low, dy_t = prepare(where, tie(cotangent, send))
    grad_hidden = dot_t(dy_low, w_down)
    got_next = tie(over_tensor(send, 2), dy_t, grad_hidden)
    inputs = lax.dynamic_slice_in_dim(hidden_in, tensor_at * own_rows, own_rows, 0).astype(FULL)
    got = tie(got, got_next)
    middle = inputs + mine[:own_rows] + got[:own_rows].astype(FULL) + got_next.astype(FULL)
    inv_two = lax.rsqrt(jnp.mean(middle * middle, axis=-1, keepdims=True) + EPS)
    normed_two = middle * inv_two
    own = (normed_two * gain_two).astype(LOW)

    got = over_tensor(own, 2)
    got_own = over_tensor(own, 1)
    near = jnp.concatenate([own, got_own], axis=0)
    back_near = jnp.concatenate(
        [grad_hidden[:own_rows], grad_hidden[half : half + own_rows]], axis=0
    )
    done_near = gated(dot(near, w_gate), dot(near, w_up), back_near)
    got = tie(got, *done_near)
    hidden, grad_gate, grad_up, mlp_grads = feed(
        [own, got, got_own, over_tensor(got, 1)],
        done_near,
        w_gate,
        w_up,
        grad_hidden,
        dy_t,
    )

    def grad_of(side, fan, ring):
        return Grad(links, place, core, side, fan, ring)

    same = yh == core
    mlp_sum = scatter_planes(mlp_grads)
    mine, other = feed_back(grad_gate, grad_up, w_gate, w_up)
    got = over_tensor(other, 1)
    send = (mine[own_rows:] + got[own_rows:].astype(FULL)).astype(LOW)
    got_next = over_tensor(send, 2)
    mlp_send = dot(tie(hidden, send)[half:], w_down).astype(LOW)
    mlp_got = over_tensor(mlp_send, 1)
    mlp_mine = dot(tie(hidden, mlp_send)[:half], w_down)
    got_next = tie(got_next, mlp_mine)
    got = tie(got, got_next)
    mlp_back = mine[:own_rows] + got[:own_rows].astype(FULL) + got_next.astype(FULL)

    scaled_two = mlp_back * gain_two
    dmid = dy_low[:own_rows].astype(FULL) + inv_two * (
        scaled_two - normed_two * jnp.mean(scaled_two * normed_two, axis=-1, keepdims=True)
    )
    gain_two_part = jnp.sum(mlp_back * normed_two, axis=0)
    own = dmid.astype(LOW)
    got = over_tensor(own, 2)
    mlp_got = tie(mlp_got, own)
    mlp_send = (mlp_mine[own_rows:] + mlp_got[own_rows:].astype(FULL)).astype(LOW)
    output_rows = middle + mlp_mine[:own_rows] + mlp_got[:own_rows].astype(FULL)
    got = tie(got, mlp_send, output_rows)
    mlp_got = over_tensor(tie(mlp_send, got), 2)
    pair = jnp.concatenate([own, got], axis=0)
    got_last = over_tensor(pair, 1)
    dmid_low = jnp.concatenate([pair, got_last], axis=0)

    grad_attended = dot_t(dmid_low, w_out).astype(LOW)
    query_low, dboth = attend_back(
        where, queries, packed, partner, grad_attended, lse, cosine, sine
    )
    incoming = over_tensor(dboth[1], 1)
    incoming = tie(incoming, mlp_got)
    key_value_low = join_back(dboth, incoming, cosine, sine)
    qkv_low = jnp.concatenate([query_low, key_value_low], axis=1)
    mine, other, gain_one_sum = input_back(
        query_low, key_value_low, w_query, w_key.T, w_value.T, attn_in
    )
    gains = jnp.stack([gain_one_sum[0] / gain_one, gain_two_part])
    got = over_tensor(other, 1)
    send = (mine[own_rows:] + got[own_rows:].astype(FULL)).astype(LOW)
    got_next = over_tensor(send, 2)
    for ring in ("x", "z"):
        gains = sum_ring(tie(gains, send), ring)
    qkv = grad_of(attn_in, tie(qkv_low, gains), "z")
    out = grad_of(tie(dmid_low, *qkv.sent), attended, "x")
    qkv.first()
    out.first()
    got = tie(got, got_next)
    attn_back = mine[:own_rows] + got[:own_rows].astype(FULL) + got_next.astype(FULL)

    output_rows = (output_rows + mlp_got.astype(FULL)).astype(LOW)

    inv_one = lax.rsqrt(jnp.mean(inputs * inputs, axis=-1, keepdims=True) + EPS)
    normed_one = inputs * inv_one
    scaled_one = attn_back * gain_one
    input_grad = dmid + inv_one * (
        scaled_one - normed_one * jnp.mean(scaled_one * normed_one, axis=-1, keepdims=True)
    )
    mlp_keep = lax.dynamic_slice_in_dim(mlp_sum, yh * 64, 64, 0).astype(FULL)
    mlp_send = lax.dynamic_slice_in_dim(mlp_sum, (1 - yh) * 64, 64, 0)
    gains = tie(gains, input_grad, *out.sent)
    gains = gains + over_yh(gains)
    gains = gains + over_tensor(gains, 2)
    gains = gains + over_tensor(gains, 1)
    out.second()
    qkv.second()
    mlp_rows_got = over_yh(mlp_send)
    qkv.got_next[0] = tie(qkv.got_next[0], mlp_rows_got)
    ends = [End(links, out, z), End(links, qkv, x)]
    out_rows, qkv_rows = finish_together(ends, same)
    down_rows, gate_rows, up_rows = split_turns(mlp_keep + mlp_rows_got.astype(FULL))
    q_cols = heads * HDIM
    return (
        output_rows,
        input_grad,
        gains[0],
        qkv_rows[:, :q_cols],
        qkv_rows[:, q_cols : q_cols + HDIM],
        qkv_rows[:, q_cols + HDIM :],
        out_rows.T,
        gains[1],
        gate_rows,
        up_rows,
        down_rows.T,
    )


def solution(mesh):
    return jax.shard_map(
        per_device,
        mesh=mesh,
        in_specs=(
            P("dp", None),
            P("dp", None),
            P(),
            P("dp"),
            P(),
            P(None, "tensor"),
            P(None, "tensor"),
            P(None, "tensor"),
            P("tensor", None),
            P(),
            P(None, "tensor"),
            P(None, "tensor"),
            P("tensor", None),
        ),
        out_specs=(
            P(("dp", "tensor"), None),
            P(("dp", "tensor"), None),
            P(),
            P("dp", "tensor"),
            P("dp", "tensor"),
            P("dp", "tensor"),
            P("tensor", "dp"),
            P(),
            P("dp", "tensor"),
            P("dp", "tensor"),
            P("tensor", "dp"),
        ),
        check_vma=False,
    )
```

```python
import functools

import jax
import jax.numpy as jnp
import numpy as np
from jax import lax
from jax.experimental import pallas as pl
from jax.experimental.pallas import tpu as pltpu
from jax.sharding import PartitionSpec as P

HDIM = 64
EPS = 1e-05
LOW = jnp.bfloat16
FULL = jnp.float32


def ring_perm(ring, bits):
    step = bits * (4 if ring == "x" else 1)
    return [(i, i ^ step) for i in range(32)]


class Links:
    def __init__(self):
        self.last = {}

    def send(self, value, ring, bits):
        names = [(ring, name) for name in ((1, 3) if bits == 2 else (bits,))]
        before = [self.last[name] for name in names if name in self.last]
        if before:
            value = tie(value, *before)
        out = over_ring(value, ring, bits)
        for name in names:
            self.last[name] = out
        return out


def over_ring(value, ring, bits):
    return lax.ppermute(value, "dp", ring_perm(ring, bits))


def over_yh(value):
    return lax.ppermute(value, "dp", [(i, i ^ 16) for i in range(32)])


def over_tensor(value, bits):
    return lax.ppermute(value, "tensor", [(i, i ^ bits) for i in range(4)])


def dot(a, b):
    return jnp.dot(a, b, preferred_element_type=FULL)


def dot_t(a, b):
    return lax.dot_general(a, b, (((1,), (1,)), ((), ())), preferred_element_type=FULL)


def dot_rows(a, b):
    return lax.dot_general(a, b, (((0,), (0,)), ((), ())), preferred_element_type=FULL)


def rope_tables(rows):
    position = np.arange(rows, dtype=np.float32)[:, None]
    exponent = np.arange(HDIM // 2, dtype=np.float32) * np.float32(2.0 / HDIM)
    angles = position / np.power(np.float32(10000.0), exponent)[None, :]
    angles = angles.astype(np.float32).astype(np.float64)
    cosine, sine = np.cos(angles).astype(np.float32), np.sin(angles).astype(np.float32)
    return (
        np.concatenate([cosine] * 4, axis=1),
        np.concatenate([-sine, sine, -sine, sine], axis=1),
    )


def turned(value, cosine, sine):
    width = value.shape[1]
    lane = lax.broadcasted_iota(jnp.int32, value.shape, 1) % HDIM
    swapped = jnp.where(
        lane < HDIM // 2,
        pltpu.roll(value, width - HDIM // 2, 1),
        pltpu.roll(value, HDIM // 2, 1),
    )
    count = width // 128
    if count > 1:
        cosine = jnp.concatenate([cosine] * count, axis=1)
        sine = jnp.concatenate([sine] * count, axis=1)
    return value * cosine + swapped * sine


def project_body(where, *refs):
    rows, cosine, sine, (gain, w_query, w_key, w_value) = refs[:2], refs[2:4], refs[4:6], refs[6:10]
    normed_out, query_out, pair_out, cosine_out, sine_out, w_pair = refs[10:]
    rows, cosine, sine = [
        jnp.concatenate([pair[0][...], pair[1][...]], axis=0) for pair in (rows, cosine, sine)
    ]
    cosine_out[...] = cosine
    sine_out[...] = sine

    @pl.when(pl.program_id(0) == 0)
    def _():
        w_pair[...] = jnp.concatenate([w_key[...], w_value[...]], axis=0)

    value = rows.astype(FULL)
    inv = lax.rsqrt(jnp.mean(value * value, axis=-1, keepdims=True) + EPS)
    normed = (value * inv * gain[...].astype(FULL)).astype(LOW)
    normed_out[...] = normed
    query_out[...] = turned(dot(normed, w_query[...]), cosine, sine).astype(LOW)
    pair = dot_t(normed, w_pair[...])
    lane = lax.broadcasted_iota(jnp.int32, pair.shape, 1)
    pair_out[...] = jnp.where(lane < HDIM, turned(pair, cosine, sine), pair).astype(LOW)


def project(blocks, hidden_in, gain, w_query, w_key, w_value):
    rows, model = hidden_in.shape
    step = rows // 4
    cosine, sine = rope_tables(rows)

    def chosen(width):
        return [
            pl.BlockSpec((step, width), lambda i, where, at=at: (where[2 * i + at], 0))
            for at in range(2)
        ]

    def whole(value):
        return pl.BlockSpec(value.shape, lambda i, where: (0, 0))

    def placed(width):
        return pl.BlockSpec((2 * step, width), lambda i, where: (i, 0))

    heads = w_query.shape[1]
    return pl.pallas_call(
        project_body,
        grid_spec=pltpu.PrefetchScalarGridSpec(
            num_scalar_prefetch=1,
            grid=(2,),
            in_specs=chosen(model)
            + chosen(128)
            + chosen(128)
            + [whole(gain), whole(w_query), whole(w_key), whole(w_value)],
            out_specs=[placed(model), placed(heads)] + [placed(2 * HDIM)] * 3,
            scratch_shapes=[pltpu.VMEM((2 * HDIM, model), LOW)],
        ),
        out_shape=[
            jax.ShapeDtypeStruct((rows, model), LOW),
            jax.ShapeDtypeStruct((rows, heads), LOW),
            jax.ShapeDtypeStruct((rows, 2 * HDIM), LOW),
            jax.ShapeDtypeStruct((rows, 2 * HDIM), FULL),
            jax.ShapeDtypeStruct((rows, 2 * HDIM), FULL),
        ],
        compiler_params=pltpu.CompilerParams(
            vmem_limit_bytes=60 * 1024 * 1024, dimension_semantics=("arbitrary",)
        ),
        cost_estimate=pl.CostEstimate(
            flops=2 * rows * model * (heads + 2 * HDIM),
            bytes_accessed=2 * (2 * rows * model + model * (heads + 4 * HDIM) + rows * 640),
            transcendentals=rows,
        ),
    )(
        jnp.stack(blocks).astype(jnp.int32),
        *[hidden_in] * 2,
        *[jnp.asarray(cosine)] * 2,
        *[jnp.asarray(sine)] * 2,
        gain,
        w_query,
        w_key,
        w_value,
    )


def swap_halves(value):
    half = value.shape[0] // 2
    return jnp.concatenate([value[half:], value[:half]], axis=0)


def heads_of(where, mine, partner, step):
    use_mine = (step // 2 == 0) == (where[4] == 1)
    return jnp.where(use_mine, mine[...].astype(FULL), swap_halves(partner[...]).astype(FULL))


def allowed_pairs(where, rows):
    step = rows // 4

    def positions(shape, axis):
        index = lax.broadcasted_iota(jnp.int32, shape, axis)
        base = where[3] - 3
        for block in (2, 1, 0):
            base = jnp.where(index < (block + 1) * step, where[block] - block, base)
        return index + base * step

    keys, queries = positions((rows, 1), 0), positions((1, rows), 1)
    return (keys <= queries) & (keys < where[5])


def placed_heads(head):
    low = lax.broadcasted_iota(jnp.int32, head.shape, 1) < HDIM
    return (
        jnp.where(low, head, 0.0).astype(LOW),
        jnp.where(low, 0.0, pltpu.roll(head, HDIM, 1)).astype(LOW),
    )


def attend_body(where, query, mine, partner, out, lse_out):
    both = heads_of(where, mine, partner, pl.program_id(0))
    allowed = allowed_pairs(where, both.shape[0])
    value_t = both.T[HDIM:].astype(LOW)
    mixed = []
    for index, key in enumerate(placed_heads(both)):
        scores = dot_t(key, query[...]) * HDIM ** (-0.5)
        scores = jnp.where(allowed, scores, -1e30)
        top = jnp.max(scores, axis=0, keepdims=True)
        weights = jnp.exp(scores - top)
        total = jnp.sum(weights, axis=0, keepdims=True)
        lse_out[0, index : index + 1, :] = top + jnp.log(total)
        mixed.append(dot(value_t, (weights / total).astype(LOW)))
    out[...] = jnp.concatenate(mixed, axis=0).T.astype(LOW)


def attend_specs(rows, lanes):
    pair = pl.BlockSpec((rows, lanes), lambda i, where: (0, i))
    whole = pl.BlockSpec((rows, lanes), lambda i, where: (0, 0))
    lse = pl.BlockSpec((1, 2, rows), lambda i, where: (i, 0, 0))
    return pair, whole, lse


def attend(where, query, mine, partner):
    rows, lanes = mine.shape
    steps = query.shape[1] // lanes
    pair, whole, lse = attend_specs(rows, lanes)
    return pl.pallas_call(
        attend_body,
        grid_spec=pltpu.PrefetchScalarGridSpec(
            num_scalar_prefetch=1,
            grid=(steps,),
            in_specs=[pair, whole, whole],
            out_specs=[pair, lse],
        ),
        out_shape=[
            jax.ShapeDtypeStruct(query.shape, LOW),
            jax.ShapeDtypeStruct((steps, 2, rows), FULL),
        ],
        compiler_params=pltpu.CompilerParams(
            vmem_limit_bytes=24 * 1024 * 1024, dimension_semantics=("arbitrary",)
        ),
        cost_estimate=pl.CostEstimate(
            flops=4 * rows * rows * query.shape[1],
            bytes_accessed=8 * rows * query.shape[1],
            transcendentals=2 * steps * rows * rows,
        ),
    )(where, query, mine, partner)


def attend_back_body(where, query, mine, partner, grad, lse, cosine, sine, dquery, dboth, acc):
    step = pl.program_id(0)
    both = heads_of(where, mine, partner, step)
    allowed = allowed_pairs(where, both.shape[0])
    low = lax.broadcasted_iota(jnp.int32, both.shape, 1) < HDIM
    key_t = both.T[:HDIM].astype(LOW)
    keys = placed_heads(both)
    values = placed_heads(pltpu.roll(both, HDIM, 1))
    dkeys, dvalues, mixed = [], [], []
    for index in range(2):
        scores = dot_t(keys[index], query[...]) * HDIM ** (-0.5)
        probs = jnp.where(allowed, jnp.exp(scores - lse[0, index : index + 1, :]), 0.0)
        dprobs = dot_t(values[index], grad[...])
        delta = jnp.sum(dprobs * probs, axis=0, keepdims=True)
        dscores = (probs * (dprobs - delta)).astype(LOW)
        dvalues.append(dot(probs.astype(LOW), grad[...]))
        dkeys.append(dot(dscores, query[...]))
        mixed.append(dot(key_t, dscores))
    turn_back = jnp.concatenate(mixed, axis=0).T * HDIM ** (-0.5)
    dquery[...] = turned(turn_back, cosine[...], -sine[...]).astype(LOW)
    dkey = jnp.where(low, dkeys[0], dkeys[1]) * HDIM ** (-0.5)
    dvalue = jnp.where(low, dvalues[0], dvalues[1])

    @pl.when(step % 2 == 0)
    def _():
        acc[0], acc[1] = dkey, dvalue

    @pl.when(step % 2 == 1)
    def _():
        key_sum, value_sum = acc[0] + dkey, acc[1] + dvalue
        dboth[0] = jnp.where(
            low,
            key_sum + pltpu.roll(key_sum, HDIM, 1),
            value_sum + pltpu.roll(value_sum, HDIM, 1),
        )


def attend_back(where, query, mine, partner, grad, lse, cosine, sine):
    rows, lanes = mine.shape
    steps = query.shape[1] // lanes
    pair, whole, lse_spec = attend_specs(rows, lanes)
    slot = pl.BlockSpec((1, rows, lanes), lambda i, where: ((i // 2) ^ (1 - where[4]), 0, 0))
    return pl.pallas_call(
        attend_back_body,
        grid_spec=pltpu.PrefetchScalarGridSpec(
            num_scalar_prefetch=1,
            grid=(steps,),
            in_specs=[pair, whole, whole, pair, lse_spec, whole, whole],
            out_specs=[pair, slot],
            scratch_shapes=[pltpu.VMEM((2, rows, lanes), FULL)],
        ),
        out_shape=[
            jax.ShapeDtypeStruct(query.shape, LOW),
            jax.ShapeDtypeStruct((2, rows, lanes), FULL),
        ],
        compiler_params=pltpu.CompilerParams(
            vmem_limit_bytes=24 * 1024 * 1024, dimension_semantics=("arbitrary",)
        ),
        cost_estimate=pl.CostEstimate(
            flops=10 * rows * rows * query.shape[1],
            bytes_accessed=8 * rows * query.shape[1],
            transcendentals=2 * steps * rows * rows,
        ),
    )(where, query, mine, partner, grad, lse, cosine, sine)


def join_back_body(dboth, incoming, cosine, sine, out):
    total = dboth[0] + swap_halves(incoming[...])
    low = lax.broadcasted_iota(jnp.int32, total.shape, 1) < HDIM
    out[...] = jnp.where(low, turned(total, cosine[...], -sine[...]), total).astype(LOW)


def join_back(dboth, incoming, cosine, sine):
    return pl.pallas_call(
        join_back_body,
        out_shape=jax.ShapeDtypeStruct(incoming.shape, LOW),
        compiler_params=pltpu.CompilerParams(vmem_limit_bytes=24 * 1024 * 1024),
    )(dboth, incoming, cosine, sine)


def put_turned(value, out):
    for block in range(0, 32, 2):
        pair = value[:, block * 64 : block * 64 + 128].T
        for which in range(2):
            at = ((block + which) % 16 * 2 + block // 16) * 64
            out[at : at + 64] = pair[which * 64 : which * 64 + 64]


def prepare_body(where, cotangent, out, out_t):
    value = cotangent[...]
    step = value.shape[0]
    row = lax.broadcasted_iota(jnp.int32, (step, 1), 0) + where[pl.program_id(0)] * step
    value = jnp.where(row < where[5], value, jnp.zeros_like(value))
    out[...] = value
    put_turned(value, out_t)


def prepare(where, cotangent):
    rows, model = cotangent.shape
    step = rows // 4
    return pl.pallas_call(
        prepare_body,
        grid_spec=pltpu.PrefetchScalarGridSpec(
            num_scalar_prefetch=1,
            grid=(4,),
            in_specs=[pl.BlockSpec((step, model), lambda i, where: (where[i], 0))],
            out_specs=[
                pl.BlockSpec((step, model), lambda i, where: (i, 0)),
                pl.BlockSpec((model, step), lambda i, where: (0, i)),
            ],
        ),
        out_shape=[
            jax.ShapeDtypeStruct((rows, model), LOW),
            jax.ShapeDtypeStruct((model, rows), LOW),
        ],
        compiler_params=pltpu.CompilerParams(
            vmem_limit_bytes=24 * 1024 * 1024, dimension_semantics=("arbitrary",)
        ),
        cost_estimate=pl.CostEstimate(
            flops=rows * model, bytes_accessed=6 * rows * model, transcendentals=0
        ),
    )(where, cotangent)


def gated(gate, up, back):
    gate, up = gate.astype(LOW).astype(FULL), up.astype(LOW).astype(FULL)
    sigmoid = jax.nn.sigmoid(gate)
    activated = gate * sigmoid
    dgate = back * up * sigmoid * (1.0 + gate * (1.0 - sigmoid))
    return (activated * up).astype(LOW), dgate.astype(LOW), (back * activated).astype(LOW)


def feed_body(*refs):
    pieces, near, (w_gate, w_up, dhidden, dy_t) = refs[:4], refs[4:7], refs[7:11]
    outs, (grads, far, rows_t) = refs[11:14], refs[14:]
    height = pieces[0].shape[0]
    step, last = pl.program_id(0), pl.num_programs(0) - 1

    @pl.when(step == 0)
    def _():
        far[:height] = pieces[1][...]
        far[height:] = pieces[3][...]
        put_turned(jnp.concatenate([piece[...] for piece in pieces], axis=0), rows_t)

    rest = grads.shape[1] // 6

    def columns(width):
        at = slice(0, width)

        products = [dot(far[...], weight[:, at]) for weight in (w_gate, w_up)]
        back = jnp.concatenate(
            [dhidden[height : 2 * height, at], dhidden[3 * height :, at]], axis=0
        )
        fans = []
        for close, other, out in zip(near, gated(*products, back), outs):
            close = close[:, at]
            parts = [close[:height], other[:height], close[height:], other[height:]]
            fans.append(jnp.concatenate(parts, axis=0))
            out[:, at] = fans[-1]
        for index, (side, fan) in enumerate(zip((dy_t, rows_t, rows_t), fans)):
            grads[:, index * width : (index + 1) * width] = dot(side[...], fan).astype(LOW)

    pl.when(step < last)(lambda: columns(256))
    pl.when(step == last)(lambda: columns(rest))


def feed(pieces, near, w_gate, w_up, dhidden, dy_t):
    rows, width = dhidden.shape
    model = w_gate.shape[0]
    across = pl.BlockSpec((rows, 256), lambda i: (0, i))
    weight = pl.BlockSpec((model, 256), lambda i: (0, i))
    whole = lambda value: pl.BlockSpec(value.shape, lambda i: (0, 0))
    return pl.pallas_call(
        feed_body,
        grid=(pl.cdiv(width, 256),),
        in_specs=[whole(piece) for piece in pieces]
        + [pl.BlockSpec((rows // 2, 256), lambda i: (0, i))] * 3
        + [weight, weight, across, whole(dy_t)],
        out_specs=[across] * 3 + [pl.BlockSpec((model, 768), lambda i: (0, i))],
        out_shape=[jax.ShapeDtypeStruct((rows, width), LOW)] * 3
        + [jax.ShapeDtypeStruct((model, 3 * width), LOW)],
        scratch_shapes=[pltpu.VMEM((rows // 2, model), LOW), pltpu.VMEM((model, rows), LOW)],
        compiler_params=pltpu.CompilerParams(
            vmem_limit_bytes=48 * 1024 * 1024, dimension_semantics=("arbitrary",)
        ),
        cost_estimate=pl.CostEstimate(
            flops=10 * rows * model * width,
            bytes_accessed=10 * model * width + 10 * rows * width + 4 * rows * model,
            transcendentals=rows * width,
        ),
    )(*pieces, *near, w_gate, w_up, dhidden, dy_t)


def split_turns(value):
    width = value.shape[1] // 3
    turns, rest = width // 256, width % 256
    out = []
    for at in range(3):
        parts = [value[:, i * 768 + at * 256 : i * 768 + at * 256 + 256] for i in range(turns)]
        start = turns * 768 + at * rest
        out.append(jnp.concatenate(parts + [value[:, start : start + rest]], axis=1))
    return out


def feed_back_body(dgate, dup, w_gate, w_up, mine, other):
    value = dot_t(dgate[...], w_gate[...]) + dot_t(dup[...], w_up[...])
    half = value.shape[0] // 2
    mine[...] = value[:half]
    other[...] = value[half:].astype(LOW)


def feed_back(dgate, dup, w_gate, w_up):
    rows, width = dgate.shape
    model = w_gate.shape[0]
    whole = pl.BlockSpec((rows, width), lambda i: (0, 0))
    weight = pl.BlockSpec((256, width), lambda i: (i, 0))
    across = pl.BlockSpec((rows // 2, 256), lambda i: (0, i))
    return pl.pallas_call(
        feed_back_body,
        grid=(model // 256,),
        in_specs=[whole, whole, weight, weight],
        out_specs=[across, across],
        out_shape=[
            jax.ShapeDtypeStruct((rows // 2, model), FULL),
            jax.ShapeDtypeStruct((rows // 2, model), LOW),
        ],
        compiler_params=pltpu.CompilerParams(
            vmem_limit_bytes=60 * 1024 * 1024, dimension_semantics=("arbitrary",)
        ),
        cost_estimate=pl.CostEstimate(
            flops=4 * rows * model * width,
            bytes_accessed=4 * model * width + 4 * rows * width + 3 * rows * model,
            transcendentals=0,
        ),
    )(dgate, dup, w_gate, w_up)


def input_back_body(dquery, dpair, w_query, w_key, w_value, rows, mine, other, gain, w_pair):
    w_pair[:HDIM] = w_key[...]
    w_pair[HDIM:] = w_value[...]
    value = dot_t(dquery[...], w_query[...]) + dot(dpair[...], w_pair[...])
    half = value.shape[0] // 2
    mine[...] = value[:half]
    other[...] = value[half:].astype(LOW)
    gain[...] = jnp.sum(value * rows[...].astype(FULL), axis=0, keepdims=True)


def input_back(dquery, dpair, w_query, w_key, w_value, normed):
    rows, model = normed.shape
    whole = lambda value: pl.BlockSpec(value.shape, lambda i: (0, 0))
    across = lambda height: pl.BlockSpec((height, 256), lambda i: (0, i))
    return pl.pallas_call(
        input_back_body,
        grid=(model // 256,),
        in_specs=[
            whole(dquery),
            whole(dpair),
            pl.BlockSpec((256, w_query.shape[1]), lambda i: (i, 0)),
            across(HDIM),
            across(HDIM),
            across(rows),
        ],
        out_specs=[across(rows // 2), across(rows // 2), across(1)],
        out_shape=[
            jax.ShapeDtypeStruct((rows // 2, model), FULL),
            jax.ShapeDtypeStruct((rows // 2, model), LOW),
            jax.ShapeDtypeStruct((1, model), FULL),
        ],
        scratch_shapes=[pltpu.VMEM((2 * HDIM, 256), LOW)],
        compiler_params=pltpu.CompilerParams(
            vmem_limit_bytes=60 * 1024 * 1024, dimension_semantics=("arbitrary",)
        ),
        cost_estimate=pl.CostEstimate(
            flops=2 * rows * model * 640,
            bytes_accessed=model * 1280 + 5 * rows * model,
            transcendentals=0,
        ),
    )(dquery, dpair, w_query, w_key, w_value, normed)


def wgrad_body(ring, orders, where, side, fan, *refs):
    step = pl.program_id(0)
    value = dot_rows(side[...], fan[...])
    if ring == "z":
        total = refs[4]
        total[...] = value

    for half in range(2):
        send_ref, keep_ref = refs[2 * half : 2 * half + 2]
        at = step - 4 * half
        if ring == "z":
            def piece(bits):
                start = pl.multiple_of(where[8 + bits], 64)
                return total[pl.ds(start, 64), :].astype(LOW)

            @pl.when((at >= 0) & (at < 4))
            def _():
                order = orders[half]
                send_ref[0:64] = piece(order[0])
                send_ref[64:128] = piece(order[1])
                keep_ref[0:64] = piece(order[2])
                keep_ref[64:128] = piece(order[3])
        else:

            @pl.when((at >= 0) & (at < 2))
            def _():
                send_ref[...] = value.astype(LOW)

            @pl.when((at >= 2) & (at < 4))
            def _():
                keep_ref[...] = value.astype(LOW)


def wgrad(place, core, side, fan, ring):
    tokens, width = fan.shape
    x, z = place
    orders = [(first, 2, 0, 4 - first) for first in (1, 3)]
    blocks = []
    for half in range(2):
        steps = orders[half] if ring == "x" else range(4)
        blocks += [(core ^ half) * 4 + (x ^ bits) for bits in steps]
    where = jnp.stack(blocks + [(z ^ bits) * 64 for bits in range(4)]).astype(jnp.int32)
    rows = 256 if ring == "x" else 128

    def place_of(low, high):
        return pl.BlockSpec((rows, width), lambda i, where: (jnp.clip(i - low, 0, high), 0))

    if ring == "x":
        out_specs = [place_of(low, 1) for low in (0, 2, 4, 6)]
    else:
        out_specs = [place_of(low, 3) for low in (0, 0, 4, 4)]
    return pl.pallas_call(
        functools.partial(wgrad_body, ring, orders),
        grid_spec=pltpu.PrefetchScalarGridSpec(
            num_scalar_prefetch=1,
            grid=(8,),
            in_specs=[
                pl.BlockSpec((tokens, 256), lambda i, where: (0, where[i])),
                pl.BlockSpec((tokens, width), lambda i, where: (0, 0)),
            ],
            out_specs=out_specs,
            scratch_shapes=[pltpu.VMEM((256, width), FULL)] if ring == "z" else [],
        ),
        out_shape=[jax.ShapeDtypeStruct((512, width), LOW)] * 4,
        compiler_params=pltpu.CompilerParams(
            vmem_limit_bytes=24 * 1024 * 1024, dimension_semantics=("arbitrary",)
        ),
        cost_estimate=pl.CostEstimate(
            flops=2 * tokens * 2048 * width,
            bytes_accessed=2 * tokens * (2048 + width) + 4 * 2048 * width,
            transcendentals=0,
        ),
    )(where, side, fan)


def scatter_planes(value):
    groups = [[16 * yh + i for i in range(16)] for yh in range(2)]
    return lax.psum_scatter(
        value, "dp", scatter_dimension=0, axis_index_groups=groups, tiled=True
    )


def tie(value, *others):
    return lax.optimization_barrier((value, *others))[0]


class Grad:
    def __init__(self, links, place, core, side, fan, ring):
        self.links, self.ring = links, ring
        send0, keep0, send1, keep1 = wgrad(place, core, side, fan, ring)
        self.shape = (4, 2, 64, fan.shape[1]) if ring == "z" else (2, 4, 64, fan.shape[1])
        self.sent = [send0, send1]
        self.keep = [keep0.reshape(self.shape), keep1.reshape(self.shape)]

    def part(self, value, which):
        axis = 1 if self.ring == "z" else 0
        return lax.index_in_dim(value, which, axis, False).astype(FULL)

    def first(self):
        got = [self.links.send(self.sent[half], self.ring, (1, 3)[half]) for half in range(2)]
        self.got = [item.reshape(self.shape) for item in got]

    def second(self):
        self.sent = [
            (self.part(self.keep[half], 1) + self.part(self.got[half], 1)).astype(LOW)
            for half in range(2)
        ]
        self.got_next = [
            self.links.send(self.sent[half], self.ring, (3, 1)[half]) for half in range(2)
        ]

    def halves(self):
        halves = []
        for half in range(2):
            got_next = self.got_next[half]
            got = tie(self.got[half], got_next)
            halves.append(
                self.part(self.keep[half], 0) + self.part(got, 0) + got_next.astype(FULL)
            )
        return halves


class End:
    def __init__(self, links, grad, at):
        ring = "z" if grad.ring == "x" else "x"
        values = jnp.stack(grad.halves(), axis=1)

        def block(bits):
            index = at ^ bits if ring == "z" else bits
            return lax.dynamic_index_in_dim(values, index, 0, False)

        self.keep = block(0)
        self.sent = [block(bits).astype(LOW) for bits in (1, 3, 2)]
        before = [links.last[ring, 1], links.last[ring, 3]]
        self.got = [
            over_ring(tie(item, *before), ring, bits)
            for item, bits in zip(self.sent, (1, 3, 2))
        ]

    def totals(self):
        return self.keep + sum(item.astype(FULL) for item in self.got)


def finish_together(ends, same):
    parts = [end.totals() for end in ends]
    values = jnp.concatenate(parts, axis=2)
    send = jnp.where(same, values[1], values[0]).astype(LOW)
    total = jnp.where(same, values[0], values[1]) + over_yh(send).astype(FULL)
    out, at = [], 0
    for part in parts:
        width = part.shape[2]
        out.append(total[:, at : at + width])
        at += width
    return out


def sent(*tasks):
    return [item for task in tasks for item in task.sent]


def sum_ring(value, ring):
    return value + over_ring(value, ring, 1) + over_ring(value, ring, 3) + over_ring(value, ring, 2)


def per_device(
    hidden_in,
    cotangent,
    seq_lengths,
    slot_order,
    attn_gain,
    w_query,
    w_key,
    w_value,
    w_out,
    mlp_gain,
    w_gate,
    w_up,
    w_down,
):
    rows = hidden_in.shape[0]
    own_rows = rows // 4
    heads = w_query.shape[1] // HDIM
    ff = w_gate.shape[1]
    dp_at = lax.axis_index("dp")
    yh, x, z = dp_at // 16, (dp_at // 4) % 4, dp_at % 4
    place = (x, z)
    tensor_at = lax.axis_index("tensor")
    core = tensor_at % 2
    blocks = [tensor_at ^ bits for bits in (0, 2, 1, 3)]

    sequence = slot_order[0]
    length = jnp.sum(
        jnp.where(jnp.arange(seq_lengths.shape[0], dtype=jnp.int32) == sequence, seq_lengths, 0)
    )
    gain_one = attn_gain.astype(FULL)
    gain_two = mlp_gain.astype(FULL)

    links = Links()
    links = Links()
    attn_in, queries, packed, cosine, sine = project(
        blocks, hidden_in, attn_gain[None, :], w_query, w_key.T, w_value.T
    )
    partner = over_tensor(packed, 1)
    where = jnp.stack(blocks + [1 - core, length]).astype(jnp.int32)
    attended, lse = attend(where, queries, packed, partner)

    half = 2 * own_rows

    got = over_tensor(dot(attended[half:], w_out).astype(LOW), 1)
    mine = dot(attended[:half], w_out)
    send = (mine[own_rows:] + got[own_rows:].astype(FULL)).astype(LOW)
    dy_low, dy_t = prepare(where, tie(cotangent, send))
    grad_hidden = dot_t(dy_low, w_down)
    got_next = tie(over_tensor(send, 2), dy_t, grad_hidden)
    inputs = lax.dynamic_slice_in_dim(hidden_in, tensor_at * own_rows, own_rows, 0).astype(FULL)
    got = tie(got, got_next)
    middle = inputs + mine[:own_rows] + got[:own_rows].astype(FULL) + got_next.astype(FULL)
    inv_two = lax.rsqrt(jnp.mean(middle * middle, axis=-1, keepdims=True) + EPS)
    normed_two = middle * inv_two
    own = (normed_two * gain_two).astype(LOW)

    got = over_tensor(own, 2)
    got_own = over_tensor(own, 1)
    near = jnp.concatenate([own, got_own], axis=0)
    back_near = jnp.concatenate(
        [grad_hidden[:own_rows], grad_hidden[half : half + own_rows]], axis=0
    )
    done_near = gated(dot(near, w_gate), dot(near, w_up), back_near)
    got = tie(got, *done_near)
    hidden, grad_gate, grad_up, mlp_grads = feed(
        [own, got, got_own, over_tensor(got, 1)],
        done_near,
        w_gate,
        w_up,
        grad_hidden,
        dy_t,
    )

    def grad_of(side, fan, ring):
        return Grad(links, place, core, side, fan, ring)

    same = yh == core
    mlp_sum = scatter_planes(mlp_grads)
    mine, other = feed_back(grad_gate, grad_up, w_gate, w_up)
    got = over_tensor(other, 1)
    send = (mine[own_rows:] + got[own_rows:].astype(FULL)).astype(LOW)
    got_next = over_tensor(send, 2)
    mlp_send = dot(tie(hidden, send)[half:], w_down).astype(LOW)
    mlp_got = over_tensor(mlp_send, 1)
    mlp_mine = dot(tie(hidden, mlp_send)[:half], w_down)
    got_next = tie(got_next, mlp_mine)
    got = tie(got, got_next)
    mlp_back = mine[:own_rows] + got[:own_rows].astype(FULL) + got_next.astype(FULL)

    scaled_two = mlp_back * gain_two
    dmid = dy_low[:own_rows].astype(FULL) + inv_two * (
        scaled_two - normed_two * jnp.mean(scaled_two * normed_two, axis=-1, keepdims=True)
    )
    gain_two_part = jnp.sum(mlp_back * normed_two, axis=0)
    own = dmid.astype(LOW)
    got = over_tensor(own, 2)
    mlp_got = tie(mlp_got, own)
    mlp_send = (mlp_mine[own_rows:] + mlp_got[own_rows:].astype(FULL)).astype(LOW)
    output_rows = middle + mlp_mine[:own_rows] + mlp_got[:own_rows].astype(FULL)
    got = tie(got, mlp_send, output_rows)
    mlp_got = over_tensor(tie(mlp_send, got), 2)
    pair = jnp.concatenate([own, got], axis=0)
    got_last = over_tensor(pair, 1)
    dmid_low = jnp.concatenate([pair, got_last], axis=0)

    grad_attended = dot_t(dmid_low, w_out).astype(LOW)
    query_low, dboth = attend_back(
        where, queries, packed, partner, grad_attended, lse, cosine, sine
    )
    incoming = over_tensor(dboth[1], 1)
    incoming = tie(incoming, mlp_got)
    key_value_low = join_back(dboth, incoming, cosine, sine)
    qkv_low = jnp.concatenate([query_low, key_value_low], axis=1)
    mine, other, gain_one_sum = input_back(
        query_low, key_value_low, w_query, w_key.T, w_value.T, attn_in
    )
    gains = jnp.stack([gain_one_sum[0] / gain_one, gain_two_part])
    got = over_tensor(other, 1)
    send = (mine[own_rows:] + got[own_rows:].astype(FULL)).astype(LOW)
    got_next = over_tensor(send, 2)
    for ring in ("x", "z"):
        gains = sum_ring(tie(gains, send), ring)
    qkv = grad_of(attn_in, tie(qkv_low, gains), "z")
    out = grad_of(tie(dmid_low, *qkv.sent), attended, "x")
    qkv.first()
    out.first()
    got = tie(got, got_next)
    attn_back = mine[:own_rows] + got[:own_rows].astype(FULL) + got_next.astype(FULL)

    output_rows = (output_rows + mlp_got.astype(FULL)).astype(LOW)

    inv_one = lax.rsqrt(jnp.mean(inputs * inputs, axis=-1, keepdims=True) + EPS)
    normed_one = inputs * inv_one
    scaled_one = attn_back * gain_one
    input_grad = dmid + inv_one * (
        scaled_one - normed_one * jnp.mean(scaled_one * normed_one, axis=-1, keepdims=True)
    )
    mlp_keep = lax.dynamic_slice_in_dim(mlp_sum, yh * 64, 64, 0).astype(FULL)
    mlp_send = lax.dynamic_slice_in_dim(mlp_sum, (1 - yh) * 64, 64, 0)
    gains = tie(gains, input_grad, *out.sent)
    gains = gains + over_yh(gains)
    gains = gains + over_tensor(gains, 2)
    gains = gains + over_tensor(gains, 1)
    out.second()
    qkv.second()
    mlp_rows_got = over_yh(mlp_send)
    qkv.got_next[0] = tie(qkv.got_next[0], mlp_rows_got)
    out.got_next[0] = tie(out.got_next[0], mlp_rows_got)
    ends = [End(links, out, z), End(links, qkv, x)]
    out_rows, qkv_rows = finish_together(ends, same)
    down_rows, gate_rows, up_rows = split_turns(mlp_keep + mlp_rows_got.astype(FULL))
    q_cols = heads * HDIM
    return (
        output_rows,
        input_grad,
        gains[0],
        qkv_rows[:, :q_cols],
        qkv_rows[:, q_cols : q_cols + HDIM],
        qkv_rows[:, q_cols + HDIM :],
        out_rows.T,
        gains[1],
        gate_rows,
        up_rows,
        down_rows.T,
    )


def solution(mesh):
    return jax.shard_map(
        per_device,
        mesh=mesh,
        in_specs=(
            P("dp", None),
            P("dp", None),
            P(),
            P("dp"),
            P(),
            P(None, "tensor"),
            P(None, "tensor"),
            P(None, "tensor"),
            P("tensor", None),
            P(),
            P(None, "tensor"),
            P(None, "tensor"),
            P("tensor", None),
        ),
        out_specs=(
            P(("dp", "tensor"), None),
            P(("dp", "tensor"), None),
            P(),
            P("dp", "tensor"),
            P("dp", "tensor"),
            P("dp", "tensor"),
            P("tensor", "dp"),
            P(),
            P("dp", "tensor"),
            P("dp", "tensor"),
            P("tensor", "dp"),
        ),
        check_vma=False,
    )
```

```python
import functools

import jax
import jax.numpy as jnp
import numpy as np
from jax import lax
from jax.experimental import pallas as pl
from jax.experimental.pallas import tpu as pltpu
from jax.sharding import PartitionSpec as P

HDIM = 64
EPS = 1e-05
LOW = jnp.bfloat16
FULL = jnp.float32


def ring_perm(ring, bits):
    step = bits * (4 if ring == "x" else 1)
    return [(i, i ^ step) for i in range(32)]


class Links:
    def __init__(self):
        self.last = {}

    def send(self, value, ring, bits):
        names = [(ring, name) for name in ((1, 3) if bits == 2 else (bits,))]
        before = [self.last[name] for name in names if name in self.last]
        if before:
            value = tie(value, *before)
        out = over_ring(value, ring, bits)
        for name in names:
            self.last[name] = out
        return out


def over_ring(value, ring, bits):
    return lax.ppermute(value, "dp", ring_perm(ring, bits))


def over_yh(value):
    return lax.ppermute(value, "dp", [(i, i ^ 16) for i in range(32)])


def over_tensor(value, bits):
    return lax.ppermute(value, "tensor", [(i, i ^ bits) for i in range(4)])


def dot(a, b):
    return jnp.dot(a, b, preferred_element_type=FULL)


def dot_t(a, b):
    return lax.dot_general(a, b, (((1,), (1,)), ((), ())), preferred_element_type=FULL)


def dot_rows(a, b):
    return lax.dot_general(a, b, (((0,), (0,)), ((), ())), preferred_element_type=FULL)


def rope_tables(rows):
    position = np.arange(rows, dtype=np.float32)[:, None]
    exponent = np.arange(HDIM // 2, dtype=np.float32) * np.float32(2.0 / HDIM)
    angles = position / np.power(np.float32(10000.0), exponent)[None, :]
    angles = angles.astype(np.float32).astype(np.float64)
    cosine, sine = np.cos(angles).astype(np.float32), np.sin(angles).astype(np.float32)
    return (
        np.concatenate([cosine] * 4, axis=1),
        np.concatenate([-sine, sine, -sine, sine], axis=1),
    )


def turned(value, cosine, sine):
    width = value.shape[1]
    lane = lax.broadcasted_iota(jnp.int32, value.shape, 1) % HDIM
    swapped = jnp.where(
        lane < HDIM // 2,
        pltpu.roll(value, width - HDIM // 2, 1),
        pltpu.roll(value, HDIM // 2, 1),
    )
    count = width // 128
    if count > 1:
        cosine = jnp.concatenate([cosine] * count, axis=1)
        sine = jnp.concatenate([sine] * count, axis=1)
    return value * cosine + swapped * sine


def project_body(where, rows, gain, w_query, w_key, w_value, cosine, sine, *refs):
    normed_out, query_out, pair_out, cosine_out, sine_out, w_pair = refs
    cosine_out[...] = cosine[...]
    sine_out[...] = sine[...]

    @pl.when(pl.program_id(0) == 0)
    def _():
        w_pair[...] = jnp.concatenate([w_key[...], w_value[...]], axis=0)

    value = rows[...].astype(FULL)
    inv = lax.rsqrt(jnp.mean(value * value, axis=-1, keepdims=True) + EPS)
    normed = (value * inv * gain[...].astype(FULL)).astype(LOW)
    normed_out[...] = normed
    query_out[...] = turned(dot(normed, w_query[...]), cosine[...], sine[...]).astype(LOW)
    pair = dot_t(normed, w_pair[...])
    lane = lax.broadcasted_iota(jnp.int32, pair.shape, 1)
    pair_out[...] = jnp.where(lane < HDIM, turned(pair, cosine[...], sine[...]), pair).astype(LOW)


def project(blocks, hidden_in, gain, w_query, w_key, w_value):
    rows, model = hidden_in.shape
    step = rows // 4
    cosine, sine = rope_tables(rows)

    def chosen(width):
        return pl.BlockSpec((step, width), lambda i, where: (where[i], 0))

    def whole(value):
        return pl.BlockSpec(value.shape, lambda i, where: (0, 0))

    def placed(width):
        return pl.BlockSpec((step, width), lambda i, where: (i, 0))

    heads = w_query.shape[1]
    return pl.pallas_call(
        project_body,
        grid_spec=pltpu.PrefetchScalarGridSpec(
            num_scalar_prefetch=1,
            grid=(4,),
            in_specs=[
                chosen(model),
                whole(gain),
                whole(w_query),
                whole(w_key),
                whole(w_value),
                chosen(128),
                chosen(128),
            ],
            out_specs=[placed(model), placed(heads)] + [placed(2 * HDIM)] * 3,
            scratch_shapes=[pltpu.VMEM((2 * HDIM, model), LOW)],
        ),
        out_shape=[
            jax.ShapeDtypeStruct((rows, model), LOW),
            jax.ShapeDtypeStruct((rows, heads), LOW),
            jax.ShapeDtypeStruct((rows, 2 * HDIM), LOW),
            jax.ShapeDtypeStruct((rows, 2 * HDIM), FULL),
            jax.ShapeDtypeStruct((rows, 2 * HDIM), FULL),
        ],
        compiler_params=pltpu.CompilerParams(
            vmem_limit_bytes=60 * 1024 * 1024, dimension_semantics=("arbitrary",)
        ),
        cost_estimate=pl.CostEstimate(
            flops=2 * rows * model * (heads + 2 * HDIM),
            bytes_accessed=2 * (2 * rows * model + model * (heads + 4 * HDIM) + rows * 640),
            transcendentals=rows,
        ),
    )(
        jnp.stack(blocks).astype(jnp.int32),
        hidden_in,
        gain,
        w_query,
        w_key,
        w_value,
        jnp.asarray(cosine),
        jnp.asarray(sine),
    )


def swap_halves(value):
    half = value.shape[0] // 2
    return jnp.concatenate([value[half:], value[:half]], axis=0)


def heads_of(where, mine, partner, step):
    use_mine = (step // 2 == 0) == (where[4] == 1)
    return jnp.where(use_mine, mine[...].astype(FULL), swap_halves(partner[...]).astype(FULL))


def allowed_pairs(where, rows):
    step = rows // 4

    def positions(shape, axis):
        index = lax.broadcasted_iota(jnp.int32, shape, axis)
        base = where[3] - 3
        for block in (2, 1, 0):
            base = jnp.where(index < (block + 1) * step, where[block] - block, base)
        return index + base * step

    keys, queries = positions((rows, 1), 0), positions((1, rows), 1)
    return (keys <= queries) & (keys < where[5])


def placed_heads(head):
    low = lax.broadcasted_iota(jnp.int32, head.shape, 1) < HDIM
    return (
        jnp.where(low, head, 0.0).astype(LOW),
        jnp.where(low, 0.0, pltpu.roll(head, HDIM, 1)).astype(LOW),
    )


def attend_body(where, query, mine, partner, out, lse_out):
    both = heads_of(where, mine, partner, pl.program_id(0))
    allowed = allowed_pairs(where, both.shape[0])
    value_t = both.T[HDIM:].astype(LOW)
    mixed = []
    for index, key in enumerate(placed_heads(both)):
        scores = dot_t(key, query[...]) * HDIM ** (-0.5)
        scores = jnp.where(allowed, scores, -1e30)
        top = jnp.max(scores, axis=0, keepdims=True)
        weights = jnp.exp(scores - top)
        total = jnp.sum(weights, axis=0, keepdims=True)
        lse_out[0, index : index + 1, :] = top + jnp.log(total)
        mixed.append(dot(value_t, (weights / total).astype(LOW)))
    out[...] = jnp.concatenate(mixed, axis=0).T.astype(LOW)


def attend_specs(rows, lanes):
    pair = pl.BlockSpec((rows, lanes), lambda i, where: (0, i))
    whole = pl.BlockSpec((rows, lanes), lambda i, where: (0, 0))
    lse = pl.BlockSpec((1, 2, rows), lambda i, where: (i, 0, 0))
    return pair, whole, lse


def attend(where, query, mine, partner):
    rows, lanes = mine.shape
    steps = query.shape[1] // lanes
    pair, whole, lse = attend_specs(rows, lanes)
    return pl.pallas_call(
        attend_body,
        grid_spec=pltpu.PrefetchScalarGridSpec(
            num_scalar_prefetch=1,
            grid=(steps,),
            in_specs=[pair, whole, whole],
            out_specs=[pair, lse],
        ),
        out_shape=[
            jax.ShapeDtypeStruct(query.shape, LOW),
            jax.ShapeDtypeStruct((steps, 2, rows), FULL),
        ],
        compiler_params=pltpu.CompilerParams(
            vmem_limit_bytes=24 * 1024 * 1024, dimension_semantics=("arbitrary",)
        ),
        cost_estimate=pl.CostEstimate(
            flops=4 * rows * rows * query.shape[1],
            bytes_accessed=8 * rows * query.shape[1],
            transcendentals=2 * steps * rows * rows,
        ),
    )(where, query, mine, partner)


def attend_back_body(where, query, mine, partner, grad, lse, cosine, sine, dquery, dboth, acc):
    step = pl.program_id(0)
    both = heads_of(where, mine, partner, step)
    allowed = allowed_pairs(where, both.shape[0])
    low = lax.broadcasted_iota(jnp.int32, both.shape, 1) < HDIM
    key_t = both.T[:HDIM].astype(LOW)
    keys = placed_heads(both)
    values = placed_heads(pltpu.roll(both, HDIM, 1))
    dkeys, dvalues, mixed = [], [], []
    for index in range(2):
        scores = dot_t(keys[index], query[...]) * HDIM ** (-0.5)
        probs = jnp.where(allowed, jnp.exp(scores - lse[0, index : index + 1, :]), 0.0)
        dprobs = dot_t(values[index], grad[...])
        delta = jnp.sum(dprobs * probs, axis=0, keepdims=True)
        dscores = (probs * (dprobs - delta)).astype(LOW)
        dvalues.append(dot(probs.astype(LOW), grad[...]))
        dkeys.append(dot(dscores, query[...]))
        mixed.append(dot(key_t, dscores))
    turn_back = jnp.concatenate(mixed, axis=0).T * HDIM ** (-0.5)
    dquery[...] = turned(turn_back, cosine[...], -sine[...]).astype(LOW)
    dkey = jnp.where(low, dkeys[0], dkeys[1]) * HDIM ** (-0.5)
    dvalue = jnp.where(low, dvalues[0], dvalues[1])

    @pl.when(step % 2 == 0)
    def _():
        acc[0], acc[1] = dkey, dvalue

    @pl.when(step % 2 == 1)
    def _():
        key_sum, value_sum = acc[0] + dkey, acc[1] + dvalue
        dboth[0] = jnp.where(
            low,
            key_sum + pltpu.roll(key_sum, HDIM, 1),
            value_sum + pltpu.roll(value_sum, HDIM, 1),
        )


def attend_back(where, query, mine, partner, grad, lse, cosine, sine):
    rows, lanes = mine.shape
    steps = query.shape[1] // lanes
    pair, whole, lse_spec = attend_specs(rows, lanes)
    slot = pl.BlockSpec((1, rows, lanes), lambda i, where: ((i // 2) ^ (1 - where[4]), 0, 0))
    return pl.pallas_call(
        attend_back_body,
        grid_spec=pltpu.PrefetchScalarGridSpec(
            num_scalar_prefetch=1,
            grid=(steps,),
            in_specs=[pair, whole, whole, pair, lse_spec, whole, whole],
            out_specs=[pair, slot],
            scratch_shapes=[pltpu.VMEM((2, rows, lanes), FULL)],
        ),
        out_shape=[
            jax.ShapeDtypeStruct(query.shape, LOW),
            jax.ShapeDtypeStruct((2, rows, lanes), FULL),
        ],
        compiler_params=pltpu.CompilerParams(
            vmem_limit_bytes=24 * 1024 * 1024, dimension_semantics=("arbitrary",)
        ),
        cost_estimate=pl.CostEstimate(
            flops=10 * rows * rows * query.shape[1],
            bytes_accessed=8 * rows * query.shape[1],
            transcendentals=2 * steps * rows * rows,
        ),
    )(where, query, mine, partner, grad, lse, cosine, sine)


def join_back_body(dboth, incoming, cosine, sine, out):
    total = dboth[0] + swap_halves(incoming[...])
    low = lax.broadcasted_iota(jnp.int32, total.shape, 1) < HDIM
    out[...] = jnp.where(low, turned(total, cosine[...], -sine[...]), total).astype(LOW)


def join_back(dboth, incoming, cosine, sine):
    return pl.pallas_call(
        join_back_body,
        out_shape=jax.ShapeDtypeStruct(incoming.shape, LOW),
        compiler_params=pltpu.CompilerParams(vmem_limit_bytes=24 * 1024 * 1024),
    )(dboth, incoming, cosine, sine)


def put_turned(value, out):
    for block in range(0, 32, 2):
        pair = value[:, block * 64 : block * 64 + 128].T
        for which in range(2):
            at = ((block + which) % 16 * 2 + block // 16) * 64
            out[at : at + 64] = pair[which * 64 : which * 64 + 64]


def prepare_body(where, cotangent, out, out_t):
    value = cotangent[...]
    step = value.shape[0]
    row = lax.broadcasted_iota(jnp.int32, (step, 1), 0) + where[pl.program_id(0)] * step
    value = jnp.where(row < where[5], value, jnp.zeros_like(value))
    out[...] = value
    put_turned(value, out_t)


def prepare(where, cotangent):
    rows, model = cotangent.shape
    step = rows // 4
    return pl.pallas_call(
        prepare_body,
        grid_spec=pltpu.PrefetchScalarGridSpec(
            num_scalar_prefetch=1,
            grid=(4,),
            in_specs=[pl.BlockSpec((step, model), lambda i, where: (where[i], 0))],
            out_specs=[
                pl.BlockSpec((step, model), lambda i, where: (i, 0)),
                pl.BlockSpec((model, step), lambda i, where: (0, i)),
            ],
        ),
        out_shape=[
            jax.ShapeDtypeStruct((rows, model), LOW),
            jax.ShapeDtypeStruct((model, rows), LOW),
        ],
        compiler_params=pltpu.CompilerParams(
            vmem_limit_bytes=24 * 1024 * 1024, dimension_semantics=("arbitrary",)
        ),
        cost_estimate=pl.CostEstimate(
            flops=rows * model, bytes_accessed=6 * rows * model, transcendentals=0
        ),
    )(where, cotangent)


def feed_body(*refs):
    pieces, (w_gate, w_up, dhidden, dy_t) = refs[:4], refs[4:8]
    hidden_out, dgate_out, dup_out, grads, rows, rows_t = refs[8:]
    height = pieces[0].shape[0]
    step, last = pl.program_id(0), pl.num_programs(0) - 1

    @pl.when(step == 0)
    def _():
        for index, piece in enumerate(pieces):
            rows[index * height : (index + 1) * height] = piece[...]
        put_turned(rows[...], rows_t)

    rest = grads.shape[1] // 6

    def columns(width):
        at = slice(0, width)
        gate = dot(rows[...], w_gate[:, at]).astype(LOW).astype(FULL)
        up = dot(rows[...], w_up[:, at]).astype(LOW).astype(FULL)
        sigmoid = jax.nn.sigmoid(gate)
        activated = gate * sigmoid
        hidden = (activated * up).astype(LOW)
        back = dhidden[:, at]
        dgate = (back * up * sigmoid * (1.0 + gate * (1.0 - sigmoid))).astype(LOW)
        dup = (back * activated).astype(LOW)
        hidden_out[:, at], dgate_out[:, at], dup_out[:, at] = hidden, dgate, dup
        pairs = ((dy_t, hidden), (rows_t, dgate), (rows_t, dup))
        for index, (side, fan) in enumerate(pairs):
            grads[:, index * width : (index + 1) * width] = dot(side[...], fan).astype(LOW)

    pl.when(step < last)(lambda: columns(256))
    pl.when(step == last)(lambda: columns(rest))


def feed(pieces, w_gate, w_up, dhidden, dy_t):
    rows, width = dhidden.shape
    model = w_gate.shape[0]
    across = pl.BlockSpec((rows, 256), lambda i: (0, i))
    weight = pl.BlockSpec((model, 256), lambda i: (0, i))
    whole = lambda value: pl.BlockSpec(value.shape, lambda i: (0, 0))
    return pl.pallas_call(
        feed_body,
        grid=(pl.cdiv(width, 256),),
        in_specs=[whole(piece) for piece in pieces] + [weight, weight, across, whole(dy_t)],
        out_specs=[across] * 3 + [pl.BlockSpec((model, 768), lambda i: (0, i))],
        out_shape=[jax.ShapeDtypeStruct((rows, width), LOW)] * 3
        + [jax.ShapeDtypeStruct((model, 3 * width), LOW)],
        scratch_shapes=[pltpu.VMEM((rows, model), LOW), pltpu.VMEM((model, rows), LOW)],
        compiler_params=pltpu.CompilerParams(
            vmem_limit_bytes=60 * 1024 * 1024, dimension_semantics=("arbitrary",)
        ),
        cost_estimate=pl.CostEstimate(
            flops=10 * rows * model * width,
            bytes_accessed=10 * model * width + 10 * rows * width + 4 * rows * model,
            transcendentals=rows * width,
        ),
    )(*pieces, w_gate, w_up, dhidden, dy_t)


def split_turns(value):
    width = value.shape[1] // 3
    turns, rest = width // 256, width % 256
    out = []
    for at in range(3):
        parts = [value[:, i * 768 + at * 256 : i * 768 + at * 256 + 256] for i in range(turns)]
        start = turns * 768 + at * rest
        out.append(jnp.concatenate(parts + [value[:, start : start + rest]], axis=1))
    return out


def feed_back_body(dgate, dup, w_gate, w_up, mine, other):
    value = dot_t(dgate[...], w_gate[...]) + dot_t(dup[...], w_up[...])
    half = value.shape[0] // 2
    mine[...] = value[:half]
    other[...] = value[half:].astype(LOW)


def feed_back(dgate, dup, w_gate, w_up):
    rows, width = dgate.shape
    model = w_gate.shape[0]
    whole = pl.BlockSpec((rows, width), lambda i: (0, 0))
    weight = pl.BlockSpec((256, width), lambda i: (i, 0))
    across = pl.BlockSpec((rows // 2, 256), lambda i: (0, i))
    return pl.pallas_call(
        feed_back_body,
        grid=(model // 256,),
        in_specs=[whole, whole, weight, weight],
        out_specs=[across, across],
        out_shape=[
            jax.ShapeDtypeStruct((rows // 2, model), FULL),
            jax.ShapeDtypeStruct((rows // 2, model), LOW),
        ],
        compiler_params=pltpu.CompilerParams(
            vmem_limit_bytes=60 * 1024 * 1024, dimension_semantics=("arbitrary",)
        ),
        cost_estimate=pl.CostEstimate(
            flops=4 * rows * model * width,
            bytes_accessed=4 * model * width + 4 * rows * width + 3 * rows * model,
            transcendentals=0,
        ),
    )(dgate, dup, w_gate, w_up)


def input_back_body(dquery, dpair, w_query, w_key, w_value, rows, mine, other, gain, w_pair):
    w_pair[:HDIM] = w_key[...]
    w_pair[HDIM:] = w_value[...]
    value = dot_t(dquery[...], w_query[...]) + dot(dpair[...], w_pair[...])
    half = value.shape[0] // 2
    mine[...] = value[:half]
    other[...] = value[half:].astype(LOW)
    gain[...] = jnp.sum(value * rows[...].astype(FULL), axis=0, keepdims=True)


def input_back(dquery, dpair, w_query, w_key, w_value, normed):
    rows, model = normed.shape
    whole = lambda value: pl.BlockSpec(value.shape, lambda i: (0, 0))
    across = lambda height: pl.BlockSpec((height, 256), lambda i: (0, i))
    return pl.pallas_call(
        input_back_body,
        grid=(model // 256,),
        in_specs=[
            whole(dquery),
            whole(dpair),
            pl.BlockSpec((256, w_query.shape[1]), lambda i: (i, 0)),
            across(HDIM),
            across(HDIM),
            across(rows),
        ],
        out_specs=[across(rows // 2), across(rows // 2), across(1)],
        out_shape=[
            jax.ShapeDtypeStruct((rows // 2, model), FULL),
            jax.ShapeDtypeStruct((rows // 2, model), LOW),
            jax.ShapeDtypeStruct((1, model), FULL),
        ],
        scratch_shapes=[pltpu.VMEM((2 * HDIM, 256), LOW)],
        compiler_params=pltpu.CompilerParams(
            vmem_limit_bytes=60 * 1024 * 1024, dimension_semantics=("arbitrary",)
        ),
        cost_estimate=pl.CostEstimate(
            flops=2 * rows * model * 640,
            bytes_accessed=model * 1280 + 5 * rows * model,
            transcendentals=0,
        ),
    )(dquery, dpair, w_query, w_key, w_value, normed)


def wgrad_body(ring, orders, where, side, fan, *refs):
    step = pl.program_id(0)
    value = dot_rows(side[...], fan[...])
    if ring == "z":
        total = refs[4]
        total[...] = value

    for half in range(2):
        send_ref, keep_ref = refs[2 * half : 2 * half + 2]
        at = step - 4 * half
        if ring == "z":
            def piece(bits):
                start = pl.multiple_of(where[8 + bits], 64)
                return total[pl.ds(start, 64), :].astype(LOW)

            @pl.when((at >= 0) & (at < 4))
            def _():
                order = orders[half]
                send_ref[0:64] = piece(order[0])
                send_ref[64:128] = piece(order[1])
                keep_ref[0:64] = piece(order[2])
                keep_ref[64:128] = piece(order[3])
        else:

            @pl.when((at >= 0) & (at < 2))
            def _():
                send_ref[...] = value.astype(LOW)

            @pl.when((at >= 2) & (at < 4))
            def _():
                keep_ref[...] = value.astype(LOW)


def wgrad(place, core, side, fan, ring):
    tokens, width = fan.shape
    x, z = place
    orders = [(first, 2, 0, 4 - first) for first in (1, 3)]
    blocks = []
    for half in range(2):
        steps = orders[half] if ring == "x" else range(4)
        blocks += [(core ^ half) * 4 + (x ^ bits) for bits in steps]
    where = jnp.stack(blocks + [(z ^ bits) * 64 for bits in range(4)]).astype(jnp.int32)
    rows = 256 if ring == "x" else 128

    def place_of(low, high):
        return pl.BlockSpec((rows, width), lambda i, where: (jnp.clip(i - low, 0, high), 0))

    if ring == "x":
        out_specs = [place_of(low, 1) for low in (0, 2, 4, 6)]
    else:
        out_specs = [place_of(low, 3) for low in (0, 0, 4, 4)]
    return pl.pallas_call(
        functools.partial(wgrad_body, ring, orders),
        grid_spec=pltpu.PrefetchScalarGridSpec(
            num_scalar_prefetch=1,
            grid=(8,),
            in_specs=[
                pl.BlockSpec((tokens, 256), lambda i, where: (0, where[i])),
                pl.BlockSpec((tokens, width), lambda i, where: (0, 0)),
            ],
            out_specs=out_specs,
            scratch_shapes=[pltpu.VMEM((256, width), FULL)] if ring == "z" else [],
        ),
        out_shape=[jax.ShapeDtypeStruct((512, width), LOW)] * 4,
        compiler_params=pltpu.CompilerParams(
            vmem_limit_bytes=24 * 1024 * 1024, dimension_semantics=("arbitrary",)
        ),
        cost_estimate=pl.CostEstimate(
            flops=2 * tokens * 2048 * width,
            bytes_accessed=2 * tokens * (2048 + width) + 4 * 2048 * width,
            transcendentals=0,
        ),
    )(where, side, fan)


def scatter_planes(value):
    groups = [[16 * yh + i for i in range(16)] for yh in range(2)]
    return lax.psum_scatter(
        value, "dp", scatter_dimension=0, axis_index_groups=groups, tiled=True
    )


def tie(value, *others):
    return lax.optimization_barrier((value, *others))[0]


class Grad:
    def __init__(self, links, place, core, side, fan, ring):
        self.links, self.ring = links, ring
        send0, keep0, send1, keep1 = wgrad(place, core, side, fan, ring)
        self.shape = (4, 2, 64, fan.shape[1]) if ring == "z" else (2, 4, 64, fan.shape[1])
        self.sent = [send0, send1]
        self.keep = [keep0.reshape(self.shape), keep1.reshape(self.shape)]

    def part(self, value, which):
        axis = 1 if self.ring == "z" else 0
        return lax.index_in_dim(value, which, axis, False).astype(FULL)

    def first(self):
        got = [self.links.send(self.sent[half], self.ring, (1, 3)[half]) for half in range(2)]
        self.got = [item.reshape(self.shape) for item in got]

    def second(self):
        self.sent = [
            (self.part(self.keep[half], 1) + self.part(self.got[half], 1)).astype(LOW)
            for half in range(2)
        ]
        self.got_next = [
            self.links.send(self.sent[half], self.ring, (3, 1)[half]) for half in range(2)
        ]

    def halves(self):
        halves = []
        for half in range(2):
            got_next = self.got_next[half]
            got = tie(self.got[half], got_next)
            halves.append(
                self.part(self.keep[half], 0) + self.part(got, 0) + got_next.astype(FULL)
            )
        return halves


class End:
    def __init__(self, links, grad, at):
        ring = "z" if grad.ring == "x" else "x"
        values = jnp.stack(grad.halves(), axis=1)

        def block(bits):
            index = at ^ bits if ring == "z" else bits
            return lax.dynamic_index_in_dim(values, index, 0, False)

        self.keep = block(0)
        self.sent = [block(bits).astype(LOW) for bits in (1, 3, 2)]
        before = [links.last[ring, 1], links.last[ring, 3]]
        self.got = [
            over_ring(tie(item, *before), ring, bits)
            for item, bits in zip(self.sent, (1, 3, 2))
        ]

    def totals(self):
        return self.keep + sum(item.astype(FULL) for item in self.got)


def finish_together(ends, same):
    parts = [end.totals() for end in ends]
    values = jnp.concatenate(parts, axis=2)
    send = jnp.where(same, values[1], values[0]).astype(LOW)
    total = jnp.where(same, values[0], values[1]) + over_yh(send).astype(FULL)
    out, at = [], 0
    for part in parts:
        width = part.shape[2]
        out.append(total[:, at : at + width])
        at += width
    return out


def sent(*tasks):
    return [item for task in tasks for item in task.sent]


def sum_ring(value, ring):
    return value + over_ring(value, ring, 1) + over_ring(value, ring, 3) + over_ring(value, ring, 2)


def per_device(
    hidden_in,
    cotangent,
    seq_lengths,
    slot_order,
    attn_gain,
    w_query,
    w_key,
    w_value,
    w_out,
    mlp_gain,
    w_gate,
    w_up,
    w_down,
):
    rows = hidden_in.shape[0]
    own_rows = rows // 4
    heads = w_query.shape[1] // HDIM
    ff = w_gate.shape[1]
    dp_at = lax.axis_index("dp")
    yh, x, z = dp_at // 16, (dp_at // 4) % 4, dp_at % 4
    place = (x, z)
    tensor_at = lax.axis_index("tensor")
    core = tensor_at % 2
    blocks = [tensor_at ^ bits for bits in (0, 2, 1, 3)]

    sequence = slot_order[0]
    length = jnp.sum(
        jnp.where(jnp.arange(seq_lengths.shape[0], dtype=jnp.int32) == sequence, seq_lengths, 0)
    )
    gain_one = attn_gain.astype(FULL)
    gain_two = mlp_gain.astype(FULL)

    links = Links()
    links = Links()
    attn_in, queries, packed, cosine, sine = project(
        blocks, hidden_in, attn_gain[None, :], w_query, w_key.T, w_value.T
    )
    partner = over_tensor(packed, 1)
    where = jnp.stack(blocks + [1 - core, length]).astype(jnp.int32)
    attended, lse = attend(where, queries, packed, partner)
    dy_low, dy_t = prepare(where, cotangent)

    half = 2 * own_rows

    got = over_tensor(dot(attended[half:], w_out).astype(LOW), 1)
    mine = dot(attended[:half], w_out)
    send = (mine[own_rows:] + got[own_rows:].astype(FULL)).astype(LOW)
    got_next = tie(over_tensor(send, 2), dy_low, dy_t)
    inputs = lax.dynamic_slice_in_dim(hidden_in, tensor_at * own_rows, own_rows, 0).astype(FULL)
    got = tie(got, got_next)
    middle = inputs + mine[:own_rows] + got[:own_rows].astype(FULL) + got_next.astype(FULL)
    inv_two = lax.rsqrt(jnp.mean(middle * middle, axis=-1, keepdims=True) + EPS)
    normed_two = middle * inv_two
    own = (normed_two * gain_two).astype(LOW)

    got = over_tensor(own, 2)
    got_own = over_tensor(own, 1)
    grad_hidden = dot_t(tie(dy_low, own), w_down)
    got = tie(got, grad_hidden)
    hidden, grad_gate, grad_up, mlp_grads = feed(
        [own, got, got_own, over_tensor(got, 1)], w_gate, w_up, grad_hidden, dy_t
    )

    def grad_of(side, fan, ring):
        return Grad(links, place, core, side, fan, ring)

    same = yh == core
    mlp_sum = scatter_planes(mlp_grads)
    mine, other = feed_back(grad_gate, grad_up, w_gate, w_up)
    got = over_tensor(other, 1)
    send = (mine[own_rows:] + got[own_rows:].astype(FULL)).astype(LOW)
    got_next = over_tensor(send, 2)
    mlp_send = dot(tie(hidden, send)[half:], w_down).astype(LOW)
    mlp_got = over_tensor(mlp_send, 1)
    mlp_mine = dot(tie(hidden, mlp_send)[:half], w_down)
    got_next = tie(got_next, mlp_mine)
    got = tie(got, got_next)
    mlp_back = mine[:own_rows] + got[:own_rows].astype(FULL) + got_next.astype(FULL)

    scaled_two = mlp_back * gain_two
    dmid = dy_low[:own_rows].astype(FULL) + inv_two * (
        scaled_two - normed_two * jnp.mean(scaled_two * normed_two, axis=-1, keepdims=True)
    )
    gain_two_part = jnp.sum(mlp_back * normed_two, axis=0)
    own = dmid.astype(LOW)
    got = over_tensor(own, 2)
    mlp_got = tie(mlp_got, own)
    mlp_send = (mlp_mine[own_rows:] + mlp_got[own_rows:].astype(FULL)).astype(LOW)
    output_rows = middle + mlp_mine[:own_rows] + mlp_got[:own_rows].astype(FULL)
    got = tie(got, mlp_send, output_rows)
    mlp_got = over_tensor(tie(mlp_send, got), 2)
    pair = jnp.concatenate([own, got], axis=0)
    got_last = over_tensor(pair, 1)
    dmid_low = jnp.concatenate([pair, got_last], axis=0)

    grad_attended = dot_t(dmid_low, w_out).astype(LOW)
    query_low, dboth = attend_back(
        where, queries, packed, partner, grad_attended, lse, cosine, sine
    )
    incoming = over_tensor(dboth[1], 1)
    incoming = tie(incoming, mlp_got)
    key_value_low = join_back(dboth, incoming, cosine, sine)
    qkv_low = jnp.concatenate([query_low, key_value_low], axis=1)
    mine, other, gain_one_sum = input_back(
        query_low, key_value_low, w_query, w_key.T, w_value.T, attn_in
    )
    gains = jnp.stack([gain_one_sum[0] / gain_one, gain_two_part])
    got = over_tensor(other, 1)
    send = (mine[own_rows:] + got[own_rows:].astype(FULL)).astype(LOW)
    got_next = over_tensor(send, 2)
    for ring in ("x", "z"):
        gains = sum_ring(tie(gains, send), ring)
    qkv = grad_of(attn_in, tie(qkv_low, gains), "z")
    out = grad_of(tie(dmid_low, *qkv.sent), attended, "x")
    qkv.first()
    out.first()
    got = tie(got, got_next)
    attn_back = mine[:own_rows] + got[:own_rows].astype(FULL) + got_next.astype(FULL)

    output_rows = (output_rows + mlp_got.astype(FULL)).astype(LOW)

    inv_one = lax.rsqrt(jnp.mean(inputs * inputs, axis=-1, keepdims=True) + EPS)
    normed_one = inputs * inv_one
    scaled_one = attn_back * gain_one
    input_grad = dmid + inv_one * (
        scaled_one - normed_one * jnp.mean(scaled_one * normed_one, axis=-1, keepdims=True)
    )
    mlp_keep = lax.dynamic_slice_in_dim(mlp_sum, yh * 64, 64, 0).astype(FULL)
    mlp_send = lax.dynamic_slice_in_dim(mlp_sum, (1 - yh) * 64, 64, 0)
    gains = tie(gains, input_grad, *out.sent)
    gains = gains + over_yh(gains)
    gains = gains + over_tensor(gains, 2)
    gains = gains + over_tensor(gains, 1)
    out.second()
    qkv.second()
    mlp_rows_got = over_yh(mlp_send)
    qkv.got_next[0] = tie(qkv.got_next[0], mlp_rows_got)
    ends = [End(links, out, z), End(links, qkv, x)]
    out_rows, qkv_rows = finish_together(ends, same)
    down_rows, gate_rows, up_rows = split_turns(mlp_keep + mlp_rows_got.astype(FULL))
    q_cols = heads * HDIM
    return (
        output_rows,
        input_grad,
        gains[0],
        qkv_rows[:, :q_cols],
        qkv_rows[:, q_cols : q_cols + HDIM],
        qkv_rows[:, q_cols + HDIM :],
        out_rows.T,
        gains[1],
        gate_rows,
        up_rows,
        down_rows.T,
    )


def solution(mesh):
    return jax.shard_map(
        per_device,
        mesh=mesh,
        in_specs=(
            P("dp", None),
            P("dp", None),
            P(),
            P("dp"),
            P(),
            P(None, "tensor"),
            P(None, "tensor"),
            P(None, "tensor"),
            P("tensor", None),
            P(),
            P(None, "tensor"),
            P(None, "tensor"),
            P("tensor", None),
        ),
        out_specs=(
            P(("dp", "tensor"), None),
            P(("dp", "tensor"), None),
            P(),
            P("dp", "tensor"),
            P("dp", "tensor"),
            P("dp", "tensor"),
            P("tensor", "dp"),
            P(),
            P("dp", "tensor"),
            P("dp", "tensor"),
            P("tensor", "dp"),
        ),
        check_vma=False,
    )
```
